32 devices in a mesh: groups: 2 (over y), ctx: 4 (over z), head: 2 (over x), sub: 2 (over core).
Axes of the slice: x: 2, y: 2, z: 4, core: 2. Of those that a mesh axis runs over, the one named last changes fastest.
Arguments:
- att_query: bfloat16 [1024, 4096], P(('groups', 'ctx'), ('head', 'sub')), parts along dimension 0, may hold values from -4 to 4
- att_gate: bfloat16 [1024, 4096], P(('groups', 'ctx'), ('head', 'sub')), parts along dimension 0, may hold values from -6 to 6
- att_kv: bfloat16 [1024, 1024], P(('groups', 'ctx')), parts along dimension 0, may hold values from -4 to 4
- residual: bfloat16 [1024, 2048], P(('groups', 'ctx'), ('head', 'sub')), parts along dimension 0, may hold values from -0.19921875 to 0.19921875
- out_weight: bfloat16 [4096, 2048], P(('head', 'sub')), may hold values from -0.5 to 0.5
- norm_gain: float32 [2048], replicated, may hold values from 0.1 to 1.9
- in_weight: bfloat16 [2048, 8192], P(None, ('head', 'sub')), may hold values from -0.125 to 0.125
- beta_weight: bfloat16 [2048, 32], P(None, ('head', 'sub')), may hold values from -0.125 to 0.125
- log_decay: float32 [1024, 32], P(('groups', 'ctx'), ('head', 'sub')), parts along dimension 0, may hold values from -0.7 to 0, as said below
- delta_gain: float32 [128], replicated, may hold values from 0.1 to 1.9
Outputs:
- new_residual: bfloat16 [1024, 2048], P(('groups', 'ctx'), ('head', 'sub')), parts along dimension 0
- delta_out: bfloat16 [1024, 4096], P(('groups', 'ctx'), ('head', 'sub')), parts along dimension 0
The draws below stay inside these ranges and needn't reach their ends.
There are 2 independent parts, one for each index of `groups`. The reference program is written for one: setup_inputs(seed, part) draws one part's arguments, and reference() takes and returns one part's arrays. A program takes and returns all parts, laid end to end along the dimension named above; an argument that names none is the same for every part. Nothing has to cross between parts.
Inputs may be any that keep to these rules, and one draw needn't show every extreme that they name: `log_decay`: negative.
All inputs are finite; a program needn't handle non-finite values.
Results may differ from the reference program's by a relative error of at most 0.035.
Values may be sent and summed in bfloat16 or wider, within the bound.
No kernel may reach another device: no remote copies, remote signals or barrier semaphores. Data moves between devices by JAX's collectives and lax.ppermute only.
A program may use at most 64 MiB of HBM per device.

```python
import math
import jax
import jax.numpy as jnp
from jax import lax

D = 2048
HEADS = 16
KV_HEADS = 2
HD = 256
KEY_HEADS = 16
DELTA_VALUE_HEADS = 32
DK = 128
DV = 128
PROMPT_TOKENS = 512
N_CTX = 4


def draw_att_kv(key, part):
    base_key = jax.random.fold_in(key, 11)
    entries = jnp.clip(jax.random.normal(base_key, (PROMPT_TOKENS, KV_HEADS, 2, HD), jnp.float32), -4.0, 4.0)
    return entries.reshape(PROMPT_TOKENS, KV_HEADS * 2 * HD).astype(jnp.bfloat16)


def draw_att_query(key, part):
    base_key = jax.random.fold_in(key, 13)
    entries = jnp.clip(jax.random.normal(base_key, (PROMPT_TOKENS, HEADS, HD), jnp.float32), -4.0, 4.0)
    return entries.reshape(PROMPT_TOKENS, HEADS * HD).astype(jnp.bfloat16)


def draw_log_decay(key, part):
    key_sequence = jax.random.split(jax.random.fold_in(key, 17), 4)
    quick_heads = jax.random.randint(key_sequence[0], (DELTA_VALUE_HEADS,), 0, 10) >= 5
    baseline_rate = jnp.where(quick_heads, -1.0 / 40.0, -math.log(10.0) / (2.0 * PROMPT_TOKENS))
    jaggedness = jnp.exp(jax.random.uniform(key_sequence[1], (PROMPT_TOKENS, DELTA_VALUE_HEADS), jnp.float32, math.log(0.5), math.log(2.0)))
    spike_events = jax.random.randint(key_sequence[2], (PROMPT_TOKENS, DELTA_VALUE_HEADS), 0, PROMPT_TOKENS) < 2
    spike_rate = jnp.log(jax.random.uniform(key_sequence[3], (PROMPT_TOKENS, DELTA_VALUE_HEADS), jnp.float32, 0.5, 0.8))
    gentle_spike = jnp.logical_and(spike_events, jnp.logical_not(quick_heads)[None, :])
    return jnp.where(gentle_spike, spike_rate, baseline_rate[None, :] * jaggedness).astype(jnp.float32)


def raised(values, stream_key, source, target, blocks, factor):
    owner, partner = [(jnp.arange(values.shape[position]) // (values.shape[position] // blocks)).reshape([-1 if axis == position else 1 for axis in range(values.ndim)]) for position in (source, target)]
    chosen = jax.random.permutation(stream_key, blocks)[partner]
    strong = (owner == chosen) | (owner == (partner + blocks // 2) % blocks)
    return jnp.where(strong, factor * values, values)


def steps_of(own_key, extent, cuts, least, top_value):
    level, own = 1.0, jax.random.fold_in(own_key, 6)
    for axis_at, shards_of in cuts:
        heights = jnp.exp(jax.random.uniform(jax.random.fold_in(own, axis_at), (shards_of,), jnp.float32, least / len(cuts), top_value / len(cuts)))
        level = level * jnp.repeat(heights, extent[axis_at] // shards_of).reshape([-1 if axis == axis_at else 1 for axis in range(len(extent))])
    return level


def centred(key, dims, width, bound, cuts=(), held_as=jnp.bfloat16):
    drawn = width * jax.random.normal(key, dims, jnp.float32)
    if cuts:
        drawn = drawn * steps_of(key, dims, cuts, -0.22, 0.18)
    return jnp.clip(drawn, -bound, bound).astype(held_as)


def noise_with(own_key, extent, width, limit, cuts, heavy, kind=jnp.bfloat16):
    array = width * jax.random.normal(own_key, extent, jnp.float32)
    if cuts:
        array = array * steps_of(own_key, extent, cuts, -0.22, 0.18)
    return jnp.clip(raised(array, jax.random.fold_in(own_key, 3), *heavy), -limit, limit).astype(kind)


def setup_inputs(seed: int = 0, part: int = 0) -> dict:
    arg_keys = jax.random.split(jax.random.key(seed), 11)
    part_keys = jax.random.split(jax.random.fold_in(arg_keys[10], part), 11)
    att_query = draw_att_query(jax.random.fold_in(jax.random.fold_in(arg_keys[10], part), 71), part)
    att_gate = centred(part_keys[1], (PROMPT_TOKENS, HEADS * HD), 1.0, 6.0, ((0, 4), (1, 4)))
    att_kv = draw_att_kv(jax.random.fold_in(jax.random.fold_in(arg_keys[10], part), 71), part)
    residual = jnp.clip(jax.random.uniform(part_keys[3], (PROMPT_TOKENS, D), jnp.float32, -0.19921875, 0.19921875) * steps_of(part_keys[3], (PROMPT_TOKENS, D), ((0, 4), (1, 4)), -0.4, 0.0), -0.19921875, 0.19921875).astype(jnp.bfloat16)
    out_weight = noise_with(arg_keys[4], (HEADS * HD, D), HD ** -0.5, 0.5, ((0, 4),), (0, 1, 4, 2.0))
    norm_gain = jnp.clip(1.0 + 0.18 * jax.random.normal(arg_keys[5], (D,), jnp.float32), 0.1, 1.9)
    in_weight = centred(arg_keys[6], (D, KEY_HEADS * (2 * DK + 2 * DV)), D ** -0.5, 0.125, ((1, 4),))
    beta_weight = centred(arg_keys[7], (D, DELTA_VALUE_HEADS), D ** -0.5, 0.125, ((1, 4),))
    log_decay = draw_log_decay(jax.random.fold_in(jax.random.fold_in(arg_keys[10], part), 71), part)
    delta_gain = jnp.clip(1.0 + 0.18 * jax.random.normal(arg_keys[9], (DV,), jnp.float32), 0.1, 1.9)
    return {"att_query": att_query, "att_gate": att_gate, "att_kv": att_kv, "residual": residual, "out_weight": out_weight, "norm_gain": norm_gain, "in_weight": in_weight, "beta_weight": beta_weight, "log_decay": log_decay, "delta_gain": delta_gain}


TOP_PRECISION = lax.Precision.HIGHEST
EPSILON = 1e-06

def stored_positions(total_rows, ctx_devices):
    half_rows = total_rows // (2 * ctx_devices)
    row_index = jnp.arange(total_rows, dtype=jnp.int32)
    device_of = row_index // (2 * half_rows)
    within_dev = row_index % (2 * half_rows)
    block_number = jnp.where(within_dev < half_rows, device_of, 2 * ctx_devices - 1 - device_of)
    return (block_number * half_rows + within_dev % half_rows).astype(jnp.int32)

def unit_rows(matrix):
    return matrix * lax.rsqrt(lax.optimization_barrier(jnp.sum(matrix * matrix, axis=-1, keepdims=True)) + EPSILON)

def reference(att_query, att_gate, att_kv, residual, out_weight, norm_gain, in_weight, beta_weight, log_decay, delta_gain):
    places = stored_positions(PROMPT_TOKENS, N_CTX)
    visible = places[:, None] >= places[None, :]
    group_size = HEADS // KV_HEADS
    score_scale = HD ** (-0.5)

    def one_head(head_number):
        query_rows = lax.dynamic_slice_in_dim(att_query, head_number * HD, HD, 1)
        gate_rows = lax.dynamic_slice_in_dim(att_gate, head_number * HD, HD, 1)
        kv_number = head_number // group_size
        key_rows = lax.dynamic_slice_in_dim(att_kv, kv_number * 2 * HD, HD, 1)
        value_rows = lax.dynamic_slice_in_dim(att_kv, kv_number * 2 * HD + HD, HD, 1)
        scores = jnp.dot(query_rows, key_rows.T, preferred_element_type=jnp.float32) * score_scale
        scores = jnp.where(visible, scores, -1e+30)
        row_max = lax.optimization_barrier(jnp.max(scores, axis=1, keepdims=True))
        weights = jnp.where(visible, jnp.exp(scores - row_max), 0.0)
        denominator = lax.optimization_barrier(jnp.sum(weights, axis=1, keepdims=True))
        attended = jnp.dot(weights.astype(jnp.bfloat16), value_rows, preferred_element_type=jnp.float32) / denominator
        return (attended * jax.nn.sigmoid(gate_rows.astype(jnp.float32))).astype(jnp.bfloat16)
    per_head = lax.map(one_head, jnp.arange(HEADS, dtype=jnp.int32))
    att_heads = jnp.transpose(per_head, (1, 0, 2)).reshape(PROMPT_TOKENS, HEADS * HD)
    hidden = residual.astype(jnp.float32) + jnp.dot(att_heads, out_weight, preferred_element_type=jnp.float32)
    new_residual = hidden.astype(jnp.bfloat16)
    mean_square = lax.optimization_barrier(jnp.mean(hidden * hidden, axis=1, keepdims=True))
    normed = (hidden * lax.rsqrt(mean_square + EPSILON) * norm_gain).astype(jnp.bfloat16)
    projected = jnp.dot(normed, in_weight, preferred_element_type=jnp.float32)
    grouped = projected.reshape(PROMPT_TOKENS, KEY_HEADS, 2 * DK + 2 * DV)
    query_unit = jnp.repeat(unit_rows(jax.nn.silu(grouped[:, :, :DK])) * DK ** (-0.5), 2, axis=1)
    key_unit = jnp.repeat(unit_rows(jax.nn.silu(grouped[:, :, DK:2 * DK])), 2, axis=1)
    value_all = jax.nn.silu(grouped[:, :, 2 * DK:]).reshape(PROMPT_TOKENS, DELTA_VALUE_HEADS, DV)
    beta_rows = jax.nn.sigmoid(jnp.dot(normed, beta_weight, preferred_element_type=jnp.float32))
    natural_order = jnp.argsort(places).astype(jnp.int32)

    def advance(recurrent_state, inputs):
        current_query, current_key, value_now, beta_now, decay_now = inputs
        retention = jnp.exp(decay_now)[:, None]
        retrieved_values = jnp.einsum('ge,gej->gj', current_key, recurrent_state, precision=TOP_PRECISION)
        written = beta_now[:, None] * (value_now - retention * retrieved_values)
        recurrent_state = retention[:, :, None] * recurrent_state + current_key[:, :, None] * written[:, None, :]
        layer_output = jnp.einsum('ge,gej->gj', current_query, recurrent_state, precision=TOP_PRECISION)
        return (recurrent_state, layer_output)
    start_state = jnp.zeros((DELTA_VALUE_HEADS, DK, DV), jnp.float32)
    sequence_inputs = (query_unit[natural_order], key_unit[natural_order], value_all[natural_order], beta_rows[natural_order], log_decay[natural_order])
    final_state, natural_out = lax.scan(advance, start_state, sequence_inputs)
    stored_out = natural_out[places]
    out_square = lax.optimization_barrier(jnp.mean(stored_out * stored_out, axis=2, keepdims=True))
    delta_out = (stored_out * lax.rsqrt(out_square + EPSILON) * delta_gain).astype(jnp.bfloat16)
    return (new_residual, delta_out.reshape(PROMPT_TOKENS, DELTA_VALUE_HEADS * DV))
```

```python
import functools

import jax
import jax.numpy as jnp
from jax import lax
from jax.experimental import pallas as pl
from jax.experimental.pallas import tpu as pltpu
from jax.sharding import PartitionSpec as P

HEADS = 16
KV_HEADS = 2
HD = 256
DK = 128
DV = 128


TOP_PRECISION = lax.Precision.HIGHEST
EPSILON = 1e-06
NEGATIVE = -1e30


def passed_along(value, axis, steps):
    count = lax.axis_size(axis)
    initial, last = (max(0, -steps), min(count, count - steps))
    return lax.ppermute(value, axis, [(source, source + steps) for source in range(initial, last)])


def stored_positions(first_row, row_total, half_rows, ctx_count):
    row_index = first_row + jnp.arange(row_total, dtype=jnp.int32)
    device_of = row_index // (2 * half_rows)
    within_dev = row_index % (2 * half_rows)
    block_number = jnp.where(within_dev < half_rows, device_of, 2 * ctx_count - 1 - device_of)
    return block_number * half_rows + within_dev % half_rows


def unit_rows(matrix):
    return matrix * lax.rsqrt(jnp.sum(matrix * matrix, axis=-1, keepdims=True) + EPSILON)


def to_blocks(array, half_rows):
    heads_count = array.shape[1]
    width = array.shape[2]
    shaped = array.reshape(2, half_rows, heads_count, width).transpose(2, 0, 1, 3)
    return shaped.reshape(heads_count * 2, half_rows, width)


def block_terms(query_rows, key_rows, value_rows, beta_rows, decay_rows):
    length = query_rows.shape[0]
    cumulative = jnp.cumsum(decay_rows)
    position = jnp.arange(length)
    on_or_below = position[:, None] >= position[None, :]
    strictly_below = position[:, None] > position[None, :]
    decay_gap = cumulative[:, None] - cumulative[None, :]
    decay_grid = jnp.where(on_or_below, jnp.exp(jnp.where(on_or_below, decay_gap, 0.0)), 0.0)
    key_gram = jnp.dot(key_rows, key_rows.T, precision=TOP_PRECISION)
    system = jnp.eye(length, dtype=jnp.float32) + jnp.where(
        strictly_below, beta_rows[:, None] * key_gram * decay_grid, 0.0
    )
    growth = jnp.exp(cumulative)
    right_side = beta_rows[:, None] * jnp.concatenate(
        [value_rows, growth[:, None] * key_rows], axis=1
    )
    solved = jax.scipy.linalg.solve_triangular(system, right_side, lower=True, unit_diagonal=True)
    update_rows = solved[:, : value_rows.shape[1]]
    weight_rows = solved[:, value_rows.shape[1] :]
    attend_grid = jnp.where(
        on_or_below, jnp.dot(query_rows, key_rows.T, precision=TOP_PRECISION) * decay_grid, 0.0
    )
    local_out = jnp.dot(attend_grid, update_rows, precision=TOP_PRECISION)
    read_rows = growth[:, None] * query_rows - jnp.dot(
        attend_grid, weight_rows, precision=TOP_PRECISION
    )
    carried_keys = jnp.exp(cumulative[-1] - cumulative)[:, None] * key_rows
    identity_map = jnp.eye(key_rows.shape[1], dtype=jnp.float32)
    transition = jnp.exp(cumulative[-1]) * identity_map - jnp.dot(
        carried_keys.T, weight_rows, precision=TOP_PRECISION
    )
    offset_state = jnp.dot(carried_keys.T, update_rows, precision=TOP_PRECISION)
    return (local_out, read_rows, transition, offset_state)


def apply_map(matrix_maps, offsets, states):
    return jnp.einsum("hij,hjk->hik", matrix_maps, states, precision=TOP_PRECISION) + offsets


def attend_rows(running, query_block, key_block, value_block, visible, score_scale):
    run_max, run_sum, run_acc = running
    scores = (
        jnp.einsum("rhd,kd->rhk", query_block, key_block, preferred_element_type=jnp.float32)
        * score_scale
    )
    if visible is not None:
        scores = jnp.where(visible[:, None, :], scores, NEGATIVE)
    new_max = jnp.maximum(run_max, jnp.max(scores, axis=2))
    weights = jnp.exp(scores - new_max[:, :, None])
    if visible is not None:
        weights = jnp.where(visible[:, None, :], weights, 0.0)
    rescale = jnp.exp(run_max - new_max)
    run_sum = run_sum * rescale + jnp.sum(weights, axis=2)
    added = jnp.einsum(
        "rhk,kd->rhd", weights.astype(jnp.bfloat16), value_block, preferred_element_type=jnp.float32
    )
    run_acc = run_acc * rescale[:, :, None] + added
    return (new_max, run_sum, run_acc)


def hop_local(
    att_query,
    att_gate,
    att_kv,
    residual,
    out_weight,
    norm_gain,
    in_weight,
    beta_weight,
    log_decay,
    delta_gain,
):
    ctx_count = lax.axis_size("ctx")
    ctx_rank = lax.axis_index("ctx")
    shard_rank = lax.axis_index(("head", "sub"))
    rows_here = att_query.shape[0]
    half_rows = rows_here // 2
    heads_here = att_query.shape[1] // HD
    kv_number = shard_rank * heads_here // (HEADS // KV_HEADS)
    key_local = lax.dynamic_slice_in_dim(att_kv, kv_number * 2 * HD, HD, 1)
    value_local = lax.dynamic_slice_in_dim(att_kv, kv_number * 2 * HD + HD, HD, 1)
    query_heads = att_query.reshape(rows_here, heads_here, HD)
    late_queries = query_heads[half_rows:]
    query_places = stored_positions(ctx_rank * rows_here, rows_here, half_rows, ctx_count)
    same_visible = query_places[:, None] >= query_places[None, :]
    score_scale = HD ** (-0.5)

    def earlier_shard(running, key_shard, value_shard):
        return attend_rows(
            running, query_heads, key_shard[:half_rows], value_shard[:half_rows], None, score_scale
        )

    def same_shard(running, key_shard, value_shard):
        return attend_rows(running, query_heads, key_shard, value_shard, same_visible, score_scale)

    def later_shard(running, key_shard, value_shard):
        late_part = tuple((member[half_rows:] for member in running))
        renewed = attend_rows(late_part, late_queries, key_shard, value_shard, None, score_scale)
        return tuple(
            (
                jnp.concatenate([member[:half_rows], latest], axis=0)
                for member, latest in zip(running, renewed)
            )
        )

    start_running = (
        jnp.full((rows_here, heads_here), NEGATIVE, jnp.float32),
        jnp.zeros((rows_here, heads_here), jnp.float32),
        jnp.zeros((rows_here, heads_here, HD), jnp.float32),
    )
    key_block = lax.all_gather(key_local, "ctx", axis=0, tiled=True)
    value_block = lax.all_gather(value_local, "ctx", axis=0, tiled=True)
    piece_rows = key_block.shape[0]

    def one_shard(number, current):
        offset = number * rows_here
        key_shard = lax.dynamic_slice_in_dim(key_block, offset, rows_here, 0)
        value_shard = lax.dynamic_slice_in_dim(value_block, offset, rows_here, 0)
        shard_number = offset // rows_here
        branch = jnp.clip(shard_number - ctx_rank, -1, 1) + 1
        return lax.switch(
            branch, [earlier_shard, same_shard, later_shard], current, key_shard, value_shard
        )

    run_max, run_sum, run_acc = lax.fori_loop(0, piece_rows // rows_here, one_shard, start_running)
    gate_heads = jax.nn.sigmoid(att_gate.reshape(rows_here, heads_here, HD).astype(jnp.float32))
    att_heads = (
        (run_acc / run_sum[:, :, None] * gate_heads)
        .astype(jnp.bfloat16)
        .reshape(rows_here, heads_here * HD)
    )
    partial_term = jnp.dot(att_heads, out_weight, preferred_element_type=jnp.float32)
    col_width = residual.shape[1]
    col_start = shard_rank * col_width
    placed = lax.dynamic_slice_in_dim(partial_term, col_start, col_width, 1) + residual.astype(
        jnp.float32
    )
    partial_term = lax.dynamic_update_slice_in_dim(partial_term, placed, col_start, 1)
    hidden = lax.psum(partial_term.astype(jnp.bfloat16), ("head", "sub")).astype(jnp.float32)
    mean_square = jnp.mean(hidden * hidden, axis=1, keepdims=True)
    normed = (hidden * lax.rsqrt(mean_square + EPSILON) * norm_gain).astype(jnp.bfloat16)
    new_residual = lax.dynamic_slice_in_dim(hidden, col_start, col_width, 1).astype(jnp.bfloat16)
    mixed_cols = jnp.dot(normed, in_weight, preferred_element_type=jnp.float32)
    beta_logits = jnp.dot(normed, beta_weight, preferred_element_type=jnp.float32)
    key_here = in_weight.shape[1] // (2 * DK + 2 * DV)
    value_here = 2 * key_here
    grouped = mixed_cols.reshape(rows_here, key_here, 2 * DK + 2 * DV)
    query_unit = jnp.repeat(unit_rows(jax.nn.silu(grouped[:, :, :DK])) * DK ** (-0.5), 2, axis=1)
    key_unit = jnp.repeat(unit_rows(jax.nn.silu(grouped[:, :, DK : 2 * DK])), 2, axis=1)
    value_all = jax.nn.silu(grouped[:, :, 2 * DK :]).reshape(rows_here, value_here, DV)
    beta_all = jax.nn.sigmoid(beta_logits)
    local_out, read_rows, transition, offset_state = jax.vmap(block_terms)(
        to_blocks(query_unit, half_rows),
        to_blocks(key_unit, half_rows),
        to_blocks(value_all, half_rows),
        to_blocks(beta_all[:, :, None], half_rows)[:, :, 0],
        to_blocks(log_decay[:, :, None], half_rows)[:, :, 0],
    )
    transition = transition.reshape(value_here, 2, DK, DK)
    offset_state = offset_state.reshape(value_here, 2, DK, DV)
    early_map, late_map = (transition[:, 0], transition[:, 1])
    early_offset, late_offset = (offset_state[:, 0], offset_state[:, 1])
    last_rank = ctx_count - 1
    zero_states = jnp.zeros_like(early_offset)

    def early_turn(number, incoming):
        return passed_along(
            apply_map(early_map, early_offset, incoming).astype(jnp.bfloat16), "ctx", 1
        ).astype(jnp.float32)

    early_in = lax.fori_loop(0, ctx_count - 1, early_turn, zero_states)
    early_end = apply_map(early_map, early_offset, early_in)
    late_start = jnp.where(ctx_rank == last_rank, early_end, zero_states)

    def late_turn(number, incoming):
        moved = passed_along(
            apply_map(late_map, late_offset, incoming).astype(jnp.bfloat16), "ctx", -1
        ).astype(jnp.float32)
        return jnp.where(ctx_rank == last_rank, early_end, moved)

    late_in = lax.fori_loop(0, ctx_count - 1, late_turn, late_start)
    states_in = jnp.stack([early_in, late_in], axis=1)
    block_out = local_out.reshape(value_here, 2, half_rows, DV) + jnp.einsum(
        "hbck,hbkv->hbcv",
        read_rows.reshape(value_here, 2, half_rows, DK),
        states_in,
        precision=TOP_PRECISION,
    )
    token_out = block_out.transpose(1, 2, 0, 3).reshape(rows_here, value_here, DV)
    out_square = jnp.mean(token_out * token_out, axis=2, keepdims=True)
    delta_out = (token_out * lax.rsqrt(out_square + EPSILON) * delta_gain).astype(jnp.bfloat16)
    return (new_residual, delta_out.reshape(rows_here, value_here * DV))


KEY_HEADS = 16
IN_VMEM = pl.BlockSpec(memory_space=pltpu.VMEM)
IN_HBM = pl.BlockSpec(memory_space=pl.ANY)
MIB = 2**20
LANES = 128


def owners_fit(mesh):
    shards = mesh.shape["head"] * mesh.shape["sub"]
    key_here = KEY_HEADS // shards
    return mesh.shape["head"] == 2 and mesh.shape["sub"] == 2 and key_here == mesh.shape["ctx"]


def in_vmem(array):
    return pltpu.with_memory_space_constraint(array, pltpu.VMEM)


def in_hbm(array):
    return pltpu.with_memory_space_constraint(array, pltpu.HBM)


def vmem_call(kernel, outs, operands, scratch=(), limit=16, aliases=None, last=False, cost=None):
    make = jax.ShapeDtypeStruct if last else pltpu.VMEM
    return pl.pallas_call(
        kernel,
        out_shape=[make(shape, dtype) for shape, dtype in outs],
        in_specs=[IN_VMEM] * len(operands),
        out_specs=[IN_VMEM] * len(outs),
        scratch_shapes=list(scratch),
        input_output_aliases=aliases or {},
        cost_estimate=cost,
        compiler_params=pltpu.CompilerParams(vmem_limit_bytes=limit * MIB),
    )(*[in_vmem(operand) for operand in operands])


def rotated(value, axis, steps):
    count = lax.axis_size(axis)
    return lax.ppermute(value, axis, [(i, (i + steps) % count) for i in range(count)])


def dot(left, right, dims=((1,), (0,))):
    return lax.dot_general(left, right, (dims, ((), ())), preferred_element_type=jnp.float32)


def halves(value):
    high = value.astype(jnp.bfloat16)
    return high, (value - high.astype(jnp.float32)).astype(jnp.bfloat16)


def dot3(left, right):
    left_high, left_low = halves(left)
    right_high, right_low = halves(right)
    return dot(left_high, right_high) + (dot(left_high, right_low) + dot(left_low, right_high))


def sigmoid(value):
    return 1.0 / (1.0 + jnp.exp(-value))


def silu(value):
    return value / (1.0 + jnp.exp(-value))


def piece_kernel(kv_ref, piece_ref, own_ref, sems):
    start = pl.multiple_of(lax.axis_index("head") * 2 * HD, 2 * HD)
    share = pl.multiple_of(start + lax.axis_index("sub") * HD, HD)
    first = pltpu.make_async_copy(kv_ref.at[:, pl.ds(share, HD)], piece_ref, sems.at[0])
    second = pltpu.make_async_copy(kv_ref.at[:, pl.ds(start, 2 * HD)], own_ref, sems.at[1])
    first.start()
    second.start()
    first.wait()
    second.wait()


def attention_kernel(
    query_ref, gate_ref, own_ref, mine1, mine2, mine3, twin1, twin2, twin3, weight_ref, residual_ref,
    keep_ref, send_ref, keys, values, heads, partial,
):
    rows, head_columns = query_ref.shape
    half = rows // 2
    ctx_rank, head_rank, sub_rank = (lax.axis_index(name) for name in ("ctx", "head", "sub"))
    count = 4
    keys[0:rows] = own_ref[:, 0:HD]
    values[0:rows] = own_ref[:, HD : 2 * HD]

    @pl.when(sub_rank == 0)
    def _():
        for step, (mine, twin) in enumerate(((mine1, twin1), (mine2, twin2), (mine3, twin3)), 1):
            keys[step * rows : (step + 1) * rows] = mine[...]
            values[step * rows : (step + 1) * rows] = twin[...]

    @pl.when(sub_rank != 0)
    def _():
        for step, (mine, twin) in enumerate(((mine1, twin1), (mine2, twin2), (mine3, twin3)), 1):
            keys[step * rows : (step + 1) * rows] = twin[...]
            values[step * rows : (step + 1) * rows] = mine[...]

    def places(row, device):
        within = row % rows
        block = jnp.where(within < half, device, 2 * count - 1 - device)
        return block * half + within % half

    query_place = places(lax.broadcasted_iota(jnp.int32, (rows, 1), 0), ctx_rank)
    key_row = lax.broadcasted_iota(jnp.int32, (1, count * rows), 1)
    key_place = places(key_row, (ctx_rank - key_row // rows + count) % count)
    visible = query_place >= key_place
    for head in range(head_columns // HD):
        columns = slice(head * HD, (head + 1) * HD)
        scores = dot(query_ref[:, columns], keys[...], ((1,), (1,))) * HD ** (-0.5)
        scores = jnp.where(visible, scores, NEGATIVE)
        weights = jnp.exp(scores - jnp.max(scores, axis=1, keepdims=True))
        total = jnp.sum(weights, axis=1, keepdims=True)
        gathered = dot(weights.astype(jnp.bfloat16), values[...])
        gate = sigmoid(gate_ref[:, columns].astype(jnp.float32))
        heads[:, columns] = (gathered / total * gate).astype(jnp.bfloat16)
    partial[...] = dot(heads[...], weight_ref[...])
    width = residual_ref.shape[1]
    mid = partial.shape[1] // 2
    own_columns = pl.ds(pl.multiple_of((head_rank * 2 + sub_rank) * width, width), width)
    partial[:, own_columns] += residual_ref[...].astype(jnp.float32)
    keep_ref[...] = partial[:, pl.ds(pl.multiple_of(sub_rank * mid, mid), mid)]
    send_ref[...] = partial[:, pl.ds(pl.multiple_of((1 - sub_rank) * mid, mid), mid)].astype(jnp.bfloat16)


def chip_sum_kernel(keep_ref, came_ref, sum_ref, send_ref):
    total = keep_ref[...] + came_ref[...].astype(jnp.float32)
    sum_ref[...] = total
    send_ref[...] = total.astype(jnp.bfloat16)


def hidden_kernel(keep_ref, came_ref, hidden_ref):
    hidden_ref[...] = (keep_ref[...] + came_ref[...].astype(jnp.float32)).astype(jnp.bfloat16)


def norm_kernel(own_ref, twin_ref, gain_ref, beta_ref, decay_ref, residual_ref, normed_ref, extra_ref):
    head_rank, sub_rank = lax.axis_index("head"), lax.axis_index("sub")
    mid = own_ref.shape[1]
    width = residual_ref.shape[1]
    columns = pl.ds(pl.multiple_of(sub_rank * width, width), width)

    @pl.when(sub_rank == head_rank)
    def _():
        residual_ref[...] = own_ref[:, columns]

    @pl.when(sub_rank != head_rank)
    def _():
        residual_ref[...] = twin_ref[:, columns]

    own, twin = own_ref[...].astype(jnp.float32), twin_ref[...].astype(jnp.float32)
    squares = jnp.sum(own * own, axis=1, keepdims=True) + jnp.sum(twin * twin, axis=1, keepdims=True)
    scale = lax.rsqrt(squares / (2 * mid) + EPSILON)
    own_half = pl.ds(pl.multiple_of(sub_rank * mid, mid), mid)
    twin_half = pl.ds(pl.multiple_of((1 - sub_rank) * mid, mid), mid)
    normed_ref[:, own_half] = (own * scale * gain_ref[:, own_half]).astype(jnp.bfloat16)
    normed_ref[:, twin_half] = (twin * scale * gain_ref[:, twin_half]).astype(jnp.bfloat16)
    values = decay_ref.shape[0]
    extra_ref[0:values] = decay_ref[...]
    extra_ref[values : 2 * values] = sigmoid(dot(beta_ref[...], normed_ref[...], ((1,), (1,))))


def payload_kernel(step, normed_ref, weight_ref, extra_ref, payload_ref, small):
    rows = normed_ref.shape[0]
    group = 2 * DK + 2 * DV
    count = 4
    target = (lax.axis_index("ctx") + step) % count
    columns = pl.ds(pl.multiple_of(target * group, group), group)
    mixed = silu(dot(normed_ref[...], weight_ref[:, columns]))
    query, key = mixed[:, :DK], mixed[:, DK : 2 * DK]
    payload_ref[0:rows] = (unit_rows(query) * DK ** (-0.5)).astype(jnp.bfloat16)
    payload_ref[rows : 2 * rows] = unit_rows(key).astype(jnp.bfloat16)
    payload_ref[2 * rows : 3 * rows] = mixed[:, 2 * DK : 2 * DK + DV].astype(jnp.bfloat16)
    payload_ref[3 * rows : 4 * rows] = mixed[:, 2 * DK + DV :].astype(jnp.bfloat16)
    values = extra_ref.shape[0] // 2
    small[...] = jnp.zeros_like(small)
    for place, base in ((0, 0), (4, values)):
        full = extra_ref[pl.ds(base + 2 * target, 2), :]
        high = full.astype(jnp.bfloat16).astype(jnp.float32)
        small[place : place + 2] = high
        small[place + 2 : place + 4] = full - high
    payload_ref[4 * rows : 4 * rows + 16] = small[...].astype(jnp.bfloat16)


def unit_lower_inverse(strict, row, column):
    same = lambda size: (row // size) == (column // size)
    small = jnp.where(same(8), strict, 0.0)
    second = dot3(small, small)
    start = jnp.where(row == column, 1.0, 0.0) - small
    start = start + dot3(start, second)
    inverse = start + dot3(start, dot3(second, second))
    for size in (8, 16, 32):
        corner = jnp.where(same(2 * size) & jnp.logical_not(same(size)), strict, 0.0)
        inverse = inverse - dot3(inverse, dot3(corner, inverse))
    return inverse


def block_kernel(step, payload_ref, *refs):
    offset_ref, linear_ref, local_ref, growth_ref = refs[-4:]
    count = 4
    source = (lax.axis_index("ctx") + count - step) % count
    rows = (payload_ref.shape[0] - 16) // 4
    half = rows // 2
    query, key = payload_ref[0:rows], payload_ref[rows : 2 * rows]
    extra = payload_ref[4 * rows : 4 * rows + 16]
    row = lax.broadcasted_iota(jnp.int32, (rows, rows), 0)
    column = lax.broadcasted_iota(jnp.int32, (rows, rows), 1)
    together = (row // half) == (column // half)
    inclusive = together & (row >= column)
    strictly = together & (row > column)
    below = jnp.where(inclusive, 1.0, 0.0).astype(jnp.bfloat16)
    diagonal = jnp.where(row == column, 1.0, 0.0).astype(jnp.bfloat16)
    sums_row = dot(extra, below, ((1,), (1,)))
    sums_column = dot(below, extra, ((1,), (1,)))
    plain_column = dot(diagonal, extra, ((1,), (1,)))
    key_wide = key.astype(jnp.float32)
    key_turned = jnp.transpose(key_wide)
    key_gram = dot(key, key, ((1,), (1,)))
    query_gram = dot(query, key, ((1,), (1,)))
    early_lane = lax.broadcasted_iota(jnp.int32, (1, rows), 1) < half
    for head in range(2):
        total_row = sums_row[head : head + 1] + sums_row[head + 2 : head + 3]
        total = sums_column[:, head : head + 1] + sums_column[:, head + 2 : head + 3]
        beta = plain_column[:, head + 4 : head + 5] + plain_column[:, head + 6 : head + 7]
        decay = jnp.exp(jnp.where(inclusive, total - total_row, NEGATIVE))
        strict = jnp.where(strictly, beta * key_gram * decay, 0.0)
        inverse_high, inverse_low = halves(unit_lower_inverse(strict, row, column))
        growth = jnp.exp(total)
        value = payload_ref[(2 + head) * rows : (3 + head) * rows].astype(jnp.float32)
        right = jnp.concatenate([beta * value, (beta * growth) * key_wide], axis=1).astype(jnp.bfloat16)
        solved = (dot(inverse_high, right) + dot(inverse_low, right)).astype(jnp.bfloat16)
        attended = dot((query_gram * decay).astype(jnp.bfloat16), solved)
        local_ref[source, head] = attended[:, :DV]
        reads = (growth * query.astype(jnp.float32) - attended[:, DV:]).astype(jnp.bfloat16)
        end_row = jnp.where(early_lane, total_row[:, half - 1 : half], total_row[:, rows - 1 : rows])
        carried = key_turned * jnp.exp(end_row - total_row)
        ends = jnp.exp(end_row)
        for block in range(2):
            inside = early_lane if block == 0 else jnp.logical_not(early_lane)
            moved = dot(jnp.where(inside, carried, 0.0).astype(jnp.bfloat16), solved)
            offset_ref[source, head, block] = moved[:, :DV]
            linear_ref[source, head, block, 0:DK] = moved[:, DV:].astype(jnp.bfloat16)
            linear_ref[source, head, block, DK : DK + half] = reads[block * half : (block + 1) * half]
            last = (block + 1) * half - 1
            growth_ref[source, head, block] = jnp.broadcast_to(ends[:, last : last + 1], growth_ref.shape[3:])


def scan_kernel(offset_ref, linear_ref, local_ref, growth_ref, gain_ref, own_ref, back1, back2, back3, outs):
    count = offset_ref.shape[0]
    half = local_ref.shape[2] // 2
    rank = lax.axis_index("ctx")
    states = [None, None]
    for number in range(2 * count):
        source, block = (number, 0) if number < count else (2 * count - 1 - number, 1)
        block_rows = slice(block * half, (block + 1) * half)
        for head in range(2):
            out = local_ref[source, head, block_rows]
            state = offset_ref[source, head, block]
            if states[head] is not None:
                moved = dot(linear_ref[source, head, block], states[head].astype(jnp.bfloat16))
                out = out + moved[DK:]
                state = state - moved[:DK] + growth_ref[source, head, block, 0:1] * states[head]
            states[head] = state
            scale = lax.rsqrt(jnp.mean(out * out, axis=1, keepdims=True) + EPSILON)
            outs[source, block_rows, head * DV : (head + 1) * DV] = (out * scale * gain_ref[...]).astype(jnp.bfloat16)
    own_ref[...] = outs[rank]
    for step, back in enumerate((back1, back2, back3), 1):
        back[...] = outs[(rank + count - step) % count]


def place_kernel(own_ref, back1, back2, back3, out_ref):
    count = 4
    width = own_ref.shape[1]
    rank = lax.axis_index("ctx")
    for step, back in enumerate((own_ref, back1, back2, back3)):
        columns = pl.ds(pl.multiple_of((rank + step) % count * width, width), width)
        out_ref[:, columns] = back[...]


def owner_local(
    att_query,
    att_gate,
    att_kv,
    residual,
    out_weight,
    norm_gain,
    in_weight,
    beta_weight,
    log_decay,
    delta_gain,
):
    bf16, f32 = jnp.bfloat16, jnp.float32
    rows, head_columns = att_query.shape
    model = out_weight.shape[1]
    half_model = model // 2
    steps = (1, 2, 3)
    piece, own_kv = pl.pallas_call(
        piece_kernel,
        out_shape=[pltpu.VMEM((rows, HD), bf16), pltpu.VMEM((rows, 2 * HD), bf16)],
        in_specs=[IN_HBM],
        out_specs=[IN_VMEM] * 2,
        scratch_shapes=[pltpu.SemaphoreType.DMA((2,))],
    )(in_hbm(att_kv))
    mine = [rotated(piece, "ctx", step) for step in steps]
    twin = [rotated(part, "sub", 1) for part in mine]
    keep, send = vmem_call(
        attention_kernel,
        [((rows, half_model), f32), ((rows, half_model), bf16)],
        [att_query, att_gate, own_kv, *mine, *twin, out_weight, residual],
        [
            pltpu.VMEM((4 * rows, HD), bf16),
            pltpu.VMEM((4 * rows, HD), bf16),
            pltpu.VMEM((rows, head_columns), bf16),
            pltpu.VMEM((rows, model), f32),
        ],
    )
    chip_sum, send = vmem_call(
        chip_sum_kernel,
        [((rows, half_model), f32), ((rows, half_model), bf16)],
        [keep, rotated(send, "sub", 1)],
    )
    hidden = vmem_call(hidden_kernel, [((rows, half_model), bf16)], [chip_sum, rotated(send, "head", 1)])[0]
    value_here = log_decay.shape[1]
    new_residual, normed, extra = vmem_call(
        norm_kernel,
        [(residual.shape, bf16), ((rows, model), bf16), ((2 * value_here, rows), f32)],
        [hidden, rotated(hidden, "sub", 1), norm_gain[None, :], beta_weight.T, log_decay.T],
    )
    payloads = [
        vmem_call(
            functools.partial(payload_kernel, step),
            [((4 * rows + 16, LANES), bf16)],
            [normed, in_weight, extra],
            [pltpu.VMEM((16, LANES), f32)],
        )[0]
        for step in range(4)
    ]
    came = [payloads[0]] + [rotated(payloads[step], "ctx", step) for step in steps]
    half = rows // 2
    terms_shapes = [
        ((4, 2, 2, DK, DV), f32),
        ((4, 2, 2, DK + half, DK), bf16),
        ((4, 2, rows, DV), f32),
        ((4, 2, 2, 8, LANES), f32),
    ]
    terms = []
    for step in range(4):
        terms = vmem_call(
            functools.partial(block_kernel, step),
            terms_shapes,
            [came[step], *terms],
            aliases={1 + i: i for i in range(4)} if terms else None,
        )
    own, *backs = vmem_call(
        scan_kernel,
        [((rows, 2 * DV), bf16)] * 4,
        [*terms, delta_gain[None, :]],
        [pltpu.VMEM((4, rows, 2 * DV), bf16)],
    )
    backs = [rotated(back, "ctx", -step) for step, back in zip(steps, backs)]
    delta_out = vmem_call(place_kernel, [((rows, value_here * DV), bf16)], [own, *backs], last=True)[0]
    return (new_residual, delta_out)


def solution(mesh):
    local = owner_local if owners_fit(mesh) else hop_local
    return jax.shard_map(
        local,
        mesh=mesh,
        in_specs=(
            P(("groups", "ctx"), ("head", "sub")),
            P(("groups", "ctx"), ("head", "sub")),
            P(("groups", "ctx"), None),
            P(("groups", "ctx"), ("head", "sub")),
            P(("head", "sub"), None),
            P(),
            P(None, ("head", "sub")),
            P(None, ("head", "sub")),
            P(("groups", "ctx"), ("head", "sub")),
            P(),
        ),
        out_specs=(P(("groups", "ctx"), ("head", "sub")), P(("groups", "ctx"), ("head", "sub"))),
        check_vma=False,
    )
```

```python
import functools

import jax
import jax.numpy as jnp
from jax import lax
from jax.experimental import pallas as pl
from jax.experimental.pallas import tpu as pltpu
from jax.sharding import PartitionSpec as P

HEADS = 16
KV_HEADS = 2
HD = 256
DK = 128
DV = 128


TOP_PRECISION = lax.Precision.HIGHEST
EPSILON = 1e-06
NEGATIVE = -1e30


def passed_along(value, axis, steps):
    count = lax.axis_size(axis)
    initial, last = (max(0, -steps), min(count, count - steps))
    return lax.ppermute(value, axis, [(source, source + steps) for source in range(initial, last)])


def stored_positions(first_row, row_total, half_rows, ctx_count):
    row_index = first_row + jnp.arange(row_total, dtype=jnp.int32)
    device_of = row_index // (2 * half_rows)
    within_dev = row_index % (2 * half_rows)
    block_number = jnp.where(within_dev < half_rows, device_of, 2 * ctx_count - 1 - device_of)
    return block_number * half_rows + within_dev % half_rows


def unit_rows(matrix):
    return matrix * lax.rsqrt(jnp.sum(matrix * matrix, axis=-1, keepdims=True) + EPSILON)


def to_blocks(array, half_rows):
    heads_count = array.shape[1]
    width = array.shape[2]
    shaped = array.reshape(2, half_rows, heads_count, width).transpose(2, 0, 1, 3)
    return shaped.reshape(heads_count * 2, half_rows, width)


def block_terms(query_rows, key_rows, value_rows, beta_rows, decay_rows):
    length = query_rows.shape[0]
    cumulative = jnp.cumsum(decay_rows)
    position = jnp.arange(length)
    on_or_below = position[:, None] >= position[None, :]
    strictly_below = position[:, None] > position[None, :]
    decay_gap = cumulative[:, None] - cumulative[None, :]
    decay_grid = jnp.where(on_or_below, jnp.exp(jnp.where(on_or_below, decay_gap, 0.0)), 0.0)
    key_gram = jnp.dot(key_rows, key_rows.T, precision=TOP_PRECISION)
    system = jnp.eye(length, dtype=jnp.float32) + jnp.where(
        strictly_below, beta_rows[:, None] * key_gram * decay_grid, 0.0
    )
    growth = jnp.exp(cumulative)
    right_side = beta_rows[:, None] * jnp.concatenate(
        [value_rows, growth[:, None] * key_rows], axis=1
    )
    solved = jax.scipy.linalg.solve_triangular(system, right_side, lower=True, unit_diagonal=True)
    update_rows = solved[:, : value_rows.shape[1]]
    weight_rows = solved[:, value_rows.shape[1] :]
    attend_grid = jnp.where(
        on_or_below, jnp.dot(query_rows, key_rows.T, precision=TOP_PRECISION) * decay_grid, 0.0
    )
    local_out = jnp.dot(attend_grid, update_rows, precision=TOP_PRECISION)
    read_rows = growth[:, None] * query_rows - jnp.dot(
        attend_grid, weight_rows, precision=TOP_PRECISION
    )
    carried_keys = jnp.exp(cumulative[-1] - cumulative)[:, None] * key_rows
    identity_map = jnp.eye(key_rows.shape[1], dtype=jnp.float32)
    transition = jnp.exp(cumulative[-1]) * identity_map - jnp.dot(
        carried_keys.T, weight_rows, precision=TOP_PRECISION
    )
    offset_state = jnp.dot(carried_keys.T, update_rows, precision=TOP_PRECISION)
    return (local_out, read_rows, transition, offset_state)


def apply_map(matrix_maps, offsets, states):
    return jnp.einsum("hij,hjk->hik", matrix_maps, states, precision=TOP_PRECISION) + offsets


def attend_rows(running, query_block, key_block, value_block, visible, score_scale):
    run_max, run_sum, run_acc = running
    scores = (
        jnp.einsum("rhd,kd->rhk", query_block, key_block, preferred_element_type=jnp.float32)
        * score_scale
    )
    if visible is not None:
        scores = jnp.where(visible[:, None, :], scores, NEGATIVE)
    new_max = jnp.maximum(run_max, jnp.max(scores, axis=2))
    weights = jnp.exp(scores - new_max[:, :, None])
    if visible is not None:
        weights = jnp.where(visible[:, None, :], weights, 0.0)
    rescale = jnp.exp(run_max - new_max)
    run_sum = run_sum * rescale + jnp.sum(weights, axis=2)
    added = jnp.einsum(
        "rhk,kd->rhd", weights.astype(jnp.bfloat16), value_block, preferred_element_type=jnp.float32
    )
    run_acc = run_acc * rescale[:, :, None] + added
    return (new_max, run_sum, run_acc)


def hop_local(
    att_query,
    att_gate,
    att_kv,
    residual,
    out_weight,
    norm_gain,
    in_weight,
    beta_weight,
    log_decay,
    delta_gain,
):
    ctx_count = lax.axis_size("ctx")
    ctx_rank = lax.axis_index("ctx")
    shard_rank = lax.axis_index(("head", "sub"))
    rows_here = att_query.shape[0]
    half_rows = rows_here // 2
    heads_here = att_query.shape[1] // HD
    kv_number = shard_rank * heads_here // (HEADS // KV_HEADS)
    key_local = lax.dynamic_slice_in_dim(att_kv, kv_number * 2 * HD, HD, 1)
    value_local = lax.dynamic_slice_in_dim(att_kv, kv_number * 2 * HD + HD, HD, 1)
    query_heads = att_query.reshape(rows_here, heads_here, HD)
    late_queries = query_heads[half_rows:]
    query_places = stored_positions(ctx_rank * rows_here, rows_here, half_rows, ctx_count)
    same_visible = query_places[:, None] >= query_places[None, :]
    score_scale = HD ** (-0.5)

    def earlier_shard(running, key_shard, value_shard):
        return attend_rows(
            running, query_heads, key_shard[:half_rows], value_shard[:half_rows], None, score_scale
        )

    def same_shard(running, key_shard, value_shard):
        return attend_rows(running, query_heads, key_shard, value_shard, same_visible, score_scale)

    def later_shard(running, key_shard, value_shard):
        late_part = tuple((member[half_rows:] for member in running))
        renewed = attend_rows(late_part, late_queries, key_shard, value_shard, None, score_scale)
        return tuple(
            (
                jnp.concatenate([member[:half_rows], latest], axis=0)
                for member, latest in zip(running, renewed)
            )
        )

    start_running = (
        jnp.full((rows_here, heads_here), NEGATIVE, jnp.float32),
        jnp.zeros((rows_here, heads_here), jnp.float32),
        jnp.zeros((rows_here, heads_here, HD), jnp.float32),
    )
    key_block = lax.all_gather(key_local, "ctx", axis=0, tiled=True)
    value_block = lax.all_gather(value_local, "ctx", axis=0, tiled=True)
    piece_rows = key_block.shape[0]

    def one_shard(number, current):
        offset = number * rows_here
        key_shard = lax.dynamic_slice_in_dim(key_block, offset, rows_here, 0)
        value_shard = lax.dynamic_slice_in_dim(value_block, offset, rows_here, 0)
        shard_number = offset // rows_here
        branch = jnp.clip(shard_number - ctx_rank, -1, 1) + 1
        return lax.switch(
            branch, [earlier_shard, same_shard, later_shard], current, key_shard, value_shard
        )

    run_max, run_sum, run_acc = lax.fori_loop(0, piece_rows // rows_here, one_shard, start_running)
    gate_heads = jax.nn.sigmoid(att_gate.reshape(rows_here, heads_here, HD).astype(jnp.float32))
    att_heads = (
        (run_acc / run_sum[:, :, None] * gate_heads)
        .astype(jnp.bfloat16)
        .reshape(rows_here, heads_here * HD)
    )
    partial_term = jnp.dot(att_heads, out_weight, preferred_element_type=jnp.float32)
    col_width = residual.shape[1]
    col_start = shard_rank * col_width
    placed = lax.dynamic_slice_in_dim(partial_term, col_start, col_width, 1) + residual.astype(
        jnp.float32
    )
    partial_term = lax.dynamic_update_slice_in_dim(partial_term, placed, col_start, 1)
    hidden = lax.psum(partial_term.astype(jnp.bfloat16), ("head", "sub")).astype(jnp.float32)
    mean_square = jnp.mean(hidden * hidden, axis=1, keepdims=True)
    normed = (hidden * lax.rsqrt(mean_square + EPSILON) * norm_gain).astype(jnp.bfloat16)
    new_residual = lax.dynamic_slice_in_dim(hidden, col_start, col_width, 1).astype(jnp.bfloat16)
    mixed_cols = jnp.dot(normed, in_weight, preferred_element_type=jnp.float32)
    beta_logits = jnp.dot(normed, beta_weight, preferred_element_type=jnp.float32)
    key_here = in_weight.shape[1] // (2 * DK + 2 * DV)
    value_here = 2 * key_here
    grouped = mixed_cols.reshape(rows_here, key_here, 2 * DK + 2 * DV)
    query_unit = jnp.repeat(unit_rows(jax.nn.silu(grouped[:, :, :DK])) * DK ** (-0.5), 2, axis=1)
    key_unit = jnp.repeat(unit_rows(jax.nn.silu(grouped[:, :, DK : 2 * DK])), 2, axis=1)
    value_all = jax.nn.silu(grouped[:, :, 2 * DK :]).reshape(rows_here, value_here, DV)
    beta_all = jax.nn.sigmoid(beta_logits)
    local_out, read_rows, transition, offset_state = jax.vmap(block_terms)(
        to_blocks(query_unit, half_rows),
        to_blocks(key_unit, half_rows),
        to_blocks(value_all, half_rows),
        to_blocks(beta_all[:, :, None], half_rows)[:, :, 0],
        to_blocks(log_decay[:, :, None], half_rows)[:, :, 0],
    )
    transition = transition.reshape(value_here, 2, DK, DK)
    offset_state = offset_state.reshape(value_here, 2, DK, DV)
    early_map, late_map = (transition[:, 0], transition[:, 1])
    early_offset, late_offset = (offset_state[:, 0], offset_state[:, 1])
    last_rank = ctx_count - 1
    zero_states = jnp.zeros_like(early_offset)

    def early_turn(number, incoming):
        return passed_along(
            apply_map(early_map, early_offset, incoming).astype(jnp.bfloat16), "ctx", 1
        ).astype(jnp.float32)

    early_in = lax.fori_loop(0, ctx_count - 1, early_turn, zero_states)
    early_end = apply_map(early_map, early_offset, early_in)
    late_start = jnp.where(ctx_rank == last_rank, early_end, zero_states)

    def late_turn(number, incoming):
        moved = passed_along(
            apply_map(late_map, late_offset, incoming).astype(jnp.bfloat16), "ctx", -1
        ).astype(jnp.float32)
        return jnp.where(ctx_rank == last_rank, early_end, moved)

    late_in = lax.fori_loop(0, ctx_count - 1, late_turn, late_start)
    states_in = jnp.stack([early_in, late_in], axis=1)
    block_out = local_out.reshape(value_here, 2, half_rows, DV) + jnp.einsum(
        "hbck,hbkv->hbcv",
        read_rows.reshape(value_here, 2, half_rows, DK),
        states_in,
        precision=TOP_PRECISION,
    )
    token_out = block_out.transpose(1, 2, 0, 3).reshape(rows_here, value_here, DV)
    out_square = jnp.mean(token_out * token_out, axis=2, keepdims=True)
    delta_out = (token_out * lax.rsqrt(out_square + EPSILON) * delta_gain).astype(jnp.bfloat16)
    return (new_residual, delta_out.reshape(rows_here, value_here * DV))


KEY_HEADS = 16
IN_VMEM = pl.BlockSpec(memory_space=pltpu.VMEM)
IN_HBM = pl.BlockSpec(memory_space=pl.ANY)
MIB = 2**20
LANES = 128


def owners_fit(mesh):
    shards = mesh.shape["head"] * mesh.shape["sub"]
    key_here = KEY_HEADS // shards
    return mesh.shape["head"] == 2 and mesh.shape["sub"] == 2 and key_here == mesh.shape["ctx"]


def in_vmem(array):
    return pltpu.with_memory_space_constraint(array, pltpu.VMEM)


def in_hbm(array):
    return pltpu.with_memory_space_constraint(array, pltpu.HBM)


def vmem_call(kernel, outs, operands, scratch=(), limit=16, aliases=None, last=False, cost=None):
    make = jax.ShapeDtypeStruct if last else pltpu.VMEM
    return pl.pallas_call(
        kernel,
        out_shape=[make(shape, dtype) for shape, dtype in outs],
        in_specs=[IN_VMEM] * len(operands),
        out_specs=[IN_VMEM] * len(outs),
        scratch_shapes=list(scratch),
        input_output_aliases=aliases or {},
        cost_estimate=cost,
        compiler_params=pltpu.CompilerParams(vmem_limit_bytes=limit * MIB),
    )(*[in_vmem(operand) for operand in operands])


def rotated(value, axis, steps):
    count = lax.axis_size(axis)
    return lax.ppermute(value, axis, [(i, (i + steps) % count) for i in range(count)])


def dot(left, right, dims=((1,), (0,))):
    return lax.dot_general(left, right, (dims, ((), ())), preferred_element_type=jnp.float32)


def halves(value):
    high = value.astype(jnp.bfloat16)
    return high, (value - high.astype(jnp.float32)).astype(jnp.bfloat16)


def dot3(left, right):
    left_high, left_low = halves(left)
    right_high, right_low = halves(right)
    return dot(left_high, right_high) + (dot(left_high, right_low) + dot(left_low, right_high))


def sigmoid(value):
    return 1.0 / (1.0 + jnp.exp(-value))


def silu(value):
    return value / (1.0 + jnp.exp(-value))


def piece_kernel(kv_ref, piece_ref, own_ref, sems):
    start = pl.multiple_of(lax.axis_index("head") * 2 * HD, 2 * HD)
    share = pl.multiple_of(start + lax.axis_index("sub") * HD, HD)
    first = pltpu.make_async_copy(kv_ref.at[:, pl.ds(share, HD)], piece_ref, sems.at[0])
    second = pltpu.make_async_copy(kv_ref.at[:, pl.ds(start, 2 * HD)], own_ref, sems.at[1])
    first.start()
    second.start()
    first.wait()
    second.wait()


def fetch_kernel(*refs):
    count = len(refs) // 2
    copies = [
        pltpu.make_async_copy(refs[n], refs[count + n], refs[-1].at[n]) for n in range(count)
    ]
    for copy in copies:
        copy.start()
    for copy in copies:
        copy.wait()


def fetched(*arrays):
    moved = sum(array.size * array.dtype.itemsize for array in arrays)
    return pl.pallas_call(
        fetch_kernel,
        out_shape=[pltpu.VMEM(array.shape, array.dtype) for array in arrays],
        in_specs=[IN_HBM] * len(arrays),
        out_specs=[IN_VMEM] * len(arrays),
        scratch_shapes=[pltpu.SemaphoreType.DMA((len(arrays),))],
        compiler_params=pltpu.CompilerParams(vmem_limit_bytes=4 * MIB),
        cost_estimate=pl.CostEstimate(flops=0, bytes_accessed=moved, transcendentals=0),
    )(*[in_hbm(array) for array in arrays])


def attention_kernel(
    query_ref, gate_ref, own_ref, mine1, mine2, mine3, twin1, twin2, twin3, weight_ref, residual_ref,
    keep_ref, send_ref, keys, values, heads, partial,
):
    rows, head_columns = query_ref.shape
    half = rows // 2
    ctx_rank, head_rank, sub_rank = (lax.axis_index(name) for name in ("ctx", "head", "sub"))
    count = 4
    keys[0:rows] = own_ref[:, 0:HD]
    values[0:rows] = own_ref[:, HD : 2 * HD]

    @pl.when(sub_rank == 0)
    def _():
        for step, (mine, twin) in enumerate(((mine1, twin1), (mine2, twin2), (mine3, twin3)), 1):
            keys[step * rows : (step + 1) * rows] = mine[...]
            values[step * rows : (step + 1) * rows] = twin[...]

    @pl.when(sub_rank != 0)
    def _():
        for step, (mine, twin) in enumerate(((mine1, twin1), (mine2, twin2), (mine3, twin3)), 1):
            keys[step * rows : (step + 1) * rows] = twin[...]
            values[step * rows : (step + 1) * rows] = mine[...]

    def places(row, device):
        within = row % rows
        block = jnp.where(within < half, device, 2 * count - 1 - device)
        return block * half + within % half

    query_place = places(lax.broadcasted_iota(jnp.int32, (rows, 1), 0), ctx_rank)
    key_row = lax.broadcasted_iota(jnp.int32, (1, count * rows), 1)
    key_place = places(key_row, (ctx_rank - key_row // rows + count) % count)
    visible = query_place >= key_place
    for head in range(head_columns // HD):
        columns = slice(head * HD, (head + 1) * HD)
        scores = dot(query_ref[:, columns], keys[...], ((1,), (1,))) * HD ** (-0.5)
        scores = jnp.where(visible, scores, NEGATIVE)
        weights = jnp.exp(scores - jnp.max(scores, axis=1, keepdims=True))
        total = jnp.sum(weights, axis=1, keepdims=True)
        gathered = dot(weights.astype(jnp.bfloat16), values[...])
        gate = sigmoid(gate_ref[:, columns].astype(jnp.float32))
        heads[:, columns] = (gathered / total * gate).astype(jnp.bfloat16)
    partial[...] = dot(heads[...], weight_ref[...])
    width = residual_ref.shape[1]
    mid = partial.shape[1] // 2
    own_columns = pl.ds(pl.multiple_of((head_rank * 2 + sub_rank) * width, width), width)
    partial[:, own_columns] += residual_ref[...].astype(jnp.float32)
    keep_ref[...] = partial[:, pl.ds(pl.multiple_of(sub_rank * mid, mid), mid)]
    send_ref[...] = partial[:, pl.ds(pl.multiple_of((1 - sub_rank) * mid, mid), mid)].astype(jnp.bfloat16)


def chip_sum_kernel(keep_ref, came_ref, sum_ref, send_ref):
    total = keep_ref[...] + came_ref[...].astype(jnp.float32)
    sum_ref[...] = total
    send_ref[...] = total.astype(jnp.bfloat16)


def hidden_kernel(keep_ref, came_ref, hidden_ref):
    hidden_ref[...] = (keep_ref[...] + came_ref[...].astype(jnp.float32)).astype(jnp.bfloat16)


def norm_kernel(own_ref, twin_ref, gain_ref, beta_ref, decay_ref, residual_ref, normed_ref, extra_ref):
    head_rank, sub_rank = lax.axis_index("head"), lax.axis_index("sub")
    mid = own_ref.shape[1]
    width = residual_ref.shape[1]
    columns = pl.ds(pl.multiple_of(sub_rank * width, width), width)

    @pl.when(sub_rank == head_rank)
    def _():
        residual_ref[...] = own_ref[:, columns]

    @pl.when(sub_rank != head_rank)
    def _():
        residual_ref[...] = twin_ref[:, columns]

    own, twin = own_ref[...].astype(jnp.float32), twin_ref[...].astype(jnp.float32)
    squares = jnp.sum(own * own, axis=1, keepdims=True) + jnp.sum(twin * twin, axis=1, keepdims=True)
    scale = lax.rsqrt(squares / (2 * mid) + EPSILON)
    own_half = pl.ds(pl.multiple_of(sub_rank * mid, mid), mid)
    twin_half = pl.ds(pl.multiple_of((1 - sub_rank) * mid, mid), mid)
    normed_ref[:, own_half] = (own * scale * gain_ref[:, own_half]).astype(jnp.bfloat16)
    normed_ref[:, twin_half] = (twin * scale * gain_ref[:, twin_half]).astype(jnp.bfloat16)
    values = decay_ref.shape[0]
    extra_ref[0:values] = decay_ref[...]
    extra_ref[values : 2 * values] = sigmoid(dot(beta_ref[...], normed_ref[...], ((1,), (1,))))


def payload_kernel(step, normed_ref, weight_ref, extra_ref, payload_ref, small):
    rows = normed_ref.shape[0]
    group = 2 * DK + 2 * DV
    count = 4
    target = (lax.axis_index("ctx") + step) % count
    columns = pl.ds(pl.multiple_of(target * group, group), group)
    mixed = silu(dot(normed_ref[...], weight_ref[:, columns]))
    query, key = mixed[:, :DK], mixed[:, DK : 2 * DK]
    payload_ref[0:rows] = (unit_rows(query) * DK ** (-0.5)).astype(jnp.bfloat16)
    payload_ref[rows : 2 * rows] = unit_rows(key).astype(jnp.bfloat16)
    payload_ref[2 * rows : 3 * rows] = mixed[:, 2 * DK : 2 * DK + DV].astype(jnp.bfloat16)
    payload_ref[3 * rows : 4 * rows] = mixed[:, 2 * DK + DV :].astype(jnp.bfloat16)
    values = extra_ref.shape[0] // 2
    small[...] = jnp.zeros_like(small)
    for place, base in ((0, 0), (4, values)):
        full = extra_ref[pl.ds(base + 2 * target, 2), :]
        high = full.astype(jnp.bfloat16).astype(jnp.float32)
        small[place : place + 2] = high
        small[place + 2 : place + 4] = full - high
    payload_ref[4 * rows : 4 * rows + 16] = small[...].astype(jnp.bfloat16)


def unit_lower_inverses(stricts, row, column):
    inner = (row >> 3) == (column >> 3)
    identity = jnp.where(row == column, 1.0, 0.0)
    smalls = [jnp.where(inner, strict, 0.0) for strict in stricts]
    rests = [jnp.where(inner, 0.0, strict) for strict in stricts]
    seconds = [dot3(small, small) for small in smalls]
    inverses = [identity - small for small in smalls]
    fourths = [dot3(second, second) for second in seconds]
    inverses = [inverse + dot3(inverse, second) for inverse, second in zip(inverses, seconds)]
    inverses = [inverse + dot3(inverse, fourth) for inverse, fourth in zip(inverses, fourths)]
    steps = [dot3(inverse, rest) for inverse, rest in zip(inverses, rests)]
    results = [inverse - dot3(step, inverse) for inverse, step in zip(inverses, steps)]
    doubles = [dot3(step, step) for step in steps]
    quads = [dot3(double, double) for double in doubles]
    results = [result + dot3(double, result) for result, double in zip(results, doubles)]
    return [result + dot3(quad, result) for result, quad in zip(results, quads)]


def block_kernel(step, payload_ref, *refs):
    offset_ref, linear_ref, local_ref, growth_ref = refs[-4:]
    count = 4
    source = (lax.axis_index("ctx") + count - step) % count
    rows = (payload_ref.shape[0] - 16) // 4
    half = rows // 2
    shift = half.bit_length() - 1
    row = lax.broadcasted_iota(jnp.int32, (rows, 1), 0)
    column = lax.broadcasted_iota(jnp.int32, (1, rows), 1)
    together = (row >> shift) == (column >> shift)
    inclusive = together & (row >= column)
    strictly = together & (row > column)
    early = column < half
    below = jnp.where(inclusive, 1.0, 0.0).astype(jnp.bfloat16)
    diagonal = jnp.where(row == column, 1.0, 0.0).astype(jnp.bfloat16)
    heads = range(2)
    query, key = payload_ref[0:rows], payload_ref[rows : 2 * rows]
    extra = payload_ref[4 * rows : 4 * rows + 16]
    sums_row = dot(extra, below, ((1,), (1,)))
    turned = dot(jnp.concatenate([below, diagonal], axis=0), extra, ((1,), (1,)))
    key_gram = dot(key, key, ((1,), (1,)))
    total_rows = [sums_row[h : h + 1] + sums_row[h + 2 : h + 3] for h in heads]
    totals = [turned[:rows, h : h + 1] + turned[:rows, h + 2 : h + 3] for h in heads]
    betas = [turned[rows:, h + 4 : h + 5] + turned[rows:, h + 6 : h + 7] for h in heads]
    decays = [jnp.exp(jnp.where(inclusive, totals[h] - total_rows[h], NEGATIVE)) for h in heads]
    stricts = [jnp.where(strictly, betas[h] * key_gram * decays[h], 0.0) for h in heads]
    query_gram = dot(query, key, ((1,), (1,)))
    key_wide = key.astype(jnp.float32)
    key_turned = jnp.transpose(key_wide)
    growths = [jnp.exp(total) for total in totals]
    values = [payload_ref[(2 + h) * rows : (3 + h) * rows].astype(jnp.float32) for h in heads]
    rights = [
        jnp.concatenate([betas[h] * values[h], (betas[h] * growths[h]) * key_wide], axis=1).astype(jnp.bfloat16)
        for h in heads
    ]
    grams = [(query_gram * decays[h]).astype(jnp.bfloat16) for h in heads]
    ends = [jnp.where(early, total[:, half - 1 : half], total[:, rows - 1 : rows]) for total in total_rows]
    carried = [key_turned * jnp.exp(ends[h] - total_rows[h]) for h in heads]
    lefts = [
        jnp.concatenate([jnp.where(early, keys, 0.0), jnp.where(early, 0.0, keys)], axis=0).astype(jnp.bfloat16)
        for keys in carried
    ]
    inverses = [halves(inverse) for inverse in unit_lower_inverses(stricts, row, column)]
    solved = [
        (dot(high, right) + dot(low, right)).astype(jnp.bfloat16) for (high, low), right in zip(inverses, rights)
    ]
    moved = [dot(jnp.concatenate([lefts[h], grams[h]], axis=0), solved[h]) for h in heads]
    for h in heads:
        attended = moved[h][2 * DK :]
        local_ref[source, h] = attended[:, :DV]
        reads = (growths[h] * query.astype(jnp.float32) - attended[:, DV:]).astype(jnp.bfloat16)
        growth = jnp.exp(ends[h])
        for block in range(2):
            state = moved[h][block * DK : (block + 1) * DK]
            offset_ref[source, h, block] = state[:, :DV]
            linear_ref[source, h, block, 0:DK] = state[:, DV:].astype(jnp.bfloat16)
            linear_ref[source, h, block, DK : DK + half] = reads[block * half : (block + 1) * half]
            last = (block + 1) * half - 1
            growth_ref[source, h, block] = jnp.broadcast_to(growth[:, last : last + 1], growth_ref.shape[3:])


def scan_kernel(offset_ref, linear_ref, local_ref, growth_ref, gain_ref, own_ref, back1, back2, back3, outs):
    count = offset_ref.shape[0]
    half = local_ref.shape[2] // 2
    rank = lax.axis_index("ctx")
    states = [None, None]
    for number in range(2 * count):
        source, block = (number, 0) if number < count else (2 * count - 1 - number, 1)
        block_rows = slice(block * half, (block + 1) * half)
        for head in range(2):
            out = local_ref[source, head, block_rows]
            state = offset_ref[source, head, block]
            if states[head] is not None:
                moved = dot(linear_ref[source, head, block], states[head].astype(jnp.bfloat16))
                out = out + moved[DK:]
                state = state - moved[:DK] + growth_ref[source, head, block, 0:1] * states[head]
            states[head] = state
            scale = lax.rsqrt(jnp.mean(out * out, axis=1, keepdims=True) + EPSILON)
            outs[source, block_rows, head * DV : (head + 1) * DV] = (out * scale * gain_ref[...]).astype(jnp.bfloat16)
    own_ref[...] = outs[rank]
    for step, back in enumerate((back1, back2, back3), 1):
        back[...] = outs[(rank + count - step) % count]


def place_kernel(own_ref, back1, back2, back3, out_ref):
    count = 4
    width = own_ref.shape[1]
    rank = lax.axis_index("ctx")
    for step, back in enumerate((own_ref, back1, back2, back3)):
        columns = pl.ds(pl.multiple_of((rank + step) % count * width, width), width)
        out_ref[:, columns] = back[...]


def owner_local(
    att_query,
    att_gate,
    att_kv,
    residual,
    out_weight,
    norm_gain,
    in_weight,
    beta_weight,
    log_decay,
    delta_gain,
):
    bf16, f32 = jnp.bfloat16, jnp.float32
    rows, head_columns = att_query.shape
    model = out_weight.shape[1]
    half_model = model // 2
    steps = (1, 2, 3)
    piece, own_kv = pl.pallas_call(
        piece_kernel,
        out_shape=[pltpu.VMEM((rows, HD), bf16), pltpu.VMEM((rows, 2 * HD), bf16)],
        in_specs=[IN_HBM],
        out_specs=[IN_VMEM] * 2,
        scratch_shapes=[pltpu.SemaphoreType.DMA((2,))],
        compiler_params=pltpu.CompilerParams(vmem_limit_bytes=4 * MIB),
    )(in_hbm(att_kv))
    mine = [rotated(piece, "ctx", step) for step in steps]
    piece, *late = lax.optimization_barrier((piece, att_query, att_gate, out_weight, residual))
    late = fetched(*late)
    mine[2], (att_query, att_gate, out_weight, residual) = lax.optimization_barrier((mine[2], late))
    twin = [rotated(part, "sub", 1) for part in mine]
    keep, send = vmem_call(
        attention_kernel,
        [((rows, half_model), f32), ((rows, half_model), bf16)],
        [att_query, att_gate, own_kv, *mine, *twin, out_weight, residual],
        [
            pltpu.VMEM((4 * rows, HD), bf16),
            pltpu.VMEM((4 * rows, HD), bf16),
            pltpu.VMEM((rows, head_columns), bf16),
            pltpu.VMEM((rows, model), f32),
        ],
    )
    chip_sum, send = vmem_call(
        chip_sum_kernel,
        [((rows, half_model), f32), ((rows, half_model), bf16)],
        [keep, rotated(send, "sub", 1)],
    )
    other_sum = rotated(send, "head", 1)
    send, *late = lax.optimization_barrier((send, in_weight, norm_gain[None, :], beta_weight.T, log_decay.T))
    late = fetched(*late)
    other_sum, (in_weight, norm_gain, beta_weight, log_decay) = lax.optimization_barrier((other_sum, late))
    hidden = vmem_call(hidden_kernel, [((rows, half_model), bf16)], [chip_sum, other_sum])[0]
    value_here = log_decay.shape[0]
    new_residual, normed, extra = vmem_call(
        norm_kernel,
        [(residual.shape, bf16), ((rows, model), bf16), ((2 * value_here, rows), f32)],
        [hidden, rotated(hidden, "sub", 1), norm_gain, beta_weight, log_decay],
    )
    payloads = [
        vmem_call(
            functools.partial(payload_kernel, step),
            [((4 * rows + 16, LANES), bf16)],
            [normed, in_weight, extra],
            [pltpu.VMEM((16, LANES), f32)],
        )[0]
        for step in range(4)
    ]
    came = [payloads[0]] + [rotated(payloads[step], "ctx", step) for step in steps]
    half = rows // 2
    terms_shapes = [
        ((4, 2, 2, DK, DV), f32),
        ((4, 2, 2, DK + half, DK), bf16),
        ((4, 2, rows, DV), f32),
        ((4, 2, 2, 8, LANES), f32),
    ]
    terms = []
    for step in range(4):
        terms = vmem_call(
            functools.partial(block_kernel, step),
            terms_shapes,
            [came[step], *terms],
            aliases={1 + i: i for i in range(4)} if terms else None,
        )
    own, *backs = vmem_call(
        scan_kernel,
        [((rows, 2 * DV), bf16)] * 4,
        [*terms, delta_gain[None, :]],
        [pltpu.VMEM((4, rows, 2 * DV), bf16)],
    )
    backs = [rotated(back, "ctx", -step) for step, back in zip(steps, backs)]
    delta_out = vmem_call(place_kernel, [((rows, value_here * DV), bf16)], [own, *backs], last=True)[0]
    return (new_residual, delta_out)


def solution(mesh):
    local = owner_local if owners_fit(mesh) else hop_local
    return jax.shard_map(
        local,
        mesh=mesh,
        in_specs=(
            P(("groups", "ctx"), ("head", "sub")),
            P(("groups", "ctx"), ("head", "sub")),
            P(("groups", "ctx"), None),
            P(("groups", "ctx"), ("head", "sub")),
            P(("head", "sub"), None),
            P(),
            P(None, ("head", "sub")),
            P(None, ("head", "sub")),
            P(("groups", "ctx"), ("head", "sub")),
            P(),
        ),
        out_specs=(P(("groups", "ctx"), ("head", "sub")), P(("groups", "ctx"), ("head", "sub"))),
        check_vma=False,
    )
```

```python
import functools

import jax
import jax.numpy as jnp
from jax import lax
from jax.experimental import pallas as pl
from jax.experimental.pallas import tpu as pltpu
from jax.sharding import PartitionSpec as P

HEADS = 16
KV_HEADS = 2
HD = 256
DK = 128
DV = 128


TOP_PRECISION = lax.Precision.HIGHEST
EPSILON = 1e-06
NEGATIVE = -1e30


def passed_along(value, axis, steps):
    count = lax.axis_size(axis)
    initial, last = (max(0, -steps), min(count, count - steps))
    return lax.ppermute(value, axis, [(source, source + steps) for source in range(initial, last)])


def stored_positions(first_row, row_total, half_rows, ctx_count):
    row_index = first_row + jnp.arange(row_total, dtype=jnp.int32)
    device_of = row_index // (2 * half_rows)
    within_dev = row_index % (2 * half_rows)
    block_number = jnp.where(within_dev < half_rows, device_of, 2 * ctx_count - 1 - device_of)
    return block_number * half_rows + within_dev % half_rows


def unit_rows(matrix):
    return matrix * lax.rsqrt(jnp.sum(matrix * matrix, axis=-1, keepdims=True) + EPSILON)


def to_blocks(array, half_rows):
    heads_count = array.shape[1]
    width = array.shape[2]
    shaped = array.reshape(2, half_rows, heads_count, width).transpose(2, 0, 1, 3)
    return shaped.reshape(heads_count * 2, half_rows, width)


def block_terms(query_rows, key_rows, value_rows, beta_rows, decay_rows):
    length = query_rows.shape[0]
    cumulative = jnp.cumsum(decay_rows)
    position = jnp.arange(length)
    on_or_below = position[:, None] >= position[None, :]
    strictly_below = position[:, None] > position[None, :]
    decay_gap = cumulative[:, None] - cumulative[None, :]
    decay_grid = jnp.where(on_or_below, jnp.exp(jnp.where(on_or_below, decay_gap, 0.0)), 0.0)
    key_gram = jnp.dot(key_rows, key_rows.T, precision=TOP_PRECISION)
    system = jnp.eye(length, dtype=jnp.float32) + jnp.where(
        strictly_below, beta_rows[:, None] * key_gram * decay_grid, 0.0
    )
    growth = jnp.exp(cumulative)
    right_side = beta_rows[:, None] * jnp.concatenate(
        [value_rows, growth[:, None] * key_rows], axis=1
    )
    solved = jax.scipy.linalg.solve_triangular(system, right_side, lower=True, unit_diagonal=True)
    update_rows = solved[:, : value_rows.shape[1]]
    weight_rows = solved[:, value_rows.shape[1] :]
    attend_grid = jnp.where(
        on_or_below, jnp.dot(query_rows, key_rows.T, precision=TOP_PRECISION) * decay_grid, 0.0
    )
    local_out = jnp.dot(attend_grid, update_rows, precision=TOP_PRECISION)
    read_rows = growth[:, None] * query_rows - jnp.dot(
        attend_grid, weight_rows, precision=TOP_PRECISION
    )
    carried_keys = jnp.exp(cumulative[-1] - cumulative)[:, None] * key_rows
    identity_map = jnp.eye(key_rows.shape[1], dtype=jnp.float32)
    transition = jnp.exp(cumulative[-1]) * identity_map - jnp.dot(
        carried_keys.T, weight_rows, precision=TOP_PRECISION
    )
    offset_state = jnp.dot(carried_keys.T, update_rows, precision=TOP_PRECISION)
    return (local_out, read_rows, transition, offset_state)


def apply_map(matrix_maps, offsets, states):
    return jnp.einsum("hij,hjk->hik", matrix_maps, states, precision=TOP_PRECISION) + offsets


def attend_rows(running, query_block, key_block, value_block, visible, score_scale):
    run_max, run_sum, run_acc = running
    scores = (
        jnp.einsum("rhd,kd->rhk", query_block, key_block, preferred_element_type=jnp.float32)
        * score_scale
    )
    if visible is not None:
        scores = jnp.where(visible[:, None, :], scores, NEGATIVE)
    new_max = jnp.maximum(run_max, jnp.max(scores, axis=2))
    weights = jnp.exp(scores - new_max[:, :, None])
    if visible is not None:
        weights = jnp.where(visible[:, None, :], weights, 0.0)
    rescale = jnp.exp(run_max - new_max)
    run_sum = run_sum * rescale + jnp.sum(weights, axis=2)
    added = jnp.einsum(
        "rhk,kd->rhd", weights.astype(jnp.bfloat16), value_block, preferred_element_type=jnp.float32
    )
    run_acc = run_acc * rescale[:, :, None] + added
    return (new_max, run_sum, run_acc)


def hop_local(
    att_query,
    att_gate,
    att_kv,
    residual,
    out_weight,
    norm_gain,
    in_weight,
    beta_weight,
    log_decay,
    delta_gain,
):
    ctx_count = lax.axis_size("ctx")
    ctx_rank = lax.axis_index("ctx")
    shard_rank = lax.axis_index(("head", "sub"))
    rows_here = att_query.shape[0]
    half_rows = rows_here // 2
    heads_here = att_query.shape[1] // HD
    kv_number = shard_rank * heads_here // (HEADS // KV_HEADS)
    key_local = lax.dynamic_slice_in_dim(att_kv, kv_number * 2 * HD, HD, 1)
    value_local = lax.dynamic_slice_in_dim(att_kv, kv_number * 2 * HD + HD, HD, 1)
    query_heads = att_query.reshape(rows_here, heads_here, HD)
    late_queries = query_heads[half_rows:]
    query_places = stored_positions(ctx_rank * rows_here, rows_here, half_rows, ctx_count)
    same_visible = query_places[:, None] >= query_places[None, :]
    score_scale = HD ** (-0.5)

    def earlier_shard(running, key_shard, value_shard):
        return attend_rows(
            running, query_heads, key_shard[:half_rows], value_shard[:half_rows], None, score_scale
        )

    def same_shard(running, key_shard, value_shard):
        return attend_rows(running, query_heads, key_shard, value_shard, same_visible, score_scale)

    def later_shard(running, key_shard, value_shard):
        late_part = tuple((member[half_rows:] for member in running))
        renewed = attend_rows(late_part, late_queries, key_shard, value_shard, None, score_scale)
        return tuple(
            (
                jnp.concatenate([member[:half_rows], latest], axis=0)
                for member, latest in zip(running, renewed)
            )
        )

    start_running = (
        jnp.full((rows_here, heads_here), NEGATIVE, jnp.float32),
        jnp.zeros((rows_here, heads_here), jnp.float32),
        jnp.zeros((rows_here, heads_here, HD), jnp.float32),
    )
    key_block = lax.all_gather(key_local, "ctx", axis=0, tiled=True)
    value_block = lax.all_gather(value_local, "ctx", axis=0, tiled=True)
    piece_rows = key_block.shape[0]

    def one_shard(number, current):
        offset = number * rows_here
        key_shard = lax.dynamic_slice_in_dim(key_block, offset, rows_here, 0)
        value_shard = lax.dynamic_slice_in_dim(value_block, offset, rows_here, 0)
        shard_number = offset // rows_here
        branch = jnp.clip(shard_number - ctx_rank, -1, 1) + 1
        return lax.switch(
            branch, [earlier_shard, same_shard, later_shard], current, key_shard, value_shard
        )

    run_max, run_sum, run_acc = lax.fori_loop(0, piece_rows // rows_here, one_shard, start_running)
    gate_heads = jax.nn.sigmoid(att_gate.reshape(rows_here, heads_here, HD).astype(jnp.float32))
    att_heads = (
        (run_acc / run_sum[:, :, None] * gate_heads)
        .astype(jnp.bfloat16)
        .reshape(rows_here, heads_here * HD)
    )
    partial_term = jnp.dot(att_heads, out_weight, preferred_element_type=jnp.float32)
    col_width = residual.shape[1]
    col_start = shard_rank * col_width
    placed = lax.dynamic_slice_in_dim(partial_term, col_start, col_width, 1) + residual.astype(
        jnp.float32
    )
    partial_term = lax.dynamic_update_slice_in_dim(partial_term, placed, col_start, 1)
    hidden = lax.psum(partial_term.astype(jnp.bfloat16), ("head", "sub")).astype(jnp.float32)
    mean_square = jnp.mean(hidden * hidden, axis=1, keepdims=True)
    normed = (hidden * lax.rsqrt(mean_square + EPSILON) * norm_gain).astype(jnp.bfloat16)
    new_residual = lax.dynamic_slice_in_dim(hidden, col_start, col_width, 1).astype(jnp.bfloat16)
    mixed_cols = jnp.dot(normed, in_weight, preferred_element_type=jnp.float32)
    beta_logits = jnp.dot(normed, beta_weight, preferred_element_type=jnp.float32)
    key_here = in_weight.shape[1] // (2 * DK + 2 * DV)
    value_here = 2 * key_here
    grouped = mixed_cols.reshape(rows_here, key_here, 2 * DK + 2 * DV)
    query_unit = jnp.repeat(unit_rows(jax.nn.silu(grouped[:, :, :DK])) * DK ** (-0.5), 2, axis=1)
    key_unit = jnp.repeat(unit_rows(jax.nn.silu(grouped[:, :, DK : 2 * DK])), 2, axis=1)
    value_all = jax.nn.silu(grouped[:, :, 2 * DK :]).reshape(rows_here, value_here, DV)
    beta_all = jax.nn.sigmoid(beta_logits)
    local_out, read_rows, transition, offset_state = jax.vmap(block_terms)(
        to_blocks(query_unit, half_rows),
        to_blocks(key_unit, half_rows),
        to_blocks(value_all, half_rows),
        to_blocks(beta_all[:, :, None], half_rows)[:, :, 0],
        to_blocks(log_decay[:, :, None], half_rows)[:, :, 0],
    )
    transition = transition.reshape(value_here, 2, DK, DK)
    offset_state = offset_state.reshape(value_here, 2, DK, DV)
    early_map, late_map = (transition[:, 0], transition[:, 1])
    early_offset, late_offset = (offset_state[:, 0], offset_state[:, 1])
    last_rank = ctx_count - 1
    zero_states = jnp.zeros_like(early_offset)

    def early_turn(number, incoming):
        return passed_along(
            apply_map(early_map, early_offset, incoming).astype(jnp.bfloat16), "ctx", 1
        ).astype(jnp.float32)

    early_in = lax.fori_loop(0, ctx_count - 1, early_turn, zero_states)
    early_end = apply_map(early_map, early_offset, early_in)
    late_start = jnp.where(ctx_rank == last_rank, early_end, zero_states)

    def late_turn(number, incoming):
        moved = passed_along(
            apply_map(late_map, late_offset, incoming).astype(jnp.bfloat16), "ctx", -1
        ).astype(jnp.float32)
        return jnp.where(ctx_rank == last_rank, early_end, moved)

    late_in = lax.fori_loop(0, ctx_count - 1, late_turn, late_start)
    states_in = jnp.stack([early_in, late_in], axis=1)
    block_out = local_out.reshape(value_here, 2, half_rows, DV) + jnp.einsum(
        "hbck,hbkv->hbcv",
        read_rows.reshape(value_here, 2, half_rows, DK),
        states_in,
        precision=TOP_PRECISION,
    )
    token_out = block_out.transpose(1, 2, 0, 3).reshape(rows_here, value_here, DV)
    out_square = jnp.mean(token_out * token_out, axis=2, keepdims=True)
    delta_out = (token_out * lax.rsqrt(out_square + EPSILON) * delta_gain).astype(jnp.bfloat16)
    return (new_residual, delta_out.reshape(rows_here, value_here * DV))


KEY_HEADS = 16
IN_VMEM = pl.BlockSpec(memory_space=pltpu.VMEM)
IN_HBM = pl.BlockSpec(memory_space=pl.ANY)
MIB = 2**20
LANES = 128


def owners_fit(mesh):
    shards = mesh.shape["head"] * mesh.shape["sub"]
    key_here = KEY_HEADS // shards
    return mesh.shape["head"] == 2 and mesh.shape["sub"] == 2 and key_here == mesh.shape["ctx"]


def in_vmem(array):
    return pltpu.with_memory_space_constraint(array, pltpu.VMEM)


def in_hbm(array):
    return pltpu.with_memory_space_constraint(array, pltpu.HBM)


def vmem_call(kernel, outs, operands, scratch=(), limit=16, aliases=None, last=False, cost=None):
    make = jax.ShapeDtypeStruct if last else pltpu.VMEM
    return pl.pallas_call(
        kernel,
        out_shape=[make(shape, dtype) for shape, dtype in outs],
        in_specs=[IN_VMEM] * len(operands),
        out_specs=[IN_VMEM] * len(outs),
        scratch_shapes=list(scratch),
        input_output_aliases=aliases or {},
        cost_estimate=cost,
        compiler_params=pltpu.CompilerParams(vmem_limit_bytes=limit * MIB),
    )(*[in_vmem(operand) for operand in operands])


def swapped(value, axis, mask=1):
    return lax.ppermute(value, axis, [(i, i ^ mask) for i in range(lax.axis_size(axis))])


def dot(left, right, dims=((1,), (0,))):
    return lax.dot_general(left, right, (dims, ((), ())), preferred_element_type=jnp.float32)


def halves(value):
    high = value.astype(jnp.bfloat16)
    return high, (value - high.astype(jnp.float32)).astype(jnp.bfloat16)


def dot3(left, right):
    left_high, left_low = halves(left)
    right_high, right_low = halves(right)
    return dot(left_high, right_high) + (dot(left_high, right_low) + dot(left_low, right_high))


def sigmoid(value):
    return 1.0 / (1.0 + jnp.exp(-value))


def silu(value):
    return value / (1.0 + jnp.exp(-value))


def piece_kernel(kv_ref, piece_ref, sem):
    start = (lax.axis_index("head") * 2 + lax.axis_index("sub")) * HD
    copy = pltpu.make_async_copy(kv_ref.at[:, pl.ds(pl.multiple_of(start, HD), HD)], piece_ref, sem)
    copy.start()
    copy.wait()


def fetch_kernel(*refs):
    count = len(refs) // 2
    copies = [
        pltpu.make_async_copy(refs[n], refs[count + n], refs[-1].at[n]) for n in range(count)
    ]
    for copy in copies:
        copy.start()
    for copy in copies:
        copy.wait()


def fetched(*arrays):
    moved = sum(array.size * array.dtype.itemsize for array in arrays)
    return pl.pallas_call(
        fetch_kernel,
        out_shape=[pltpu.VMEM(array.shape, array.dtype) for array in arrays],
        in_specs=[IN_HBM] * len(arrays),
        out_specs=[IN_VMEM] * len(arrays),
        scratch_shapes=[pltpu.SemaphoreType.DMA((len(arrays),))],
        compiler_params=pltpu.CompilerParams(vmem_limit_bytes=4 * MIB),
        cost_estimate=pl.CostEstimate(flops=0, bytes_accessed=moved, transcendentals=0),
    )(*[in_hbm(array) for array in arrays])


def attention_kernel(
    query_ref, gate_ref, kv_ref, mine1, mine2, mine3, twin1, twin2, twin3, weight_ref, residual_ref,
    heads_ref, send_ref, keys, values, sums,
):
    rows, head_columns = query_ref.shape
    half = rows // 2
    ctx_rank, head_rank, sub_rank = (lax.axis_index(name) for name in ("ctx", "head", "sub"))
    count = 4
    own_start = pl.multiple_of(head_rank * 2 * HD, 2 * HD)
    keys[0:rows] = kv_ref[:, pl.ds(own_start, HD)]
    values[0:rows] = kv_ref[:, pl.ds(own_start + HD, HD)]

    @pl.when(sub_rank == 0)
    def _():
        for mask, (mine, twin) in enumerate(((mine1, twin1), (mine2, twin2), (mine3, twin3)), 1):
            keys[mask * rows : (mask + 1) * rows] = mine[...]
            values[mask * rows : (mask + 1) * rows] = twin[...]

    @pl.when(sub_rank != 0)
    def _():
        for mask, (mine, twin) in enumerate(((mine1, twin1), (mine2, twin2), (mine3, twin3)), 1):
            keys[mask * rows : (mask + 1) * rows] = twin[...]
            values[mask * rows : (mask + 1) * rows] = mine[...]

    def places(row, device):
        within = row & (rows - 1)
        block = jnp.where(within < half, device, 2 * count - 1 - device)
        return block * half + (within & (half - 1))

    query_place = places(lax.broadcasted_iota(jnp.int32, (rows, 1), 0), ctx_rank)
    key_row = lax.broadcasted_iota(jnp.int32, (1, count * rows), 1)
    key_place = places(key_row, jnp.bitwise_xor(ctx_rank, key_row >> (rows.bit_length() - 1)))
    visible = query_place >= key_place
    for head in range(head_columns // HD):
        columns = slice(head * HD, (head + 1) * HD)
        scores = dot(query_ref[:, columns], keys[...], ((1,), (1,))) * HD ** (-0.5)
        scores = jnp.where(visible, scores, NEGATIVE)
        weights = jnp.exp(scores - jnp.max(scores, axis=1, keepdims=True))
        total = jnp.sum(weights, axis=1, keepdims=True)
        gathered = dot(weights.astype(jnp.bfloat16), values[...])
        gate = sigmoid(gate_ref[:, columns].astype(jnp.float32))
        heads_ref[:, columns] = (gathered / total * gate).astype(jnp.bfloat16)
    mid = send_ref.shape[1]
    width = residual_ref.shape[1]
    sums[...] = dot(heads_ref[...], weight_ref[:, pl.ds(pl.multiple_of((1 - sub_rank) * mid, mid), mid)])

    @pl.when(sub_rank != head_rank)
    def _():
        sums[:, pl.ds(pl.multiple_of(sub_rank * width, width), width)] += residual_ref[...].astype(jnp.float32)

    send_ref[...] = sums[...].astype(jnp.bfloat16)


def keep_kernel(heads_ref, weight_ref, residual_ref, keep_ref):
    head_rank, sub_rank = lax.axis_index("head"), lax.axis_index("sub")
    mid = keep_ref.shape[1]
    width = residual_ref.shape[1]
    keep_ref[...] = dot(heads_ref[...], weight_ref[:, pl.ds(pl.multiple_of(sub_rank * mid, mid), mid)])

    @pl.when(sub_rank == head_rank)
    def _():
        keep_ref[:, pl.ds(pl.multiple_of(sub_rank * width, width), width)] += residual_ref[...].astype(jnp.float32)


def chip_sum_kernel(keep_ref, came_ref, sum_ref, send_ref):
    total = keep_ref[...] + came_ref[...].astype(jnp.float32)
    sum_ref[...] = total
    send_ref[...] = total.astype(jnp.bfloat16)


def hidden_kernel(keep_ref, came_ref, hidden_ref):
    hidden_ref[...] = (keep_ref[...] + came_ref[...].astype(jnp.float32)).astype(jnp.bfloat16)


def half_of(ref, own):
    sub_rank = lax.axis_index("sub")
    mid = ref.shape[-1] // 2
    return pl.ds(pl.multiple_of((sub_rank if own else 1 - sub_rank) * mid, mid), mid)


def own_half_kernel(own_ref, gain_ref, weight_ref, beta_ref, mixed_ref, logit_ref, square_ref):
    mid = own_ref.shape[1]
    own = own_ref[...].astype(jnp.float32)
    columns = half_of(gain_ref, True)
    scaled = (own * gain_ref[:, columns]).astype(jnp.bfloat16)
    square_ref[...] = jnp.broadcast_to(jnp.sum(own * own, axis=1, keepdims=True), square_ref.shape)
    logit_ref[...] = dot(beta_ref[:, columns], scaled, ((1,), (1,)))
    rows = pl.ds(pl.multiple_of(lax.axis_index("sub") * mid, mid), mid)
    mixed_ref[...] = dot(scaled, weight_ref[rows, :])


def twin_half_kernel(
    twin_ref, gain_ref, beta_ref, decay_ref, logit_ref, square_ref, weight_ref, mixed_ref,
    scaled_ref, scale_ref, extra_ref, payload_ref, small,
):
    twin = twin_ref[...].astype(jnp.float32)
    columns = half_of(gain_ref, False)
    scaled_ref[...] = (twin * gain_ref[:, columns]).astype(jnp.bfloat16)
    squares = square_ref[...] + jnp.sum(twin * twin, axis=1, keepdims=True)
    scale = lax.rsqrt(squares / gain_ref.shape[1] + EPSILON)
    scale_ref[...] = scale
    values = decay_ref.shape[0]
    logits = logit_ref[...] + dot(beta_ref[:, columns], scaled_ref[...], ((1,), (1,)))
    extra_ref[0:values] = decay_ref[...]
    extra_ref[values : 2 * values] = sigmoid(logits * jnp.transpose(scale)[0:1])
    payload_kernel(2, scaled_ref, scale_ref, weight_ref, mixed_ref, extra_ref, payload_ref, small)


def residual_kernel(own_ref, twin_ref, residual_ref):
    head_rank, sub_rank = lax.axis_index("head"), lax.axis_index("sub")
    width = residual_ref.shape[1]
    columns = pl.ds(pl.multiple_of(sub_rank * width, width), width)

    @pl.when(sub_rank == head_rank)
    def _():
        residual_ref[...] = own_ref[:, columns]

    @pl.when(sub_rank != head_rank)
    def _():
        residual_ref[...] = twin_ref[:, columns]


def payload_kernel(mask, scaled_ref, scale_ref, weight_ref, mixed_ref, extra_ref, payload_ref, small):
    rows, mid = scaled_ref.shape
    group = 2 * DK + 2 * DV
    target = jnp.bitwise_xor(lax.axis_index("ctx"), mask)
    columns = pl.ds(pl.multiple_of(target * group, group), group)
    weight_rows = pl.ds(pl.multiple_of((1 - lax.axis_index("sub")) * mid, mid), mid)
    mixed = mixed_ref[:, columns] + dot(scaled_ref[...], weight_ref[weight_rows, columns])
    mixed = silu(mixed * scale_ref[:, 0:1])
    query, key = mixed[:, :DK], mixed[:, DK : 2 * DK]
    payload_ref[0:rows] = (unit_rows(query) * DK ** (-0.5)).astype(jnp.bfloat16)
    payload_ref[rows : 2 * rows] = unit_rows(key).astype(jnp.bfloat16)
    payload_ref[2 * rows : 3 * rows] = mixed[:, 2 * DK : 2 * DK + DV].astype(jnp.bfloat16)
    payload_ref[3 * rows : 4 * rows] = mixed[:, 2 * DK + DV :].astype(jnp.bfloat16)
    values = extra_ref.shape[0] // 2
    small[...] = jnp.zeros_like(small)
    for place, base in ((0, 0), (4, values)):
        full = extra_ref[pl.ds(base + 2 * target, 2), :]
        high = full.astype(jnp.bfloat16).astype(jnp.float32)
        small[place : place + 2] = high
        small[place + 2 : place + 4] = full - high
    payload_ref[4 * rows : 4 * rows + 16] = small[...].astype(jnp.bfloat16)


def unit_lower_inverses(stricts, row, column):
    inner = (row >> 3) == (column >> 3)
    identity = jnp.where(row == column, 1.0, 0.0)
    smalls = [jnp.where(inner, strict, 0.0) for strict in stricts]
    rests = [jnp.where(inner, 0.0, strict) for strict in stricts]
    seconds = [dot3(small, small) for small in smalls]
    inverses = [identity - small for small in smalls]
    fourths = [dot3(second, second) for second in seconds]
    inverses = [inverse + dot3(inverse, second) for inverse, second in zip(inverses, seconds)]
    inverses = [inverse + dot3(inverse, fourth) for inverse, fourth in zip(inverses, fourths)]
    steps = [dot3(inverse, rest) for inverse, rest in zip(inverses, rests)]
    results = [inverse - dot3(step, inverse) for inverse, step in zip(inverses, steps)]
    doubles = [dot3(step, step) for step in steps]
    quads = [dot3(double, double) for double in doubles]
    results = [result + dot3(double, result) for result, double in zip(results, doubles)]
    return [result + dot3(quad, result) for result, quad in zip(results, quads)]


def block_kernel(mask, payload_ref, *refs):
    offset_ref, linear_ref, local_ref, growth_ref = refs[-4:]
    source = jnp.bitwise_xor(lax.axis_index("ctx"), mask)
    rows = (payload_ref.shape[0] - 16) // 4
    half = rows // 2
    shift = half.bit_length() - 1
    row = lax.broadcasted_iota(jnp.int32, (rows, 1), 0)
    column = lax.broadcasted_iota(jnp.int32, (1, rows), 1)
    together = (row >> shift) == (column >> shift)
    inclusive = together & (row >= column)
    strictly = together & (row > column)
    early = column < half
    below = jnp.where(inclusive, 1.0, 0.0).astype(jnp.bfloat16)
    diagonal = jnp.where(row == column, 1.0, 0.0).astype(jnp.bfloat16)
    heads = range(2)
    query, key = payload_ref[0:rows], payload_ref[rows : 2 * rows]
    extra = payload_ref[4 * rows : 4 * rows + 16]
    sums_row = dot(extra, below, ((1,), (1,)))
    turned = dot(jnp.concatenate([below, diagonal], axis=0), extra, ((1,), (1,)))
    key_gram = dot(key, key, ((1,), (1,)))
    total_rows = [sums_row[h : h + 1] + sums_row[h + 2 : h + 3] for h in heads]
    totals = [turned[:rows, h : h + 1] + turned[:rows, h + 2 : h + 3] for h in heads]
    betas = [turned[rows:, h + 4 : h + 5] + turned[rows:, h + 6 : h + 7] for h in heads]
    decays = [jnp.exp(jnp.where(inclusive, totals[h] - total_rows[h], NEGATIVE)) for h in heads]
    stricts = [jnp.where(strictly, betas[h] * key_gram * decays[h], 0.0) for h in heads]
    query_gram = dot(query, key, ((1,), (1,)))
    key_wide = key.astype(jnp.float32)
    key_turned = jnp.transpose(key_wide)
    growths = [jnp.exp(total) for total in totals]
    values = [payload_ref[(2 + h) * rows : (3 + h) * rows].astype(jnp.float32) for h in heads]
    rights = [
        jnp.concatenate([betas[h] * values[h], (betas[h] * growths[h]) * key_wide], axis=1).astype(jnp.bfloat16)
        for h in heads
    ]
    grams = [(query_gram * decays[h]).astype(jnp.bfloat16) for h in heads]
    ends = [jnp.where(early, total[:, half - 1 : half], total[:, rows - 1 : rows]) for total in total_rows]
    carried = [key_turned * jnp.exp(ends[h] - total_rows[h]) for h in heads]
    lefts = [
        jnp.concatenate([jnp.where(early, keys, 0.0), jnp.where(early, 0.0, keys)], axis=0).astype(jnp.bfloat16)
        for keys in carried
    ]
    inverses = [halves(inverse) for inverse in unit_lower_inverses(stricts, row, column)]
    solved = [
        (dot(high, right) + dot(low, right)).astype(jnp.bfloat16) for (high, low), right in zip(inverses, rights)
    ]
    moved = [dot(jnp.concatenate([lefts[h], grams[h]], axis=0), solved[h]) for h in heads]
    for h in heads:
        attended = moved[h][2 * DK :]
        local_ref[source, h] = attended[:, :DV]
        reads = (growths[h] * query.astype(jnp.float32) - attended[:, DV:]).astype(jnp.bfloat16)
        growth = jnp.exp(ends[h])
        for block in range(2):
            state = moved[h][block * DK : (block + 1) * DK]
            offset_ref[source, h, block] = state[:, :DV]
            linear_ref[source, h, block, 0:DK] = state[:, DV:].astype(jnp.bfloat16)
            linear_ref[source, h, block, DK : DK + half] = reads[block * half : (block + 1) * half]
            last = (block + 1) * half - 1
            growth_ref[source, h, block] = jnp.broadcast_to(growth[:, last : last + 1], growth_ref.shape[3:])


def scan_kernel(offset_ref, linear_ref, local_ref, growth_ref, gain_ref, own_ref, back1, back2, back3, outs):
    count = offset_ref.shape[0]
    half = local_ref.shape[2] // 2
    rank = lax.axis_index("ctx")
    states = [None, None]
    for number in range(2 * count):
        source, block = (number, 0) if number < count else (2 * count - 1 - number, 1)
        block_rows = slice(block * half, (block + 1) * half)
        for head in range(2):
            out = local_ref[source, head, block_rows]
            state = offset_ref[source, head, block]
            if states[head] is not None:
                moved = dot(linear_ref[source, head, block], states[head].astype(jnp.bfloat16))
                out = out + moved[DK:]
                state = state - moved[:DK] + growth_ref[source, head, block, 0:1] * states[head]
            states[head] = state
            scale = lax.rsqrt(jnp.mean(out * out, axis=1, keepdims=True) + EPSILON)
            outs[source, block_rows, head * DV : (head + 1) * DV] = (out * scale * gain_ref[...]).astype(jnp.bfloat16)
    own_ref[...] = outs[rank]
    for mask, back in enumerate((back1, back2, back3), 1):
        back[...] = outs[jnp.bitwise_xor(rank, mask)]


def place_kernel(own_ref, back1, back2, back3, out_ref, sems):
    width = own_ref.shape[1]
    rank = lax.axis_index("ctx")
    copies = []
    for mask, back in enumerate((own_ref, back1, back2, back3)):
        columns = pl.ds(pl.multiple_of(jnp.bitwise_xor(rank, mask) * width, width), width)
        copies.append(pltpu.make_async_copy(back, out_ref.at[:, columns], sems.at[mask]))
        copies[-1].start()
    for copy in copies:
        copy.wait()


def owner_local(
    att_query,
    att_gate,
    att_kv,
    residual,
    out_weight,
    norm_gain,
    in_weight,
    beta_weight,
    log_decay,
    delta_gain,
):
    bf16, f32 = jnp.bfloat16, jnp.float32
    rows, head_columns = att_query.shape
    model = out_weight.shape[1]
    half_model = model // 2
    value_here = log_decay.shape[1]
    masks = (2, 3, 1)
    piece = pl.pallas_call(
        piece_kernel,
        out_shape=pltpu.VMEM((rows, HD), bf16),
        in_specs=[IN_HBM],
        out_specs=IN_VMEM,
        scratch_shapes=[pltpu.SemaphoreType.DMA],
        compiler_params=pltpu.CompilerParams(vmem_limit_bytes=4 * MIB),
    )(in_hbm(att_kv))
    mine = {mask: swapped(piece, "ctx", mask) for mask in masks[::-1]}
    piece, *late = lax.optimization_barrier((piece, att_query, att_gate, att_kv, out_weight, residual))
    late = fetched(*late)
    mine[2], (att_query, att_gate, att_kv, out_weight, residual) = lax.optimization_barrier((mine[2], late))
    twin = {mask: swapped(mine[mask], "sub") for mask in masks}
    heads, send = vmem_call(
        attention_kernel,
        [((rows, head_columns), bf16), ((rows, half_model), bf16)],
        [att_query, att_gate, att_kv, mine[1], mine[2], mine[3], twin[1], twin[2], twin[3], out_weight, residual],
        [
            pltpu.VMEM((4 * rows, HD), bf16),
            pltpu.VMEM((4 * rows, HD), bf16),
            pltpu.VMEM((rows, half_model), f32),
        ],
    )
    came = swapped(send, "sub")
    keep = vmem_call(keep_kernel, [((rows, half_model), f32)], [heads, out_weight, residual])[0]
    came, keep = lax.optimization_barrier((came, keep))
    chip_sum, send = vmem_call(
        chip_sum_kernel, [((rows, half_model), f32), ((rows, half_model), bf16)], [keep, came]
    )
    came = swapped(send, "head")
    send, *late = lax.optimization_barrier((send, in_weight, norm_gain[None, :], beta_weight.T, log_decay.T))
    late = fetched(*late)
    came, (in_weight, norm_gain, beta_weight, log_decay) = lax.optimization_barrier((came, late))
    hidden = vmem_call(hidden_kernel, [((rows, half_model), bf16)], [chip_sum, came])[0]
    twin_hidden = swapped(hidden, "sub")
    sums = vmem_call(
        own_half_kernel,
        [((rows, in_weight.shape[1]), f32), ((value_here, rows), f32), ((rows, LANES), f32)],
        [hidden, norm_gain, in_weight, beta_weight],
    )
    twin_hidden, (mixed, logits, squares) = lax.optimization_barrier((twin_hidden, sums))
    payload_shape = ((4 * rows + 16, LANES), bf16)
    payloads = {}
    scaled, scale, extra, payloads[2] = vmem_call(
        twin_half_kernel,
        [((rows, half_model), bf16), ((rows, LANES), f32), ((2 * value_here, rows), f32), payload_shape],
        [twin_hidden, norm_gain, beta_weight, log_decay, logits, squares, in_weight, mixed],
        [pltpu.VMEM((16, LANES), f32)],
    )
    for mask in (3, 1, 0):
        payloads[mask] = vmem_call(
            functools.partial(payload_kernel, mask),
            [payload_shape],
            [scaled, scale, in_weight, mixed, extra],
            [pltpu.VMEM((16, LANES), f32)],
        )[0]
    new_residual = vmem_call(residual_kernel, [(residual.shape, bf16)], [hidden, twin_hidden], last=True)[0]
    came = {mask: swapped(payloads[mask], "ctx", mask) for mask in masks}
    came[0] = payloads[0]
    half = rows // 2
    terms_shapes = [
        ((4, 2, 2, DK, DV), f32),
        ((4, 2, 2, DK + half, DK), bf16),
        ((4, 2, rows, DV), f32),
        ((4, 2, 2, 8, LANES), f32),
    ]
    terms = []
    for mask in (0, 2, 1, 3):
        terms = vmem_call(
            functools.partial(block_kernel, mask),
            terms_shapes,
            [came[mask], *terms],
            aliases={1 + i: i for i in range(4)} if terms else None,
        )
    own, *backs = vmem_call(
        scan_kernel,
        [((rows, 2 * DV), bf16)] * 4,
        [*terms, delta_gain[None, :]],
        [pltpu.VMEM((4, rows, 2 * DV), bf16)],
    )
    backs = {mask: swapped(backs[mask - 1], "ctx", mask) for mask in masks}
    delta_out = pl.pallas_call(
        place_kernel,
        out_shape=jax.ShapeDtypeStruct((rows, value_here * DV), bf16),
        in_specs=[IN_VMEM] * 4,
        out_specs=IN_HBM,
        scratch_shapes=[pltpu.SemaphoreType.DMA((4,))],
        compiler_params=pltpu.CompilerParams(vmem_limit_bytes=4 * MIB),
    )(*[in_vmem(back) for back in (own, backs[1], backs[2], backs[3])])
    return (new_residual, delta_out)


def solution(mesh):
    local = owner_local if owners_fit(mesh) else hop_local
    return jax.shard_map(
        local,
        mesh=mesh,
        in_specs=(
            P(("groups", "ctx"), ("head", "sub")),
            P(("groups", "ctx"), ("head", "sub")),
            P(("groups", "ctx"), None),
            P(("groups", "ctx"), ("head", "sub")),
            P(("head", "sub"), None),
            P(),
            P(None, ("head", "sub")),
            P(None, ("head", "sub")),
            P(("groups", "ctx"), ("head", "sub")),
            P(),
        ),
        out_specs=(P(("groups", "ctx"), ("head", "sub")), P(("groups", "ctx"), ("head", "sub"))),
        check_vma=False,
    )
```

```python
import functools

import jax
import jax.numpy as jnp
from jax import lax
from jax.experimental import pallas as pl
from jax.experimental.pallas import tpu as pltpu
from jax.sharding import PartitionSpec as P

HEADS = 16
KV_HEADS = 2
HD = 256
DK = 128
DV = 128


TOP_PRECISION = lax.Precision.HIGHEST
EPSILON = 1e-06
NEGATIVE = -1e30


def passed_along(value, axis, steps):
    count = lax.axis_size(axis)
    initial, last = (max(0, -steps), min(count, count - steps))
    return lax.ppermute(value, axis, [(source, source + steps) for source in range(initial, last)])


def stored_positions(first_row, row_total, half_rows, ctx_count):
    row_index = first_row + jnp.arange(row_total, dtype=jnp.int32)
    device_of = row_index // (2 * half_rows)
    within_dev = row_index % (2 * half_rows)
    block_number = jnp.where(within_dev < half_rows, device_of, 2 * ctx_count - 1 - device_of)
    return block_number * half_rows + within_dev % half_rows


def unit_rows(matrix):
    return matrix * lax.rsqrt(jnp.sum(matrix * matrix, axis=-1, keepdims=True) + EPSILON)


def to_blocks(array, half_rows):
    heads_count = array.shape[1]
    width = array.shape[2]
    shaped = array.reshape(2, half_rows, heads_count, width).transpose(2, 0, 1, 3)
    return shaped.reshape(heads_count * 2, half_rows, width)


def block_terms(query_rows, key_rows, value_rows, beta_rows, decay_rows):
    length = query_rows.shape[0]
    cumulative = jnp.cumsum(decay_rows)
    position = jnp.arange(length)
    on_or_below = position[:, None] >= position[None, :]
    strictly_below = position[:, None] > position[None, :]
    decay_gap = cumulative[:, None] - cumulative[None, :]
    decay_grid = jnp.where(on_or_below, jnp.exp(jnp.where(on_or_below, decay_gap, 0.0)), 0.0)
    key_gram = jnp.dot(key_rows, key_rows.T, precision=TOP_PRECISION)
    system = jnp.eye(length, dtype=jnp.float32) + jnp.where(
        strictly_below, beta_rows[:, None] * key_gram * decay_grid, 0.0
    )
    growth = jnp.exp(cumulative)
    right_side = beta_rows[:, None] * jnp.concatenate(
        [value_rows, growth[:, None] * key_rows], axis=1
    )
    solved = jax.scipy.linalg.solve_triangular(system, right_side, lower=True, unit_diagonal=True)
    update_rows = solved[:, : value_rows.shape[1]]
    weight_rows = solved[:, value_rows.shape[1] :]
    attend_grid = jnp.where(
        on_or_below, jnp.dot(query_rows, key_rows.T, precision=TOP_PRECISION) * decay_grid, 0.0
    )
    local_out = jnp.dot(attend_grid, update_rows, precision=TOP_PRECISION)
    read_rows = growth[:, None] * query_rows - jnp.dot(
        attend_grid, weight_rows, precision=TOP_PRECISION
    )
    carried_keys = jnp.exp(cumulative[-1] - cumulative)[:, None] * key_rows
    identity_map = jnp.eye(key_rows.shape[1], dtype=jnp.float32)
    transition = jnp.exp(cumulative[-1]) * identity_map - jnp.dot(
        carried_keys.T, weight_rows, precision=TOP_PRECISION
    )
    offset_state = jnp.dot(carried_keys.T, update_rows, precision=TOP_PRECISION)
    return (local_out, read_rows, transition, offset_state)


def apply_map(matrix_maps, offsets, states):
    return jnp.einsum("hij,hjk->hik", matrix_maps, states, precision=TOP_PRECISION) + offsets


def attend_rows(running, query_block, key_block, value_block, visible, score_scale):
    run_max, run_sum, run_acc = running
    scores = (
        jnp.einsum("rhd,kd->rhk", query_block, key_block, preferred_element_type=jnp.float32)
        * score_scale
    )
    if visible is not None:
        scores = jnp.where(visible[:, None, :], scores, NEGATIVE)
    new_max = jnp.maximum(run_max, jnp.max(scores, axis=2))
    weights = jnp.exp(scores - new_max[:, :, None])
    if visible is not None:
        weights = jnp.where(visible[:, None, :], weights, 0.0)
    rescale = jnp.exp(run_max - new_max)
    run_sum = run_sum * rescale + jnp.sum(weights, axis=2)
    added = jnp.einsum(
        "rhk,kd->rhd", weights.astype(jnp.bfloat16), value_block, preferred_element_type=jnp.float32
    )
    run_acc = run_acc * rescale[:, :, None] + added
    return (new_max, run_sum, run_acc)


def hop_local(
    att_query,
    att_gate,
    att_kv,
    residual,
    out_weight,
    norm_gain,
    in_weight,
    beta_weight,
    log_decay,
    delta_gain,
):
    ctx_count = lax.axis_size("ctx")
    ctx_rank = lax.axis_index("ctx")
    shard_rank = lax.axis_index(("head", "sub"))
    rows_here = att_query.shape[0]
    half_rows = rows_here // 2
    heads_here = att_query.shape[1] // HD
    kv_number = shard_rank * heads_here // (HEADS // KV_HEADS)
    key_local = lax.dynamic_slice_in_dim(att_kv, kv_number * 2 * HD, HD, 1)
    value_local = lax.dynamic_slice_in_dim(att_kv, kv_number * 2 * HD + HD, HD, 1)
    query_heads = att_query.reshape(rows_here, heads_here, HD)
    late_queries = query_heads[half_rows:]
    query_places = stored_positions(ctx_rank * rows_here, rows_here, half_rows, ctx_count)
    same_visible = query_places[:, None] >= query_places[None, :]
    score_scale = HD ** (-0.5)

    def earlier_shard(running, key_shard, value_shard):
        return attend_rows(
            running, query_heads, key_shard[:half_rows], value_shard[:half_rows], None, score_scale
        )

    def same_shard(running, key_shard, value_shard):
        return attend_rows(running, query_heads, key_shard, value_shard, same_visible, score_scale)

    def later_shard(running, key_shard, value_shard):
        late_part = tuple((member[half_rows:] for member in running))
        renewed = attend_rows(late_part, late_queries, key_shard, value_shard, None, score_scale)
        return tuple(
            (
                jnp.concatenate([member[:half_rows], latest], axis=0)
                for member, latest in zip(running, renewed)
            )
        )

    start_running = (
        jnp.full((rows_here, heads_here), NEGATIVE, jnp.float32),
        jnp.zeros((rows_here, heads_here), jnp.float32),
        jnp.zeros((rows_here, heads_here, HD), jnp.float32),
    )
    key_block = lax.all_gather(key_local, "ctx", axis=0, tiled=True)
    value_block = lax.all_gather(value_local, "ctx", axis=0, tiled=True)
    piece_rows = key_block.shape[0]

    def one_shard(number, current):
        offset = number * rows_here
        key_shard = lax.dynamic_slice_in_dim(key_block, offset, rows_here, 0)
        value_shard = lax.dynamic_slice_in_dim(value_block, offset, rows_here, 0)
        shard_number = offset // rows_here
        branch = jnp.clip(shard_number - ctx_rank, -1, 1) + 1
        return lax.switch(
            branch, [earlier_shard, same_shard, later_shard], current, key_shard, value_shard
        )

    run_max, run_sum, run_acc = lax.fori_loop(0, piece_rows // rows_here, one_shard, start_running)
    gate_heads = jax.nn.sigmoid(att_gate.reshape(rows_here, heads_here, HD).astype(jnp.float32))
    att_heads = (
        (run_acc / run_sum[:, :, None] * gate_heads)
        .astype(jnp.bfloat16)
        .reshape(rows_here, heads_here * HD)
    )
    partial_term = jnp.dot(att_heads, out_weight, preferred_element_type=jnp.float32)
    col_width = residual.shape[1]
    col_start = shard_rank * col_width
    placed = lax.dynamic_slice_in_dim(partial_term, col_start, col_width, 1) + residual.astype(
        jnp.float32
    )
    partial_term = lax.dynamic_update_slice_in_dim(partial_term, placed, col_start, 1)
    hidden = lax.psum(partial_term.astype(jnp.bfloat16), ("head", "sub")).astype(jnp.float32)
    mean_square = jnp.mean(hidden * hidden, axis=1, keepdims=True)
    normed = (hidden * lax.rsqrt(mean_square + EPSILON) * norm_gain).astype(jnp.bfloat16)
    new_residual = lax.dynamic_slice_in_dim(hidden, col_start, col_width, 1).astype(jnp.bfloat16)
    mixed_cols = jnp.dot(normed, in_weight, preferred_element_type=jnp.float32)
    beta_logits = jnp.dot(normed, beta_weight, preferred_element_type=jnp.float32)
    key_here = in_weight.shape[1] // (2 * DK + 2 * DV)
    value_here = 2 * key_here
    grouped = mixed_cols.reshape(rows_here, key_here, 2 * DK + 2 * DV)
    query_unit = jnp.repeat(unit_rows(jax.nn.silu(grouped[:, :, :DK])) * DK ** (-0.5), 2, axis=1)
    key_unit = jnp.repeat(unit_rows(jax.nn.silu(grouped[:, :, DK : 2 * DK])), 2, axis=1)
    value_all = jax.nn.silu(grouped[:, :, 2 * DK :]).reshape(rows_here, value_here, DV)
    beta_all = jax.nn.sigmoid(beta_logits)
    local_out, read_rows, transition, offset_state = jax.vmap(block_terms)(
        to_blocks(query_unit, half_rows),
        to_blocks(key_unit, half_rows),
        to_blocks(value_all, half_rows),
        to_blocks(beta_all[:, :, None], half_rows)[:, :, 0],
        to_blocks(log_decay[:, :, None], half_rows)[:, :, 0],
    )
    transition = transition.reshape(value_here, 2, DK, DK)
    offset_state = offset_state.reshape(value_here, 2, DK, DV)
    early_map, late_map = (transition[:, 0], transition[:, 1])
    early_offset, late_offset = (offset_state[:, 0], offset_state[:, 1])
    last_rank = ctx_count - 1
    zero_states = jnp.zeros_like(early_offset)

    def early_turn(number, incoming):
        return passed_along(
            apply_map(early_map, early_offset, incoming).astype(jnp.bfloat16), "ctx", 1
        ).astype(jnp.float32)

    early_in = lax.fori_loop(0, ctx_count - 1, early_turn, zero_states)
    early_end = apply_map(early_map, early_offset, early_in)
    late_start = jnp.where(ctx_rank == last_rank, early_end, zero_states)

    def late_turn(number, incoming):
        moved = passed_along(
            apply_map(late_map, late_offset, incoming).astype(jnp.bfloat16), "ctx", -1
        ).astype(jnp.float32)
        return jnp.where(ctx_rank == last_rank, early_end, moved)

    late_in = lax.fori_loop(0, ctx_count - 1, late_turn, late_start)
    states_in = jnp.stack([early_in, late_in], axis=1)
    block_out = local_out.reshape(value_here, 2, half_rows, DV) + jnp.einsum(
        "hbck,hbkv->hbcv",
        read_rows.reshape(value_here, 2, half_rows, DK),
        states_in,
        precision=TOP_PRECISION,
    )
    token_out = block_out.transpose(1, 2, 0, 3).reshape(rows_here, value_here, DV)
    out_square = jnp.mean(token_out * token_out, axis=2, keepdims=True)
    delta_out = (token_out * lax.rsqrt(out_square + EPSILON) * delta_gain).astype(jnp.bfloat16)
    return (new_residual, delta_out.reshape(rows_here, value_here * DV))


KEY_HEADS = 16
IN_VMEM = pl.BlockSpec(memory_space=pltpu.VMEM)
IN_HBM = pl.BlockSpec(memory_space=pl.ANY)
MIB = 2**20
LANES = 128


def owners_fit(mesh):
    shards = mesh.shape["head"] * mesh.shape["sub"]
    key_here = KEY_HEADS // shards
    return mesh.shape["head"] == 2 and mesh.shape["sub"] == 2 and key_here == mesh.shape["ctx"]


def in_vmem(array):
    return pltpu.with_memory_space_constraint(array, pltpu.VMEM)


def in_hbm(array):
    return pltpu.with_memory_space_constraint(array, pltpu.HBM)


def vmem_call(kernel, outs, operands, scratch=(), limit=16, aliases=None, last=False, cost=None):
    make = jax.ShapeDtypeStruct if last else pltpu.VMEM
    return pl.pallas_call(
        kernel,
        out_shape=[make(shape, dtype) for shape, dtype in outs],
        in_specs=[IN_VMEM] * len(operands),
        out_specs=[IN_VMEM] * len(outs),
        scratch_shapes=list(scratch),
        input_output_aliases=aliases or {},
        cost_estimate=cost,
        compiler_params=pltpu.CompilerParams(vmem_limit_bytes=limit * MIB),
    )(*[in_vmem(operand) for operand in operands])


def swapped(value, axis, mask=1):
    return lax.ppermute(value, axis, [(i, i ^ mask) for i in range(lax.axis_size(axis))])


def dot(left, right, dims=((1,), (0,))):
    return lax.dot_general(left, right, (dims, ((), ())), preferred_element_type=jnp.float32)


def halves(value):
    high = value.astype(jnp.bfloat16)
    return high, (value - high.astype(jnp.float32)).astype(jnp.bfloat16)


def sigmoid(value):
    return 1.0 / (1.0 + jnp.exp(-value))


def silu(value):
    return value / (1.0 + jnp.exp(-value))


def piece_kernel(kv_ref, piece_ref, sem):
    start = (lax.axis_index("head") * 2 + lax.axis_index("sub")) * HD
    copy = pltpu.make_async_copy(kv_ref.at[:, pl.ds(pl.multiple_of(start, HD), HD)], piece_ref, sem)
    copy.start()
    copy.wait()


def fetch_kernel(*refs):
    count = len(refs) // 2
    copies = [
        pltpu.make_async_copy(refs[n], refs[count + n], refs[-1].at[n]) for n in range(count)
    ]
    for copy in copies:
        copy.start()
    for copy in copies:
        copy.wait()


def fetched(*arrays):
    moved = sum(array.size * array.dtype.itemsize for array in arrays)
    return pl.pallas_call(
        fetch_kernel,
        out_shape=[pltpu.VMEM(array.shape, array.dtype) for array in arrays],
        in_specs=[IN_HBM] * len(arrays),
        out_specs=[IN_VMEM] * len(arrays),
        scratch_shapes=[pltpu.SemaphoreType.DMA((len(arrays),))],
        compiler_params=pltpu.CompilerParams(vmem_limit_bytes=4 * MIB),
        cost_estimate=pl.CostEstimate(flops=0, bytes_accessed=moved, transcendentals=0),
    )(*[in_hbm(array) for array in arrays])


def attend(query_ref, gate_ref, keys, values, rows, key_total, visible):
    count = query_ref.shape[1] // HD
    columns = [slice(head * HD, (head + 1) * HD) for head in range(count)]
    size = rows.stop - rows.start
    queries = jnp.concatenate([query_ref[rows, part] for part in columns], axis=0)
    gates = [sigmoid(gate_ref[rows, part].astype(jnp.float32)) for part in columns]
    scores = dot(queries, keys[0:key_total], ((1,), (1,))) * HD ** (-0.5)
    scores = jnp.where(jnp.concatenate([visible] * count, axis=0), scores, NEGATIVE)
    weights = jnp.exp(scores - jnp.max(scores, axis=1, keepdims=True))
    total = jnp.sum(weights, axis=1, keepdims=True)
    gathered = dot(weights.astype(jnp.bfloat16), values[0:key_total]) / total
    gated = [gathered[head * size : (head + 1) * size] * gates[head] for head in range(count)]
    return jnp.concatenate(gated, axis=1).astype(jnp.bfloat16)


def attention_kernel(
    query_ref, gate_ref, kv_ref, mine1, mine2, mine3, twin1, twin2, twin3, weight_ref, residual_ref,
    heads_ref, send_ref, keys, values, sums,
):
    half = query_ref.shape[0] // 2
    ctx_rank, head_rank, sub_rank = (lax.axis_index(name) for name in ("ctx", "head", "sub"))
    count = 4
    own_start = pl.multiple_of(head_rank * 2 * HD, 2 * HD)

    def put(target, mask, part):
        target[mask * half : (mask + 1) * half] = part[0:half]
        target[(count + mask) * half : (count + mask + 1) * half] = part[half : 2 * half]

    put(keys, 0, kv_ref[:, pl.ds(own_start, HD)])
    put(values, 0, kv_ref[:, pl.ds(own_start + HD, HD)])

    @pl.when(sub_rank == 0)
    def _():
        for mask, (mine, twin) in enumerate(((mine1, twin1), (mine2, twin2), (mine3, twin3)), 1):
            put(keys, mask, mine[...])
            put(values, mask, twin[...])

    @pl.when(sub_rank != 0)
    def _():
        for mask, (mine, twin) in enumerate(((mine1, twin1), (mine2, twin2), (mine3, twin3)), 1):
            put(keys, mask, twin[...])
            put(values, mask, mine[...])

    shift = half.bit_length() - 1
    row = lax.broadcasted_iota(jnp.int32, (half, 1), 0)
    column = lax.broadcasted_iota(jnp.int32, (1, 2 * count * half), 1)
    device = jnp.bitwise_xor(ctx_rank, (column >> shift) & (count - 1))
    block = jnp.where(column < count * half, device, 2 * count - 1 - device)
    key_place = block * half + (column & (half - 1))
    for part, block_here in enumerate((ctx_rank, 2 * count - 1 - ctx_rank)):
        rows = slice(part * half, (part + 1) * half)
        key_total = (part + 1) * count * half
        visible = row + block_here * half >= key_place[:, :key_total]
        heads_ref[rows] = attend(query_ref, gate_ref, keys, values, rows, key_total, visible)
    mid = send_ref.shape[1]
    width = residual_ref.shape[1]
    sums[...] = dot(heads_ref[...], weight_ref[:, pl.ds(pl.multiple_of((1 - sub_rank) * mid, mid), mid)])

    @pl.when(sub_rank != head_rank)
    def _():
        sums[:, pl.ds(pl.multiple_of(sub_rank * width, width), width)] += residual_ref[...].astype(jnp.float32)

    send_ref[...] = sums[...].astype(jnp.bfloat16)


def keep_kernel(heads_ref, weight_ref, residual_ref, keep_ref):
    head_rank, sub_rank = lax.axis_index("head"), lax.axis_index("sub")
    mid = keep_ref.shape[1]
    width = residual_ref.shape[1]
    keep_ref[...] = dot(heads_ref[...], weight_ref[:, pl.ds(pl.multiple_of(sub_rank * mid, mid), mid)])

    @pl.when(sub_rank == head_rank)
    def _():
        keep_ref[:, pl.ds(pl.multiple_of(sub_rank * width, width), width)] += residual_ref[...].astype(jnp.float32)


def chip_sum_kernel(keep_ref, came_ref, sum_ref, send_ref):
    total = keep_ref[...] + came_ref[...].astype(jnp.float32)
    sum_ref[...] = total
    send_ref[...] = total.astype(jnp.bfloat16)


def hidden_kernel(keep_ref, came_ref, hidden_ref):
    hidden_ref[...] = (keep_ref[...] + came_ref[...].astype(jnp.float32)).astype(jnp.bfloat16)


def half_of(ref, own):
    sub_rank = lax.axis_index("sub")
    mid = ref.shape[-1] // 2
    return pl.ds(pl.multiple_of((sub_rank if own else 1 - sub_rank) * mid, mid), mid)


def own_half_kernel(own_ref, gain_ref, weight_ref, beta_ref, mixed_ref, logit_ref, square_ref):
    mid = own_ref.shape[1]
    own = own_ref[...].astype(jnp.float32)
    columns = half_of(gain_ref, True)
    scaled = (own * gain_ref[:, columns]).astype(jnp.bfloat16)
    square_ref[...] = jnp.broadcast_to(jnp.sum(own * own, axis=1, keepdims=True), square_ref.shape)
    logit_ref[...] = dot(beta_ref[:, columns], scaled, ((1,), (1,)))
    rows = pl.ds(pl.multiple_of(lax.axis_index("sub") * mid, mid), mid)
    mixed_ref[...] = dot(scaled, weight_ref[rows, :])


def twin_half_kernel(
    twin_ref, gain_ref, beta_ref, decay_ref, logit_ref, square_ref, weight_ref, mixed_ref,
    scaled_ref, scale_ref, extra_ref, payload_ref, small,
):
    twin = twin_ref[...].astype(jnp.float32)
    columns = half_of(gain_ref, False)
    scaled_ref[...] = (twin * gain_ref[:, columns]).astype(jnp.bfloat16)
    squares = square_ref[...] + jnp.sum(twin * twin, axis=1, keepdims=True)
    scale = lax.rsqrt(squares / gain_ref.shape[1] + EPSILON)
    scale_ref[...] = scale
    values = decay_ref.shape[0]
    logits = logit_ref[...] + dot(beta_ref[:, columns], scaled_ref[...], ((1,), (1,)))
    extra_ref[0:values] = decay_ref[...]
    extra_ref[values : 2 * values] = sigmoid(logits * jnp.transpose(scale)[0:1])
    payload_kernel(2, scaled_ref, scale_ref, weight_ref, mixed_ref, extra_ref, payload_ref, small)


def residual_kernel(own_ref, twin_ref, residual_ref):
    head_rank, sub_rank = lax.axis_index("head"), lax.axis_index("sub")
    width = residual_ref.shape[1]
    columns = pl.ds(pl.multiple_of(sub_rank * width, width), width)

    @pl.when(sub_rank == head_rank)
    def _():
        residual_ref[...] = own_ref[:, columns]

    @pl.when(sub_rank != head_rank)
    def _():
        residual_ref[...] = twin_ref[:, columns]


def payload_kernel(mask, scaled_ref, scale_ref, weight_ref, mixed_ref, extra_ref, payload_ref, small):
    rows, mid = scaled_ref.shape
    group = 2 * DK + 2 * DV
    target = jnp.bitwise_xor(lax.axis_index("ctx"), mask)
    columns = pl.ds(pl.multiple_of(target * group, group), group)
    weight_rows = pl.ds(pl.multiple_of((1 - lax.axis_index("sub")) * mid, mid), mid)
    mixed = mixed_ref[:, columns] + dot(scaled_ref[...], weight_ref[weight_rows, columns])
    mixed = silu(mixed * scale_ref[:, 0:1])
    query, key = mixed[:, :DK], mixed[:, DK : 2 * DK]
    payload_ref[0:rows] = (unit_rows(query) * DK ** (-0.5)).astype(jnp.bfloat16)
    payload_ref[rows : 2 * rows] = unit_rows(key).astype(jnp.bfloat16)
    payload_ref[2 * rows : 3 * rows] = mixed[:, 2 * DK : 2 * DK + DV].astype(jnp.bfloat16)
    payload_ref[3 * rows : 4 * rows] = mixed[:, 2 * DK + DV :].astype(jnp.bfloat16)
    values = extra_ref.shape[0] // 2
    small[...] = jnp.zeros_like(small)
    for place, base in ((0, 0), (4, values)):
        full = extra_ref[pl.ds(base + 2 * target, 2), :]
        high = full.astype(jnp.bfloat16).astype(jnp.float32)
        small[place : place + 2] = high
        small[place + 2 : place + 4] = full - high
    payload_ref[4 * rows : 4 * rows + 16] = small[...].astype(jnp.bfloat16)


def joined(left, right):
    (left_high, left_low), (right_high, right_low) = left, right
    return dot(
        jnp.concatenate([left_high, left_high, left_low], axis=1),
        jnp.concatenate([right_high, right_low, right_high], axis=0),
    )


def unit_lower_inverses(stricts, row, column):
    inner = (row >> 3) == (column >> 3)
    identity = jnp.where(row == column, 1.0, 0.0)
    number = range(len(stricts))
    smalls = [jnp.where(inner, strict, 0.0) for strict in stricts]
    rests = [halves(jnp.where(inner, 0.0, strict)) for strict in stricts]
    small = [halves(part) for part in smalls]
    inverses = [identity - part for part in smalls]
    split = [halves(inverse) for inverse in inverses]
    seconds = [halves(joined(part, part)) for part in small]
    fourths = [halves(joined(second, second)) for second in seconds]
    inverses = [inverses[n] + joined(split[n], seconds[n]) for n in number]
    split = [halves(inverse) for inverse in inverses]
    inverses = [inverses[n] + joined(split[n], fourths[n]) for n in number]
    split = [halves(inverse) for inverse in inverses]
    steps = [halves(joined(split[n], rests[n])) for n in number]
    doubles = [halves(joined(step, step)) for step in steps]
    results = [inverses[n] - joined(steps[n], split[n]) for n in number]
    quads = [halves(joined(double, double)) for double in doubles]
    results = [results[n] + joined(doubles[n], halves(results[n])) for n in number]
    return [results[n] + joined(quads[n], halves(results[n])) for n in number]


def block_kernel(mask, payload_ref, *refs):
    offset_ref, linear_ref, local_ref, growth_ref = refs[-4:]
    source = jnp.bitwise_xor(lax.axis_index("ctx"), mask)
    rows = (payload_ref.shape[0] - 16) // 4
    half = rows // 2
    shift = half.bit_length() - 1
    row = lax.broadcasted_iota(jnp.int32, (rows, 1), 0)
    column = lax.broadcasted_iota(jnp.int32, (1, rows), 1)
    together = (row >> shift) == (column >> shift)
    inclusive = together & (row >= column)
    strictly = together & (row > column)
    early = column < half
    below = jnp.where(inclusive, 1.0, 0.0).astype(jnp.bfloat16)
    diagonal = jnp.where(row == column, 1.0, 0.0).astype(jnp.bfloat16)
    heads = range(2)
    query, key = payload_ref[0:rows], payload_ref[rows : 2 * rows]
    extra = payload_ref[4 * rows : 4 * rows + 16]
    sums_row = dot(extra, below, ((1,), (1,)))
    turned = dot(jnp.concatenate([below, diagonal], axis=0), extra, ((1,), (1,)))
    key_gram = dot(key, key, ((1,), (1,)))
    total_rows = [sums_row[h : h + 1] + sums_row[h + 2 : h + 3] for h in heads]
    totals = [turned[:rows, h : h + 1] + turned[:rows, h + 2 : h + 3] for h in heads]
    betas = [turned[rows:, h + 4 : h + 5] + turned[rows:, h + 6 : h + 7] for h in heads]
    decays = [jnp.exp(jnp.where(inclusive, totals[h] - total_rows[h], NEGATIVE)) for h in heads]
    stricts = [jnp.where(strictly, betas[h] * key_gram * decays[h], 0.0) for h in heads]
    query_gram = dot(query, key, ((1,), (1,)))
    key_wide = key.astype(jnp.float32)
    key_turned = jnp.transpose(key_wide)
    growths = [jnp.exp(total) for total in totals]
    values = [payload_ref[(2 + h) * rows : (3 + h) * rows].astype(jnp.float32) for h in heads]
    rights = [
        jnp.concatenate([betas[h] * values[h], (betas[h] * growths[h]) * key_wide], axis=1).astype(jnp.bfloat16)
        for h in heads
    ]
    grams = [(query_gram * decays[h]).astype(jnp.bfloat16) for h in heads]
    ends = [jnp.where(early, total[:, half - 1 : half], total[:, rows - 1 : rows]) for total in total_rows]
    carried = [key_turned * jnp.exp(ends[h] - total_rows[h]) for h in heads]
    lefts = [
        jnp.concatenate([jnp.where(early, keys, 0.0), jnp.where(early, 0.0, keys)], axis=0).astype(jnp.bfloat16)
        for keys in carried
    ]
    inverses = [halves(inverse) for inverse in unit_lower_inverses(stricts, row, column)]
    solved = [
        (dot(high, right) + dot(low, right)).astype(jnp.bfloat16) for (high, low), right in zip(inverses, rights)
    ]
    moved = [dot(jnp.concatenate([lefts[h], grams[h]], axis=0), solved[h]) for h in heads]
    for h in heads:
        attended = moved[h][2 * DK :]
        local_ref[source, h] = attended[:, :DV]
        reads = (growths[h] * query.astype(jnp.float32) - attended[:, DV:]).astype(jnp.bfloat16)
        growth = jnp.exp(ends[h])
        for block in range(2):
            state = moved[h][block * DK : (block + 1) * DK]
            offset_ref[source, h, block] = state[:, :DV]
            linear_ref[source, h, block, 0:DK] = state[:, DV:].astype(jnp.bfloat16)
            linear_ref[source, h, block, DK : DK + half] = reads[block * half : (block + 1) * half]
            last = (block + 1) * half - 1
            growth_ref[source, h, block] = jnp.broadcast_to(growth[:, last : last + 1], growth_ref.shape[3:])


def scan_kernel(offset_ref, linear_ref, local_ref, growth_ref, gain_ref, own_ref, back1, back2, back3, outs):
    count = offset_ref.shape[0]
    half = local_ref.shape[2] // 2
    rank = lax.axis_index("ctx")
    states = [None, None]
    for number in range(2 * count):
        source, block = (number, 0) if number < count else (2 * count - 1 - number, 1)
        block_rows = slice(block * half, (block + 1) * half)
        for head in range(2):
            out = local_ref[source, head, block_rows]
            state = offset_ref[source, head, block]
            if states[head] is not None:
                moved = dot(linear_ref[source, head, block], states[head].astype(jnp.bfloat16))
                out = out + moved[DK:]
                state = state - moved[:DK] + growth_ref[source, head, block, 0:1] * states[head]
            states[head] = state
            scale = lax.rsqrt(jnp.mean(out * out, axis=1, keepdims=True) + EPSILON)
            outs[source, block_rows, head * DV : (head + 1) * DV] = (out * scale * gain_ref[...]).astype(jnp.bfloat16)
    own_ref[...] = outs[rank]
    for mask, back in enumerate((back1, back2, back3), 1):
        back[...] = outs[jnp.bitwise_xor(rank, mask)]


def place_kernel(own_ref, back1, back2, back3, out_ref, sems):
    width = own_ref.shape[1]
    rank = lax.axis_index("ctx")
    copies = []
    for mask, back in enumerate((own_ref, back1, back2, back3)):
        columns = pl.ds(pl.multiple_of(jnp.bitwise_xor(rank, mask) * width, width), width)
        copies.append(pltpu.make_async_copy(back, out_ref.at[:, columns], sems.at[mask]))
        copies[-1].start()
    for copy in copies:
        copy.wait()


def owner_local(
    att_query,
    att_gate,
    att_kv,
    residual,
    out_weight,
    norm_gain,
    in_weight,
    beta_weight,
    log_decay,
    delta_gain,
):
    bf16, f32 = jnp.bfloat16, jnp.float32
    rows, head_columns = att_query.shape
    model = out_weight.shape[1]
    half_model = model // 2
    value_here = log_decay.shape[1]
    masks = (2, 3, 1)
    piece = pl.pallas_call(
        piece_kernel,
        out_shape=pltpu.VMEM((rows, HD), bf16),
        in_specs=[IN_HBM],
        out_specs=IN_VMEM,
        scratch_shapes=[pltpu.SemaphoreType.DMA],
        compiler_params=pltpu.CompilerParams(vmem_limit_bytes=4 * MIB),
    )(in_hbm(att_kv))
    mine = {mask: swapped(piece, "ctx", mask) for mask in masks[::-1]}
    piece, *late = lax.optimization_barrier((piece, att_query, att_gate, att_kv, out_weight, residual))
    late = fetched(*late)
    mine[2], (att_query, att_gate, att_kv, out_weight, residual) = lax.optimization_barrier((mine[2], late))
    twin = {mask: swapped(mine[mask], "sub") for mask in masks}
    heads, send = vmem_call(
        attention_kernel,
        [((rows, head_columns), bf16), ((rows, half_model), bf16)],
        [att_query, att_gate, att_kv, mine[1], mine[2], mine[3], twin[1], twin[2], twin[3], out_weight, residual],
        [
            pltpu.VMEM((4 * rows, HD), bf16),
            pltpu.VMEM((4 * rows, HD), bf16),
            pltpu.VMEM((rows, half_model), f32),
        ],
    )
    came = swapped(send, "sub")
    keep = vmem_call(keep_kernel, [((rows, half_model), f32)], [heads, out_weight, residual])[0]
    came, keep = lax.optimization_barrier((came, keep))
    chip_sum, send = vmem_call(
        chip_sum_kernel, [((rows, half_model), f32), ((rows, half_model), bf16)], [keep, came]
    )
    came = swapped(send, "head")
    send, *late = lax.optimization_barrier((send, in_weight, norm_gain[None, :], beta_weight.T, log_decay.T))
    late = fetched(*late)
    came, (in_weight, norm_gain, beta_weight, log_decay) = lax.optimization_barrier((came, late))
    hidden = vmem_call(hidden_kernel, [((rows, half_model), bf16)], [chip_sum, came])[0]
    twin_hidden = swapped(hidden, "sub")
    sums = vmem_call(
        own_half_kernel,
        [((rows, in_weight.shape[1]), f32), ((value_here, rows), f32), ((rows, LANES), f32)],
        [hidden, norm_gain, in_weight, beta_weight],
    )
    twin_hidden, (mixed, logits, squares) = lax.optimization_barrier((twin_hidden, sums))
    payload_shape = ((4 * rows + 16, LANES), bf16)
    payloads = {}
    scaled, scale, extra, payloads[2] = vmem_call(
        twin_half_kernel,
        [((rows, half_model), bf16), ((rows, LANES), f32), ((2 * value_here, rows), f32), payload_shape],
        [twin_hidden, norm_gain, beta_weight, log_decay, logits, squares, in_weight, mixed],
        [pltpu.VMEM((16, LANES), f32)],
    )
    for mask in (3, 1, 0):
        payloads[mask] = vmem_call(
            functools.partial(payload_kernel, mask),
            [payload_shape],
            [scaled, scale, in_weight, mixed, extra],
            [pltpu.VMEM((16, LANES), f32)],
        )[0]
    new_residual = vmem_call(residual_kernel, [(residual.shape, bf16)], [hidden, twin_hidden], last=True)[0]
    came = {mask: swapped(payloads[mask], "ctx", mask) for mask in masks}
    came[0] = payloads[0]
    half = rows // 2
    terms_shapes = [
        ((4, 2, 2, DK, DV), f32),
        ((4, 2, 2, DK + half, DK), bf16),
        ((4, 2, rows, DV), f32),
        ((4, 2, 2, 8, LANES), f32),
    ]
    terms = []
    for mask in (0, 2, 1, 3):
        terms = vmem_call(
            functools.partial(block_kernel, mask),
            terms_shapes,
            [came[mask], *terms],
            aliases={1 + i: i for i in range(4)} if terms else None,
        )
    own, *backs = vmem_call(
        scan_kernel,
        [((rows, 2 * DV), bf16)] * 4,
        [*terms, delta_gain[None, :]],
        [pltpu.VMEM((4, rows, 2 * DV), bf16)],
    )
    backs = {mask: swapped(backs[mask - 1], "ctx", mask) for mask in masks}
    delta_out = pl.pallas_call(
        place_kernel,
        out_shape=jax.ShapeDtypeStruct((rows, value_here * DV), bf16),
        in_specs=[IN_VMEM] * 4,
        out_specs=IN_HBM,
        scratch_shapes=[pltpu.SemaphoreType.DMA((4,))],
        compiler_params=pltpu.CompilerParams(vmem_limit_bytes=4 * MIB),
    )(*[in_vmem(back) for back in (own, backs[1], backs[2], backs[3])])
    return (new_residual, delta_out)


def solution(mesh):
    local = owner_local if owners_fit(mesh) else hop_local
    return jax.shard_map(
        local,
        mesh=mesh,
        in_specs=(
            P(("groups", "ctx"), ("head", "sub")),
            P(("groups", "ctx"), ("head", "sub")),
            P(("groups", "ctx"), None),
            P(("groups", "ctx"), ("head", "sub")),
            P(("head", "sub"), None),
            P(),
            P(None, ("head", "sub")),
            P(None, ("head", "sub")),
            P(("groups", "ctx"), ("head", "sub")),
            P(),
        ),
        out_specs=(P(("groups", "ctx"), ("head", "sub")), P(("groups", "ctx"), ("head", "sub"))),
        check_vma=False,
    )
```

```python
import functools

import jax
import jax.numpy as jnp
from jax import lax
from jax.experimental import pallas as pl
from jax.experimental.pallas import tpu as pltpu
from jax.sharding import PartitionSpec as P

HEADS = 16
KV_HEADS = 2
HD = 256
DK = 128
DV = 128


TOP_PRECISION = lax.Precision.HIGHEST
EPSILON = 1e-06
NEGATIVE = -1e30


def passed_along(value, axis, steps):
    count = lax.axis_size(axis)
    initial, last = (max(0, -steps), min(count, count - steps))
    return lax.ppermute(value, axis, [(source, source + steps) for source in range(initial, last)])


def stored_positions(first_row, row_total, half_rows, ctx_count):
    row_index = first_row + jnp.arange(row_total, dtype=jnp.int32)
    device_of = row_index // (2 * half_rows)
    within_dev = row_index % (2 * half_rows)
    block_number = jnp.where(within_dev < half_rows, device_of, 2 * ctx_count - 1 - device_of)
    return block_number * half_rows + within_dev % half_rows


def unit_rows(matrix):
    return matrix * lax.rsqrt(jnp.sum(matrix * matrix, axis=-1, keepdims=True) + EPSILON)


def to_blocks(array, half_rows):
    heads_count = array.shape[1]
    width = array.shape[2]
    shaped = array.reshape(2, half_rows, heads_count, width).transpose(2, 0, 1, 3)
    return shaped.reshape(heads_count * 2, half_rows, width)


def block_terms(query_rows, key_rows, value_rows, beta_rows, decay_rows):
    length = query_rows.shape[0]
    cumulative = jnp.cumsum(decay_rows)
    position = jnp.arange(length)
    on_or_below = position[:, None] >= position[None, :]
    strictly_below = position[:, None] > position[None, :]
    decay_gap = cumulative[:, None] - cumulative[None, :]
    decay_grid = jnp.where(on_or_below, jnp.exp(jnp.where(on_or_below, decay_gap, 0.0)), 0.0)
    key_gram = jnp.dot(key_rows, key_rows.T, precision=TOP_PRECISION)
    system = jnp.eye(length, dtype=jnp.float32) + jnp.where(
        strictly_below, beta_rows[:, None] * key_gram * decay_grid, 0.0
    )
    growth = jnp.exp(cumulative)
    right_side = beta_rows[:, None] * jnp.concatenate(
        [value_rows, growth[:, None] * key_rows], axis=1
    )
    solved = jax.scipy.linalg.solve_triangular(system, right_side, lower=True, unit_diagonal=True)
    update_rows = solved[:, : value_rows.shape[1]]
    weight_rows = solved[:, value_rows.shape[1] :]
    attend_grid = jnp.where(
        on_or_below, jnp.dot(query_rows, key_rows.T, precision=TOP_PRECISION) * decay_grid, 0.0
    )
    local_out = jnp.dot(attend_grid, update_rows, precision=TOP_PRECISION)
    read_rows = growth[:, None] * query_rows - jnp.dot(
        attend_grid, weight_rows, precision=TOP_PRECISION
    )
    carried_keys = jnp.exp(cumulative[-1] - cumulative)[:, None] * key_rows
    identity_map = jnp.eye(key_rows.shape[1], dtype=jnp.float32)
    transition = jnp.exp(cumulative[-1]) * identity_map - jnp.dot(
        carried_keys.T, weight_rows, precision=TOP_PRECISION
    )
    offset_state = jnp.dot(carried_keys.T, update_rows, precision=TOP_PRECISION)
    return (local_out, read_rows, transition, offset_state)


def apply_map(matrix_maps, offsets, states):
    return jnp.einsum("hij,hjk->hik", matrix_maps, states, precision=TOP_PRECISION) + offsets


def attend_rows(running, query_block, key_block, value_block, visible, score_scale):
    run_max, run_sum, run_acc = running
    scores = (
        jnp.einsum("rhd,kd->rhk", query_block, key_block, preferred_element_type=jnp.float32)
        * score_scale
    )
    if visible is not None:
        scores = jnp.where(visible[:, None, :], scores, NEGATIVE)
    new_max = jnp.maximum(run_max, jnp.max(scores, axis=2))
    weights = jnp.exp(scores - new_max[:, :, None])
    if visible is not None:
        weights = jnp.where(visible[:, None, :], weights, 0.0)
    rescale = jnp.exp(run_max - new_max)
    run_sum = run_sum * rescale + jnp.sum(weights, axis=2)
    added = jnp.einsum(
        "rhk,kd->rhd", weights.astype(jnp.bfloat16), value_block, preferred_element_type=jnp.float32
    )
    run_acc = run_acc * rescale[:, :, None] + added
    return (new_max, run_sum, run_acc)


def hop_local(
    att_query,
    att_gate,
    att_kv,
    residual,
    out_weight,
    norm_gain,
    in_weight,
    beta_weight,
    log_decay,
    delta_gain,
):
    ctx_count = lax.axis_size("ctx")
    ctx_rank = lax.axis_index("ctx")
    shard_rank = lax.axis_index(("head", "sub"))
    rows_here = att_query.shape[0]
    half_rows = rows_here // 2
    heads_here = att_query.shape[1] // HD
    kv_number = shard_rank * heads_here // (HEADS // KV_HEADS)
    key_local = lax.dynamic_slice_in_dim(att_kv, kv_number * 2 * HD, HD, 1)
    value_local = lax.dynamic_slice_in_dim(att_kv, kv_number * 2 * HD + HD, HD, 1)
    query_heads = att_query.reshape(rows_here, heads_here, HD)
    late_queries = query_heads[half_rows:]
    query_places = stored_positions(ctx_rank * rows_here, rows_here, half_rows, ctx_count)
    same_visible = query_places[:, None] >= query_places[None, :]
    score_scale = HD ** (-0.5)

    def earlier_shard(running, key_shard, value_shard):
        return attend_rows(
            running, query_heads, key_shard[:half_rows], value_shard[:half_rows], None, score_scale
        )

    def same_shard(running, key_shard, value_shard):
        return attend_rows(running, query_heads, key_shard, value_shard, same_visible, score_scale)

    def later_shard(running, key_shard, value_shard):
        late_part = tuple((member[half_rows:] for member in running))
        renewed = attend_rows(late_part, late_queries, key_shard, value_shard, None, score_scale)
        return tuple(
            (
                jnp.concatenate([member[:half_rows], latest], axis=0)
                for member, latest in zip(running, renewed)
            )
        )

    start_running = (
        jnp.full((rows_here, heads_here), NEGATIVE, jnp.float32),
        jnp.zeros((rows_here, heads_here), jnp.float32),
        jnp.zeros((rows_here, heads_here, HD), jnp.float32),
    )
    key_block = lax.all_gather(key_local, "ctx", axis=0, tiled=True)
    value_block = lax.all_gather(value_local, "ctx", axis=0, tiled=True)
    piece_rows = key_block.shape[0]

    def one_shard(number, current):
        offset = number * rows_here
        key_shard = lax.dynamic_slice_in_dim(key_block, offset, rows_here, 0)
        value_shard = lax.dynamic_slice_in_dim(value_block, offset, rows_here, 0)
        shard_number = offset // rows_here
        branch = jnp.clip(shard_number - ctx_rank, -1, 1) + 1
        return lax.switch(
            branch, [earlier_shard, same_shard, later_shard], current, key_shard, value_shard
        )

    run_max, run_sum, run_acc = lax.fori_loop(0, piece_rows // rows_here, one_shard, start_running)
    gate_heads = jax.nn.sigmoid(att_gate.reshape(rows_here, heads_here, HD).astype(jnp.float32))
    att_heads = (
        (run_acc / run_sum[:, :, None] * gate_heads)
        .astype(jnp.bfloat16)
        .reshape(rows_here, heads_here * HD)
    )
    partial_term = jnp.dot(att_heads, out_weight, preferred_element_type=jnp.float32)
    col_width = residual.shape[1]
    col_start = shard_rank * col_width
    placed = lax.dynamic_slice_in_dim(partial_term, col_start, col_width, 1) + residual.astype(
        jnp.float32
    )
    partial_term = lax.dynamic_update_slice_in_dim(partial_term, placed, col_start, 1)
    hidden = lax.psum(partial_term.astype(jnp.bfloat16), ("head", "sub")).astype(jnp.float32)
    mean_square = jnp.mean(hidden * hidden, axis=1, keepdims=True)
    normed = (hidden * lax.rsqrt(mean_square + EPSILON) * norm_gain).astype(jnp.bfloat16)
    new_residual = lax.dynamic_slice_in_dim(hidden, col_start, col_width, 1).astype(jnp.bfloat16)
    mixed_cols = jnp.dot(normed, in_weight, preferred_element_type=jnp.float32)
    beta_logits = jnp.dot(normed, beta_weight, preferred_element_type=jnp.float32)
    key_here = in_weight.shape[1] // (2 * DK + 2 * DV)
    value_here = 2 * key_here
    grouped = mixed_cols.reshape(rows_here, key_here, 2 * DK + 2 * DV)
    query_unit = jnp.repeat(unit_rows(jax.nn.silu(grouped[:, :, :DK])) * DK ** (-0.5), 2, axis=1)
    key_unit = jnp.repeat(unit_rows(jax.nn.silu(grouped[:, :, DK : 2 * DK])), 2, axis=1)
    value_all = jax.nn.silu(grouped[:, :, 2 * DK :]).reshape(rows_here, value_here, DV)
    beta_all = jax.nn.sigmoid(beta_logits)
    local_out, read_rows, transition, offset_state = jax.vmap(block_terms)(
        to_blocks(query_unit, half_rows),
        to_blocks(key_unit, half_rows),
        to_blocks(value_all, half_rows),
        to_blocks(beta_all[:, :, None], half_rows)[:, :, 0],
        to_blocks(log_decay[:, :, None], half_rows)[:, :, 0],
    )
    transition = transition.reshape(value_here, 2, DK, DK)
    offset_state = offset_state.reshape(value_here, 2, DK, DV)
    early_map, late_map = (transition[:, 0], transition[:, 1])
    early_offset, late_offset = (offset_state[:, 0], offset_state[:, 1])
    last_rank = ctx_count - 1
    zero_states = jnp.zeros_like(early_offset)

    def early_turn(number, incoming):
        return passed_along(
            apply_map(early_map, early_offset, incoming).astype(jnp.bfloat16), "ctx", 1
        ).astype(jnp.float32)

    early_in = lax.fori_loop(0, ctx_count - 1, early_turn, zero_states)
    early_end = apply_map(early_map, early_offset, early_in)
    late_start = jnp.where(ctx_rank == last_rank, early_end, zero_states)

    def late_turn(number, incoming):
        moved = passed_along(
            apply_map(late_map, late_offset, incoming).astype(jnp.bfloat16), "ctx", -1
        ).astype(jnp.float32)
        return jnp.where(ctx_rank == last_rank, early_end, moved)

    late_in = lax.fori_loop(0, ctx_count - 1, late_turn, late_start)
    states_in = jnp.stack([early_in, late_in], axis=1)
    block_out = local_out.reshape(value_here, 2, half_rows, DV) + jnp.einsum(
        "hbck,hbkv->hbcv",
        read_rows.reshape(value_here, 2, half_rows, DK),
        states_in,
        precision=TOP_PRECISION,
    )
    token_out = block_out.transpose(1, 2, 0, 3).reshape(rows_here, value_here, DV)
    out_square = jnp.mean(token_out * token_out, axis=2, keepdims=True)
    delta_out = (token_out * lax.rsqrt(out_square + EPSILON) * delta_gain).astype(jnp.bfloat16)
    return (new_residual, delta_out.reshape(rows_here, value_here * DV))


KEY_HEADS = 16
IN_VMEM = pl.BlockSpec(memory_space=pltpu.VMEM)
IN_HBM = pl.BlockSpec(memory_space=pl.ANY)
MIB = 2**20
LANES = 128


def owners_fit(mesh):
    shards = mesh.shape["head"] * mesh.shape["sub"]
    key_here = KEY_HEADS // shards
    return mesh.shape["head"] == 2 and mesh.shape["sub"] == 2 and key_here == mesh.shape["ctx"]


def in_vmem(array):
    return pltpu.with_memory_space_constraint(array, pltpu.VMEM)


def in_hbm(array):
    return pltpu.with_memory_space_constraint(array, pltpu.HBM)


def vmem_call(kernel, outs, operands, scratch=(), limit=16, aliases=None, last=False, cost=None):
    make = jax.ShapeDtypeStruct if last else pltpu.VMEM
    return pl.pallas_call(
        kernel,
        out_shape=[make(shape, dtype) for shape, dtype in outs],
        in_specs=[IN_VMEM] * len(operands),
        out_specs=[IN_VMEM] * len(outs),
        scratch_shapes=list(scratch),
        input_output_aliases=aliases or {},
        cost_estimate=cost,
        compiler_params=pltpu.CompilerParams(vmem_limit_bytes=limit * MIB),
    )(*[in_vmem(operand) for operand in operands])


def swapped(value, axis, mask=1):
    return lax.ppermute(value, axis, [(i, i ^ mask) for i in range(lax.axis_size(axis))])


def dot(left, right, dims=((1,), (0,))):
    return lax.dot_general(left, right, (dims, ((), ())), preferred_element_type=jnp.float32)


def halves(value):
    high = value.astype(jnp.bfloat16)
    return high, (value - high.astype(jnp.float32)).astype(jnp.bfloat16)


def sigmoid(value):
    return 1.0 / (1.0 + jnp.exp(-value))


def silu(value):
    return value / (1.0 + jnp.exp(-value))


def piece_kernel(kv_ref, piece_ref, sem):
    start = (lax.axis_index("head") * 2 + lax.axis_index("sub")) * HD
    copy = pltpu.make_async_copy(kv_ref.at[:, pl.ds(pl.multiple_of(start, HD), HD)], piece_ref, sem)
    copy.start()
    copy.wait()


def fetch_kernel(*refs):
    count = len(refs) // 2
    copies = [
        pltpu.make_async_copy(refs[n], refs[count + n], refs[-1].at[n]) for n in range(count)
    ]
    for copy in copies:
        copy.start()
    for copy in copies:
        copy.wait()


def fetched(*arrays):
    moved = sum(array.size * array.dtype.itemsize for array in arrays)
    return pl.pallas_call(
        fetch_kernel,
        out_shape=[pltpu.VMEM(array.shape, array.dtype) for array in arrays],
        in_specs=[IN_HBM] * len(arrays),
        out_specs=[IN_VMEM] * len(arrays),
        scratch_shapes=[pltpu.SemaphoreType.DMA((len(arrays),))],
        compiler_params=pltpu.CompilerParams(vmem_limit_bytes=4 * MIB),
        cost_estimate=pl.CostEstimate(flops=0, bytes_accessed=moved, transcendentals=0),
    )(*[in_hbm(array) for array in arrays])


def attend(query_ref, gate_ref, keys, values, rows, key_total, visible):
    count = query_ref.shape[1] // HD
    columns = [slice(head * HD, (head + 1) * HD) for head in range(count)]
    size = rows.stop - rows.start
    queries = jnp.concatenate([query_ref[rows, part] for part in columns], axis=0)
    gates = [sigmoid(gate_ref[rows, part].astype(jnp.float32)) for part in columns]
    scores = dot(queries, keys[0:key_total], ((1,), (1,))) * HD ** (-0.5)
    scores = jnp.where(jnp.concatenate([visible] * count, axis=0), scores, NEGATIVE)
    weights = jnp.exp(scores - jnp.max(scores, axis=1, keepdims=True))
    total = jnp.sum(weights, axis=1, keepdims=True)
    gathered = dot(weights.astype(jnp.bfloat16), values[0:key_total]) / total
    gated = [gathered[head * size : (head + 1) * size] * gates[head] for head in range(count)]
    return jnp.concatenate(gated, axis=1).astype(jnp.bfloat16)


def attention_kernel(
    query_ref, gate_ref, kv_ref, mine1, mine2, mine3, twin1, twin2, twin3, weight_ref, residual_ref,
    heads_ref, send_ref, keys, values, sums,
):
    half = query_ref.shape[0] // 2
    ctx_rank, head_rank, sub_rank = (lax.axis_index(name) for name in ("ctx", "head", "sub"))
    count = 4
    own_start = pl.multiple_of(head_rank * 2 * HD, 2 * HD)

    def put(target, mask, part):
        target[mask * half : (mask + 1) * half] = part[0:half]
        target[(count + mask) * half : (count + mask + 1) * half] = part[half : 2 * half]

    put(keys, 0, kv_ref[:, pl.ds(own_start, HD)])
    put(values, 0, kv_ref[:, pl.ds(own_start + HD, HD)])

    @pl.when(sub_rank == 0)
    def _():
        for mask, (mine, twin) in enumerate(((mine1, twin1), (mine2, twin2), (mine3, twin3)), 1):
            put(keys, mask, mine[...])
            put(values, mask, twin[...])

    @pl.when(sub_rank != 0)
    def _():
        for mask, (mine, twin) in enumerate(((mine1, twin1), (mine2, twin2), (mine3, twin3)), 1):
            put(keys, mask, twin[...])
            put(values, mask, mine[...])

    shift = half.bit_length() - 1
    row = lax.broadcasted_iota(jnp.int32, (half, 1), 0)
    column = lax.broadcasted_iota(jnp.int32, (1, 2 * count * half), 1)
    device = jnp.bitwise_xor(ctx_rank, (column >> shift) & (count - 1))
    block = jnp.where(column < count * half, device, 2 * count - 1 - device)
    key_place = block * half + (column & (half - 1))
    for part, block_here in enumerate((ctx_rank, 2 * count - 1 - ctx_rank)):
        rows = slice(part * half, (part + 1) * half)
        key_total = (part + 1) * count * half
        visible = row + block_here * half >= key_place[:, :key_total]
        heads_ref[rows] = attend(query_ref, gate_ref, keys, values, rows, key_total, visible)
    mid = send_ref.shape[1]
    width = residual_ref.shape[1]
    sums[...] = dot(heads_ref[...], weight_ref[:, pl.ds(pl.multiple_of((1 - sub_rank) * mid, mid), mid)])

    @pl.when(sub_rank != head_rank)
    def _():
        sums[:, pl.ds(pl.multiple_of(sub_rank * width, width), width)] += residual_ref[...].astype(jnp.float32)

    send_ref[...] = sums[...].astype(jnp.bfloat16)


def keep_kernel(heads_ref, weight_ref, residual_ref, keep_ref):
    head_rank, sub_rank = lax.axis_index("head"), lax.axis_index("sub")
    mid = keep_ref.shape[1]
    width = residual_ref.shape[1]
    keep_ref[...] = dot(heads_ref[...], weight_ref[:, pl.ds(pl.multiple_of(sub_rank * mid, mid), mid)])

    @pl.when(sub_rank == head_rank)
    def _():
        keep_ref[:, pl.ds(pl.multiple_of(sub_rank * width, width), width)] += residual_ref[...].astype(jnp.float32)


def chip_sum_kernel(keep_ref, came_ref, sum_ref, send_ref):
    total = keep_ref[...] + came_ref[...].astype(jnp.float32)
    sum_ref[...] = total
    send_ref[...] = total.astype(jnp.bfloat16)


def hidden_kernel(keep_ref, came_ref, hidden_ref):
    hidden_ref[...] = (keep_ref[...] + came_ref[...].astype(jnp.float32)).astype(jnp.bfloat16)


def half_of(ref, own):
    sub_rank = lax.axis_index("sub")
    mid = ref.shape[-1] // 2
    return pl.ds(pl.multiple_of((sub_rank if own else 1 - sub_rank) * mid, mid), mid)


def own_half_kernel(own_ref, gain_ref, weight_ref, beta_ref, mixed_ref, logit_ref, square_ref):
    mid = own_ref.shape[1]
    own = own_ref[...].astype(jnp.float32)
    columns = half_of(gain_ref, True)
    scaled = (own * gain_ref[:, columns]).astype(jnp.bfloat16)
    square_ref[...] = jnp.broadcast_to(jnp.sum(own * own, axis=1, keepdims=True), square_ref.shape)
    logit_ref[...] = dot(beta_ref[:, columns], scaled, ((1,), (1,)))
    rows = pl.ds(pl.multiple_of(lax.axis_index("sub") * mid, mid), mid)
    mixed_ref[...] = dot(scaled, weight_ref[rows, :])


def twin_half_kernel(
    twin_ref, gain_ref, beta_ref, decay_ref, logit_ref, square_ref, weight_ref, mixed_ref,
    scaled_ref, scale_ref, extra_ref, payload_ref, small,
):
    twin = twin_ref[...].astype(jnp.float32)
    columns = half_of(gain_ref, False)
    scaled_ref[...] = (twin * gain_ref[:, columns]).astype(jnp.bfloat16)
    squares = square_ref[...] + jnp.sum(twin * twin, axis=1, keepdims=True)
    scale = lax.rsqrt(squares / gain_ref.shape[1] + EPSILON)
    scale_ref[...] = scale
    values = decay_ref.shape[0]
    logits = logit_ref[...] + dot(beta_ref[:, columns], scaled_ref[...], ((1,), (1,)))
    extra_ref[0:values] = decay_ref[...]
    extra_ref[values : 2 * values] = sigmoid(logits * jnp.transpose(scale)[0:1])
    payload_kernel(2, scaled_ref, scale_ref, weight_ref, mixed_ref, extra_ref, payload_ref, small)


def residual_kernel(own_ref, twin_ref, residual_ref):
    head_rank, sub_rank = lax.axis_index("head"), lax.axis_index("sub")
    width = residual_ref.shape[1]
    columns = pl.ds(pl.multiple_of(sub_rank * width, width), width)

    @pl.when(sub_rank == head_rank)
    def _():
        residual_ref[...] = own_ref[:, columns]

    @pl.when(sub_rank != head_rank)
    def _():
        residual_ref[...] = twin_ref[:, columns]


def payload_kernel(mask, scaled_ref, scale_ref, weight_ref, mixed_ref, extra_ref, payload_ref, small):
    rows, mid = scaled_ref.shape
    group = 2 * DK + 2 * DV
    target = jnp.bitwise_xor(lax.axis_index("ctx"), mask)
    columns = pl.ds(pl.multiple_of(target * group, group), group)
    weight_rows = pl.ds(pl.multiple_of((1 - lax.axis_index("sub")) * mid, mid), mid)
    mixed = mixed_ref[:, columns] + dot(scaled_ref[...], weight_ref[weight_rows, columns])
    mixed = silu(mixed * scale_ref[:, 0:1])
    query, key = mixed[:, :DK], mixed[:, DK : 2 * DK]
    payload_ref[0:rows] = (unit_rows(query) * DK ** (-0.5)).astype(jnp.bfloat16)
    payload_ref[rows : 2 * rows] = unit_rows(key).astype(jnp.bfloat16)
    payload_ref[2 * rows : 3 * rows] = mixed[:, 2 * DK : 2 * DK + DV].astype(jnp.bfloat16)
    payload_ref[3 * rows : 4 * rows] = mixed[:, 2 * DK + DV :].astype(jnp.bfloat16)
    values = extra_ref.shape[0] // 2
    small[...] = jnp.zeros_like(small)
    for place, base in ((0, 0), (4, values)):
        full = extra_ref[pl.ds(base + 2 * target, 2), :]
        high = full.astype(jnp.bfloat16).astype(jnp.float32)
        small[place : place + 2] = high
        small[place + 2 : place + 4] = full - high
    payload_ref[4 * rows : 4 * rows + 16] = small[...].astype(jnp.bfloat16)


def joined(left, right):
    (left_high, left_low), (right_high, right_low) = left, right
    return dot(
        jnp.concatenate([left_high, left_high, left_low], axis=1),
        jnp.concatenate([right_high, right_low, right_high], axis=0),
    )


def unit_lower_inverses(stricts, row, column):
    inner = (row >> 3) == (column >> 3)
    identity = jnp.where(row == column, 1.0, 0.0)
    number = range(len(stricts))
    smalls = [jnp.where(inner, strict, 0.0) for strict in stricts]
    rests = [halves(jnp.where(inner, 0.0, strict)) for strict in stricts]
    small = [halves(part) for part in smalls]
    inverses = [identity - part for part in smalls]
    split = [halves(inverse) for inverse in inverses]
    seconds = [halves(joined(part, part)) for part in small]
    fourths = [halves(joined(second, second)) for second in seconds]
    inverses = [inverses[n] + joined(split[n], seconds[n]) for n in number]
    split = [halves(inverse) for inverse in inverses]
    inverses = [inverses[n] + joined(split[n], fourths[n]) for n in number]
    split = [halves(inverse) for inverse in inverses]
    steps = [halves(joined(split[n], rests[n])) for n in number]
    doubles = [halves(joined(step, step)) for step in steps]
    results = [inverses[n] - joined(steps[n], split[n]) for n in number]
    quads = [halves(joined(double, double)) for double in doubles]
    results = [results[n] + joined(doubles[n], halves(results[n])) for n in number]
    return [results[n] + joined(quads[n], halves(results[n])) for n in number]


def block_kernel(mask, payload_ref, *refs):
    offset_ref, linear_ref, local_ref, growth_ref = refs[-4:]
    source = jnp.bitwise_xor(lax.axis_index("ctx"), mask)
    rows = (payload_ref.shape[0] - 16) // 4
    half = rows // 2
    shift = half.bit_length() - 1
    row = lax.broadcasted_iota(jnp.int32, (rows, 1), 0)
    column = lax.broadcasted_iota(jnp.int32, (1, rows), 1)
    together = (row >> shift) == (column >> shift)
    inclusive = together & (row >= column)
    strictly = together & (row > column)
    early = column < half
    below = jnp.where(inclusive, 1.0, 0.0).astype(jnp.bfloat16)
    diagonal = jnp.where(row == column, 1.0, 0.0).astype(jnp.bfloat16)
    heads = range(2)
    query, key = payload_ref[0:rows], payload_ref[rows : 2 * rows]
    extra = payload_ref[4 * rows : 4 * rows + 16]
    sums_row = dot(extra, below, ((1,), (1,)))
    turned = dot(jnp.concatenate([below, diagonal], axis=0), extra, ((1,), (1,)))
    key_gram = dot(key, key, ((1,), (1,)))
    total_rows = [sums_row[h : h + 1] + sums_row[h + 2 : h + 3] for h in heads]
    totals = [turned[:rows, h : h + 1] + turned[:rows, h + 2 : h + 3] for h in heads]
    betas = [turned[rows:, h + 4 : h + 5] + turned[rows:, h + 6 : h + 7] for h in heads]
    decays = [jnp.exp(jnp.where(inclusive, totals[h] - total_rows[h], NEGATIVE)) for h in heads]
    stricts = [jnp.where(strictly, betas[h] * key_gram * decays[h], 0.0) for h in heads]
    query_gram = dot(query, key, ((1,), (1,)))
    key_wide = key.astype(jnp.float32)
    key_turned = jnp.transpose(key_wide)
    growths = [jnp.exp(total) for total in totals]
    values = [payload_ref[(2 + h) * rows : (3 + h) * rows].astype(jnp.float32) for h in heads]
    rights = [
        jnp.concatenate([betas[h] * values[h], (betas[h] * growths[h]) * key_wide], axis=1).astype(jnp.bfloat16)
        for h in heads
    ]
    grams = [(query_gram * decays[h]).astype(jnp.bfloat16) for h in heads]
    ends = [jnp.where(early, total[:, half - 1 : half], total[:, rows - 1 : rows]) for total in total_rows]
    carried = [key_turned * jnp.exp(ends[h] - total_rows[h]) for h in heads]
    lefts = [
        jnp.concatenate([jnp.where(early, keys, 0.0), jnp.where(early, 0.0, keys)], axis=0).astype(jnp.bfloat16)
        for keys in carried
    ]
    inverses = [halves(inverse) for inverse in unit_lower_inverses(stricts, row, column)]
    solved = [
        (dot(high, right) + dot(low, right)).astype(jnp.bfloat16) for (high, low), right in zip(inverses, rights)
    ]
    moved = [dot(jnp.concatenate([lefts[h], grams[h]], axis=0), solved[h]) for h in heads]
    for h in heads:
        attended = moved[h][2 * DK :]
        local_ref[source, h] = attended[:, :DV]
        reads = (growths[h] * query.astype(jnp.float32) - attended[:, DV:]).astype(jnp.bfloat16)
        growth = jnp.exp(ends[h])
        for block in range(2):
            state = moved[h][block * DK : (block + 1) * DK]
            offset_ref[source, h, block] = state[:, :DV]
            linear_ref[source, h, block, 0:DK] = state[:, DV:].astype(jnp.bfloat16)
            linear_ref[source, h, block, DK : DK + half] = reads[block * half : (block + 1) * half]
            last = (block + 1) * half - 1
            growth_ref[source, h, block] = jnp.broadcast_to(growth[:, last : last + 1], growth_ref.shape[3:])


def scan_kernel(offset_ref, linear_ref, local_ref, growth_ref, gain_ref, own_ref, back1, back2, back3, outs):
    count = offset_ref.shape[0]
    half = local_ref.shape[2] // 2
    rank = lax.axis_index("ctx")
    states = [None, None]
    for number in range(2 * count):
        source, block = (number, 0) if number < count else (2 * count - 1 - number, 1)
        block_rows = slice(block * half, (block + 1) * half)
        for head in range(2):
            out = local_ref[source, head, block_rows]
            state = offset_ref[source, head, block]
            if states[head] is not None:
                moved = dot(linear_ref[source, head, block], states[head].astype(jnp.bfloat16))
                out = out + moved[DK:]
                state = state - moved[:DK] + growth_ref[source, head, block, 0:1] * states[head]
            states[head] = state
            scale = lax.rsqrt(jnp.mean(out * out, axis=1, keepdims=True) + EPSILON)
            outs[source, block_rows, head * DV : (head + 1) * DV] = (out * scale * gain_ref[...]).astype(jnp.bfloat16)
    own_ref[...] = outs[rank]
    for mask, back in enumerate((back1, back2, back3), 1):
        back[...] = outs[jnp.bitwise_xor(rank, mask)]


def place_kernel(own_ref, back3, back1, back2, out_ref, sems):
    width = own_ref.shape[1]
    rank = lax.axis_index("ctx")
    copies = []
    for mask, back in enumerate((own_ref, back1, back2, back3)):
        columns = pl.ds(pl.multiple_of(jnp.bitwise_xor(rank, mask) * width, width), width)
        copies.append(pltpu.make_async_copy(back, out_ref.at[:, columns], sems.at[mask]))
        copies[-1].start()
    for copy in copies:
        copy.wait()


def owner_local(
    att_query,
    att_gate,
    att_kv,
    residual,
    out_weight,
    norm_gain,
    in_weight,
    beta_weight,
    log_decay,
    delta_gain,
):
    bf16, f32 = jnp.bfloat16, jnp.float32
    rows, head_columns = att_query.shape
    model = out_weight.shape[1]
    half_model = model // 2
    value_here = log_decay.shape[1]
    masks = (2, 3, 1)
    piece = pl.pallas_call(
        piece_kernel,
        out_shape=pltpu.VMEM((rows, HD), bf16),
        in_specs=[IN_HBM],
        out_specs=IN_VMEM,
        scratch_shapes=[pltpu.SemaphoreType.DMA],
        compiler_params=pltpu.CompilerParams(vmem_limit_bytes=4 * MIB),
    )(in_hbm(att_kv))
    mine = {mask: swapped(piece, "ctx", mask) for mask in masks[::-1]}
    piece, *late = lax.optimization_barrier((piece, att_query, att_gate, att_kv, out_weight, residual))
    late = fetched(*late)
    mine[3], (att_query, att_gate, att_kv, out_weight, residual) = lax.optimization_barrier((mine[3], late))
    twin = {mask: swapped(mine[mask], "sub") for mask in masks}
    heads, send = vmem_call(
        attention_kernel,
        [((rows, head_columns), bf16), ((rows, half_model), bf16)],
        [att_query, att_gate, att_kv, mine[1], mine[2], mine[3], twin[1], twin[2], twin[3], out_weight, residual],
        [
            pltpu.VMEM((4 * rows, HD), bf16),
            pltpu.VMEM((4 * rows, HD), bf16),
            pltpu.VMEM((rows, half_model), f32),
        ],
    )
    came = swapped(send, "sub")
    keep = vmem_call(keep_kernel, [((rows, half_model), f32)], [heads, out_weight, residual])[0]
    came, keep = lax.optimization_barrier((came, keep))
    chip_sum, send = vmem_call(
        chip_sum_kernel, [((rows, half_model), f32), ((rows, half_model), bf16)], [keep, came]
    )
    came = swapped(send, "head")
    send, *late = lax.optimization_barrier((send, in_weight, norm_gain[None, :], beta_weight.T, log_decay.T))
    late = fetched(*late)
    came, (in_weight, norm_gain, beta_weight, log_decay) = lax.optimization_barrier((came, late))
    hidden = vmem_call(hidden_kernel, [((rows, half_model), bf16)], [chip_sum, came])[0]
    twin_hidden = swapped(hidden, "sub")
    sums = vmem_call(
        own_half_kernel,
        [((rows, in_weight.shape[1]), f32), ((value_here, rows), f32), ((rows, LANES), f32)],
        [hidden, norm_gain, in_weight, beta_weight],
    )
    twin_hidden, (mixed, logits, squares) = lax.optimization_barrier((twin_hidden, sums))
    payload_shape = ((4 * rows + 16, LANES), bf16)
    payloads = {}
    scaled, scale, extra, payloads[2] = vmem_call(
        twin_half_kernel,
        [((rows, half_model), bf16), ((rows, LANES), f32), ((2 * value_here, rows), f32), payload_shape],
        [twin_hidden, norm_gain, beta_weight, log_decay, logits, squares, in_weight, mixed],
        [pltpu.VMEM((16, LANES), f32)],
    )
    for mask in (3, 1, 0):
        payloads[mask] = vmem_call(
            functools.partial(payload_kernel, mask),
            [payload_shape],
            [scaled, scale, in_weight, mixed, extra],
            [pltpu.VMEM((16, LANES), f32)],
        )[0]
    new_residual = vmem_call(residual_kernel, [(residual.shape, bf16)], [hidden, twin_hidden], last=True)[0]
    came = {mask: swapped(payloads[mask], "ctx", mask) for mask in masks}
    came[0] = payloads[0]
    half = rows // 2
    terms_shapes = [
        ((4, 2, 2, DK, DV), f32),
        ((4, 2, 2, DK + half, DK), bf16),
        ((4, 2, rows, DV), f32),
        ((4, 2, 2, 8, LANES), f32),
    ]
    terms = []
    for mask in (0, 2, 1, 3):
        terms = vmem_call(
            functools.partial(block_kernel, mask),
            terms_shapes,
            [came[mask], *terms],
            aliases={1 + i: i for i in range(4)} if terms else None,
        )
    own, *backs = vmem_call(
        scan_kernel,
        [((rows, 2 * DV), bf16)] * 4,
        [*terms, delta_gain[None, :]],
        [pltpu.VMEM((4, rows, 2 * DV), bf16)],
    )
    backs = {mask: swapped(backs[mask - 1], "ctx", mask) for mask in masks}
    delta_out = pl.pallas_call(
        place_kernel,
        out_shape=jax.ShapeDtypeStruct((rows, value_here * DV), bf16),
        in_specs=[IN_VMEM] * 4,
        out_specs=IN_HBM,
        scratch_shapes=[pltpu.SemaphoreType.DMA((4,))],
        compiler_params=pltpu.CompilerParams(vmem_limit_bytes=4 * MIB),
    )(*[in_vmem(back) for back in (own, backs[3], backs[1], backs[2])])
    return (new_residual, delta_out)


def solution(mesh):
    local = owner_local if owners_fit(mesh) else hop_local
    return jax.shard_map(
        local,
        mesh=mesh,
        in_specs=(
            P(("groups", "ctx"), ("head", "sub")),
            P(("groups", "ctx"), ("head", "sub")),
            P(("groups", "ctx"), None),
            P(("groups", "ctx"), ("head", "sub")),
            P(("head", "sub"), None),
            P(),
            P(None, ("head", "sub")),
            P(None, ("head", "sub")),
            P(("groups", "ctx"), ("head", "sub")),
            P(),
        ),
        out_specs=(P(("groups", "ctx"), ("head", "sub")), P(("groups", "ctx"), ("head", "sub"))),
        check_vma=False,
    )
```

```python
import functools

import jax
import jax.numpy as jnp
from jax import lax
from jax.experimental import pallas as pl
from jax.experimental.pallas import tpu as pltpu
from jax.sharding import PartitionSpec as P

HEADS = 16
KV_HEADS = 2
HD = 256
DK = 128
DV = 128


TOP_PRECISION = lax.Precision.HIGHEST
EPSILON = 1e-06
NEGATIVE = -1e30


def passed_along(value, axis, steps):
    count = lax.axis_size(axis)
    initial, last = (max(0, -steps), min(count, count - steps))
    return lax.ppermute(value, axis, [(source, source + steps) for source in range(initial, last)])


def stored_positions(first_row, row_total, half_rows, ctx_count):
    row_index = first_row + jnp.arange(row_total, dtype=jnp.int32)
    device_of = row_index // (2 * half_rows)
    within_dev = row_index % (2 * half_rows)
    block_number = jnp.where(within_dev < half_rows, device_of, 2 * ctx_count - 1 - device_of)
    return block_number * half_rows + within_dev % half_rows


def unit_rows(matrix):
    return matrix * lax.rsqrt(jnp.sum(matrix * matrix, axis=-1, keepdims=True) + EPSILON)


def to_blocks(array, half_rows):
    heads_count = array.shape[1]
    width = array.shape[2]
    shaped = array.reshape(2, half_rows, heads_count, width).transpose(2, 0, 1, 3)
    return shaped.reshape(heads_count * 2, half_rows, width)


def block_terms(query_rows, key_rows, value_rows, beta_rows, decay_rows):
    length = query_rows.shape[0]
    cumulative = jnp.cumsum(decay_rows)
    position = jnp.arange(length)
    on_or_below = position[:, None] >= position[None, :]
    strictly_below = position[:, None] > position[None, :]
    decay_gap = cumulative[:, None] - cumulative[None, :]
    decay_grid = jnp.where(on_or_below, jnp.exp(jnp.where(on_or_below, decay_gap, 0.0)), 0.0)
    key_gram = jnp.dot(key_rows, key_rows.T, precision=TOP_PRECISION)
    system = jnp.eye(length, dtype=jnp.float32) + jnp.where(
        strictly_below, beta_rows[:, None] * key_gram * decay_grid, 0.0
    )
    growth = jnp.exp(cumulative)
    right_side = beta_rows[:, None] * jnp.concatenate(
        [value_rows, growth[:, None] * key_rows], axis=1
    )
    solved = jax.scipy.linalg.solve_triangular(system, right_side, lower=True, unit_diagonal=True)
    update_rows = solved[:, : value_rows.shape[1]]
    weight_rows = solved[:, value_rows.shape[1] :]
    attend_grid = jnp.where(
        on_or_below, jnp.dot(query_rows, key_rows.T, precision=TOP_PRECISION) * decay_grid, 0.0
    )
    local_out = jnp.dot(attend_grid, update_rows, precision=TOP_PRECISION)
    read_rows = growth[:, None] * query_rows - jnp.dot(
        attend_grid, weight_rows, precision=TOP_PRECISION
    )
    carried_keys = jnp.exp(cumulative[-1] - cumulative)[:, None] * key_rows
    identity_map = jnp.eye(key_rows.shape[1], dtype=jnp.float32)
    transition = jnp.exp(cumulative[-1]) * identity_map - jnp.dot(
        carried_keys.T, weight_rows, precision=TOP_PRECISION
    )
    offset_state = jnp.dot(carried_keys.T, update_rows, precision=TOP_PRECISION)
    return (local_out, read_rows, transition, offset_state)


def apply_map(matrix_maps, offsets, states):
    return jnp.einsum("hij,hjk->hik", matrix_maps, states, precision=TOP_PRECISION) + offsets


def attend_rows(running, query_block, key_block, value_block, visible, score_scale):
    run_max, run_sum, run_acc = running
    scores = (
        jnp.einsum("rhd,kd->rhk", query_block, key_block, preferred_element_type=jnp.float32)
        * score_scale
    )
    if visible is not None:
        scores = jnp.where(visible[:, None, :], scores, NEGATIVE)
    new_max = jnp.maximum(run_max, jnp.max(scores, axis=2))
    weights = jnp.exp(scores - new_max[:, :, None])
    if visible is not None:
        weights = jnp.where(visible[:, None, :], weights, 0.0)
    rescale = jnp.exp(run_max - new_max)
    run_sum = run_sum * rescale + jnp.sum(weights, axis=2)
    added = jnp.einsum(
        "rhk,kd->rhd", weights.astype(jnp.bfloat16), value_block, preferred_element_type=jnp.float32
    )
    run_acc = run_acc * rescale[:, :, None] + added
    return (new_max, run_sum, run_acc)


def hop_local(
    att_query,
    att_gate,
    att_kv,
    residual,
    out_weight,
    norm_gain,
    in_weight,
    beta_weight,
    log_decay,
    delta_gain,
):
    ctx_count = lax.axis_size("ctx")
    ctx_rank = lax.axis_index("ctx")
    shard_rank = lax.axis_index(("head", "sub"))
    rows_here = att_query.shape[0]
    half_rows = rows_here // 2
    heads_here = att_query.shape[1] // HD
    kv_number = shard_rank * heads_here // (HEADS // KV_HEADS)
    key_local = lax.dynamic_slice_in_dim(att_kv, kv_number * 2 * HD, HD, 1)
    value_local = lax.dynamic_slice_in_dim(att_kv, kv_number * 2 * HD + HD, HD, 1)
    query_heads = att_query.reshape(rows_here, heads_here, HD)
    late_queries = query_heads[half_rows:]
    query_places = stored_positions(ctx_rank * rows_here, rows_here, half_rows, ctx_count)
    same_visible = query_places[:, None] >= query_places[None, :]
    score_scale = HD ** (-0.5)

    def earlier_shard(running, key_shard, value_shard):
        return attend_rows(
            running, query_heads, key_shard[:half_rows], value_shard[:half_rows], None, score_scale
        )

    def same_shard(running, key_shard, value_shard):
        return attend_rows(running, query_heads, key_shard, value_shard, same_visible, score_scale)

    def later_shard(running, key_shard, value_shard):
        late_part = tuple((member[half_rows:] for member in running))
        renewed = attend_rows(late_part, late_queries, key_shard, value_shard, None, score_scale)
        return tuple(
            (
                jnp.concatenate([member[:half_rows], latest], axis=0)
                for member, latest in zip(running, renewed)
            )
        )

    start_running = (
        jnp.full((rows_here, heads_here), NEGATIVE, jnp.float32),
        jnp.zeros((rows_here, heads_here), jnp.float32),
        jnp.zeros((rows_here, heads_here, HD), jnp.float32),
    )
    key_block = lax.all_gather(key_local, "ctx", axis=0, tiled=True)
    value_block = lax.all_gather(value_local, "ctx", axis=0, tiled=True)
    piece_rows = key_block.shape[0]

    def one_shard(number, current):
        offset = number * rows_here
        key_shard = lax.dynamic_slice_in_dim(key_block, offset, rows_here, 0)
        value_shard = lax.dynamic_slice_in_dim(value_block, offset, rows_here, 0)
        shard_number = offset // rows_here
        branch = jnp.clip(shard_number - ctx_rank, -1, 1) + 1
        return lax.switch(
            branch, [earlier_shard, same_shard, later_shard], current, key_shard, value_shard
        )

    run_max, run_sum, run_acc = lax.fori_loop(0, piece_rows // rows_here, one_shard, start_running)
    gate_heads = jax.nn.sigmoid(att_gate.reshape(rows_here, heads_here, HD).astype(jnp.float32))
    att_heads = (
        (run_acc / run_sum[:, :, None] * gate_heads)
        .astype(jnp.bfloat16)
        .reshape(rows_here, heads_here * HD)
    )
    partial_term = jnp.dot(att_heads, out_weight, preferred_element_type=jnp.float32)
    col_width = residual.shape[1]
    col_start = shard_rank * col_width
    placed = lax.dynamic_slice_in_dim(partial_term, col_start, col_width, 1) + residual.astype(
        jnp.float32
    )
    partial_term = lax.dynamic_update_slice_in_dim(partial_term, placed, col_start, 1)
    hidden = lax.psum(partial_term.astype(jnp.bfloat16), ("head", "sub")).astype(jnp.float32)
    mean_square = jnp.mean(hidden * hidden, axis=1, keepdims=True)
    normed = (hidden * lax.rsqrt(mean_square + EPSILON) * norm_gain).astype(jnp.bfloat16)
    new_residual = lax.dynamic_slice_in_dim(hidden, col_start, col_width, 1).astype(jnp.bfloat16)
    mixed_cols = jnp.dot(normed, in_weight, preferred_element_type=jnp.float32)
    beta_logits = jnp.dot(normed, beta_weight, preferred_element_type=jnp.float32)
    key_here = in_weight.shape[1] // (2 * DK + 2 * DV)
    value_here = 2 * key_here
    grouped = mixed_cols.reshape(rows_here, key_here, 2 * DK + 2 * DV)
    query_unit = jnp.repeat(unit_rows(jax.nn.silu(grouped[:, :, :DK])) * DK ** (-0.5), 2, axis=1)
    key_unit = jnp.repeat(unit_rows(jax.nn.silu(grouped[:, :, DK : 2 * DK])), 2, axis=1)
    value_all = jax.nn.silu(grouped[:, :, 2 * DK :]).reshape(rows_here, value_here, DV)
    beta_all = jax.nn.sigmoid(beta_logits)
    local_out, read_rows, transition, offset_state = jax.vmap(block_terms)(
        to_blocks(query_unit, half_rows),
        to_blocks(key_unit, half_rows),
        to_blocks(value_all, half_rows),
        to_blocks(beta_all[:, :, None], half_rows)[:, :, 0],
        to_blocks(log_decay[:, :, None], half_rows)[:, :, 0],
    )
    transition = transition.reshape(value_here, 2, DK, DK)
    offset_state = offset_state.reshape(value_here, 2, DK, DV)
    early_map, late_map = (transition[:, 0], transition[:, 1])
    early_offset, late_offset = (offset_state[:, 0], offset_state[:, 1])
    last_rank = ctx_count - 1
    zero_states = jnp.zeros_like(early_offset)

    def early_turn(number, incoming):
        return passed_along(
            apply_map(early_map, early_offset, incoming).astype(jnp.bfloat16), "ctx", 1
        ).astype(jnp.float32)

    early_in = lax.fori_loop(0, ctx_count - 1, early_turn, zero_states)
    early_end = apply_map(early_map, early_offset, early_in)
    late_start = jnp.where(ctx_rank == last_rank, early_end, zero_states)

    def late_turn(number, incoming):
        moved = passed_along(
            apply_map(late_map, late_offset, incoming).astype(jnp.bfloat16), "ctx", -1
        ).astype(jnp.float32)
        return jnp.where(ctx_rank == last_rank, early_end, moved)

    late_in = lax.fori_loop(0, ctx_count - 1, late_turn, late_start)
    states_in = jnp.stack([early_in, late_in], axis=1)
    block_out = local_out.reshape(value_here, 2, half_rows, DV) + jnp.einsum(
        "hbck,hbkv->hbcv",
        read_rows.reshape(value_here, 2, half_rows, DK),
        states_in,
        precision=TOP_PRECISION,
    )
    token_out = block_out.transpose(1, 2, 0, 3).reshape(rows_here, value_here, DV)
    out_square = jnp.mean(token_out * token_out, axis=2, keepdims=True)
    delta_out = (token_out * lax.rsqrt(out_square + EPSILON) * delta_gain).astype(jnp.bfloat16)
    return (new_residual, delta_out.reshape(rows_here, value_here * DV))


KEY_HEADS = 16
IN_VMEM = pl.BlockSpec(memory_space=pltpu.VMEM)
IN_HBM = pl.BlockSpec(memory_space=pl.ANY)
MIB = 2**20
LANES = 128
GROUPS = ((0,), (2,), (1,), (3,))


def owners_fit(mesh):
    shards = mesh.shape["head"] * mesh.shape["sub"]
    key_here = KEY_HEADS // shards
    return mesh.shape["head"] == 2 and mesh.shape["sub"] == 2 and key_here == mesh.shape["ctx"]


def in_vmem(array):
    return pltpu.with_memory_space_constraint(array, pltpu.VMEM)


def in_hbm(array):
    return pltpu.with_memory_space_constraint(array, pltpu.HBM)


def vmem_call(kernel, outs, operands, scratch=(), limit=16, aliases=None, last=False, cost=None):
    make = jax.ShapeDtypeStruct if last else pltpu.VMEM
    return pl.pallas_call(
        kernel,
        out_shape=[make(shape, dtype) for shape, dtype in outs],
        in_specs=[IN_VMEM] * len(operands),
        out_specs=[IN_VMEM] * len(outs),
        scratch_shapes=list(scratch),
        input_output_aliases=aliases or {},
        cost_estimate=cost,
        compiler_params=pltpu.CompilerParams(vmem_limit_bytes=limit * MIB),
    )(*[in_vmem(operand) for operand in operands])


def swapped(value, axis, mask=1):
    return lax.ppermute(value, axis, [(i, i ^ mask) for i in range(lax.axis_size(axis))])


def dot(left, right, dims=((1,), (0,))):
    return lax.dot_general(left, right, (dims, ((), ())), preferred_element_type=jnp.float32)


def halves(value):
    high = value.astype(jnp.bfloat16)
    return high, (value - high.astype(jnp.float32)).astype(jnp.bfloat16)


def sigmoid(value):
    return 1.0 / (1.0 + jnp.exp(-value))


def silu(value):
    return value / (1.0 + jnp.exp(-value))


def piece_kernel(kv_ref, piece_ref, sem):
    start = (lax.axis_index("head") * 2 + lax.axis_index("sub")) * HD
    copy = pltpu.make_async_copy(kv_ref.at[:, pl.ds(pl.multiple_of(start, HD), HD)], piece_ref, sem)
    copy.start()
    copy.wait()


def fetch_kernel(*refs):
    count = len(refs) // 2
    copies = [
        pltpu.make_async_copy(refs[n], refs[count + n], refs[-1].at[n]) for n in range(count)
    ]
    for copy in copies:
        copy.start()
    for copy in copies:
        copy.wait()


def fetched(*arrays):
    moved = sum(array.size * array.dtype.itemsize for array in arrays)
    return pl.pallas_call(
        fetch_kernel,
        out_shape=[pltpu.VMEM(array.shape, array.dtype) for array in arrays],
        in_specs=[IN_HBM] * len(arrays),
        out_specs=[IN_VMEM] * len(arrays),
        scratch_shapes=[pltpu.SemaphoreType.DMA((len(arrays),))],
        compiler_params=pltpu.CompilerParams(vmem_limit_bytes=4 * MIB),
        cost_estimate=pl.CostEstimate(flops=0, bytes_accessed=moved, transcendentals=0),
    )(*[in_hbm(array) for array in arrays])


def attend(query_ref, gate_ref, keys, values, rows, key_total, visible):
    count = query_ref.shape[1] // HD
    columns = [slice(head * HD, (head + 1) * HD) for head in range(count)]
    size = rows.stop - rows.start
    queries = jnp.concatenate([query_ref[rows, part] for part in columns], axis=0)
    gates = [sigmoid(gate_ref[rows, part].astype(jnp.float32)) for part in columns]
    scores = dot(queries, keys[0:key_total], ((1,), (1,))) * HD ** (-0.5)
    scores = jnp.where(jnp.concatenate([visible] * count, axis=0), scores, NEGATIVE)
    weights = jnp.exp(scores - jnp.max(scores, axis=1, keepdims=True))
    total = jnp.sum(weights, axis=1, keepdims=True)
    gathered = dot(weights.astype(jnp.bfloat16), values[0:key_total]) / total
    gated = [gathered[head * size : (head + 1) * size] * gates[head] for head in range(count)]
    return jnp.concatenate(gated, axis=1).astype(jnp.bfloat16)


def attention_kernel(
    query_ref, gate_ref, kv_ref, mine1, mine2, mine3, twin1, twin2, twin3, weight_ref, residual_ref,
    heads_ref, send_ref, keys, values, sums,
):
    half = query_ref.shape[0] // 2
    ctx_rank, head_rank, sub_rank = (lax.axis_index(name) for name in ("ctx", "head", "sub"))
    count = 4
    own_start = pl.multiple_of(head_rank * 2 * HD, 2 * HD)

    def put(target, mask, part):
        target[mask * half : (mask + 1) * half] = part[0:half]
        target[(count + mask) * half : (count + mask + 1) * half] = part[half : 2 * half]

    put(keys, 0, kv_ref[:, pl.ds(own_start, HD)])
    put(values, 0, kv_ref[:, pl.ds(own_start + HD, HD)])

    @pl.when(sub_rank == 0)
    def _():
        for mask, (mine, twin) in enumerate(((mine1, twin1), (mine2, twin2), (mine3, twin3)), 1):
            put(keys, mask, mine[...])
            put(values, mask, twin[...])

    @pl.when(sub_rank != 0)
    def _():
        for mask, (mine, twin) in enumerate(((mine1, twin1), (mine2, twin2), (mine3, twin3)), 1):
            put(keys, mask, twin[...])
            put(values, mask, mine[...])

    shift = half.bit_length() - 1
    row = lax.broadcasted_iota(jnp.int32, (half, 1), 0)
    column = lax.broadcasted_iota(jnp.int32, (1, 2 * count * half), 1)
    device = jnp.bitwise_xor(ctx_rank, (column >> shift) & (count - 1))
    block = jnp.where(column < count * half, device, 2 * count - 1 - device)
    key_place = block * half + (column & (half - 1))
    for part, block_here in enumerate((ctx_rank, 2 * count - 1 - ctx_rank)):
        rows = slice(part * half, (part + 1) * half)
        key_total = (part + 1) * count * half
        visible = row + block_here * half >= key_place[:, :key_total]
        heads_ref[rows] = attend(query_ref, gate_ref, keys, values, rows, key_total, visible)
    mid = send_ref.shape[1]
    width = residual_ref.shape[1]
    sums[...] = dot(heads_ref[...], weight_ref[:, pl.ds(pl.multiple_of((1 - sub_rank) * mid, mid), mid)])

    @pl.when(sub_rank != head_rank)
    def _():
        sums[:, pl.ds(pl.multiple_of(sub_rank * width, width), width)] += residual_ref[...].astype(jnp.float32)

    send_ref[...] = sums[...].astype(jnp.bfloat16)


def keep_kernel(heads_ref, weight_ref, residual_ref, keep_ref):
    head_rank, sub_rank = lax.axis_index("head"), lax.axis_index("sub")
    mid = keep_ref.shape[1]
    width = residual_ref.shape[1]
    keep_ref[...] = dot(heads_ref[...], weight_ref[:, pl.ds(pl.multiple_of(sub_rank * mid, mid), mid)])

    @pl.when(sub_rank == head_rank)
    def _():
        keep_ref[:, pl.ds(pl.multiple_of(sub_rank * width, width), width)] += residual_ref[...].astype(jnp.float32)


def chip_sum_kernel(keep_ref, came_ref, sum_ref, send_ref):
    total = keep_ref[...] + came_ref[...].astype(jnp.float32)
    sum_ref[...] = total
    send_ref[...] = total.astype(jnp.bfloat16)


def hidden_kernel(keep_ref, came_ref, hidden_ref):
    hidden_ref[...] = (keep_ref[...] + came_ref[...].astype(jnp.float32)).astype(jnp.bfloat16)


def half_of(ref, own):
    sub_rank = lax.axis_index("sub")
    mid = ref.shape[-1] // 2
    return pl.ds(pl.multiple_of((sub_rank if own else 1 - sub_rank) * mid, mid), mid)


def own_half_kernel(own_ref, gain_ref, weight_ref, beta_ref, mixed_ref, logit_ref, square_ref):
    mid = own_ref.shape[1]
    own = own_ref[...].astype(jnp.float32)
    columns = half_of(gain_ref, True)
    scaled = (own * gain_ref[:, columns]).astype(jnp.bfloat16)
    square_ref[...] = jnp.broadcast_to(jnp.sum(own * own, axis=1, keepdims=True), square_ref.shape)
    logit_ref[...] = dot(beta_ref[:, columns], scaled, ((1,), (1,)))
    rows = pl.ds(pl.multiple_of(lax.axis_index("sub") * mid, mid), mid)
    mixed_ref[...] = dot(scaled, weight_ref[rows, :])


def twin_half_kernel(
    twin_ref, gain_ref, beta_ref, decay_ref, logit_ref, square_ref, weight_ref, mixed_ref,
    scaled_ref, scale_ref, extra_ref, payload_ref, small,
):
    twin = twin_ref[...].astype(jnp.float32)
    columns = half_of(gain_ref, False)
    scaled_ref[...] = (twin * gain_ref[:, columns]).astype(jnp.bfloat16)
    squares = square_ref[...] + jnp.sum(twin * twin, axis=1, keepdims=True)
    scale = lax.rsqrt(squares / gain_ref.shape[1] + EPSILON)
    scale_ref[...] = scale
    values = decay_ref.shape[0]
    logits = logit_ref[...] + dot(beta_ref[:, columns], scaled_ref[...], ((1,), (1,)))
    extra_ref[0:values] = decay_ref[...]
    extra_ref[values : 2 * values] = sigmoid(logits * jnp.transpose(scale)[0:1])
    payload_kernel(2, scaled_ref, scale_ref, weight_ref, mixed_ref, extra_ref, payload_ref, small)


def residual_kernel(own_ref, twin_ref, residual_ref):
    head_rank, sub_rank = lax.axis_index("head"), lax.axis_index("sub")
    width = residual_ref.shape[1]
    columns = pl.ds(pl.multiple_of(sub_rank * width, width), width)

    @pl.when(sub_rank == head_rank)
    def _():
        residual_ref[...] = own_ref[:, columns]

    @pl.when(sub_rank != head_rank)
    def _():
        residual_ref[...] = twin_ref[:, columns]


def payload_kernel(mask, scaled_ref, scale_ref, weight_ref, mixed_ref, extra_ref, payload_ref, small):
    rows, mid = scaled_ref.shape
    group = 2 * DK + 2 * DV
    target = jnp.bitwise_xor(lax.axis_index("ctx"), mask)
    columns = pl.ds(pl.multiple_of(target * group, group), group)
    weight_rows = pl.ds(pl.multiple_of((1 - lax.axis_index("sub")) * mid, mid), mid)
    mixed = mixed_ref[:, columns] + dot(scaled_ref[...], weight_ref[weight_rows, columns])
    mixed = silu(mixed * scale_ref[:, 0:1])
    query, key = mixed[:, :DK], mixed[:, DK : 2 * DK]
    payload_ref[0:rows] = unit_rows(key).astype(jnp.bfloat16)
    values = extra_ref.shape[0] // 2
    small[...] = jnp.zeros_like(small)
    for place, base in ((0, 0), (4, values)):
        full = extra_ref[pl.ds(base + 2 * target, 2), :]
        high = full.astype(jnp.bfloat16).astype(jnp.float32)
        small[place : place + 2] = high
        small[place + 2 : place + 4] = full - high
    payload_ref[rows : rows + 16] = small[...].astype(jnp.bfloat16)
    rest = (unit_rows(query) * DK ** (-0.5), mixed[:, 2 * DK : 2 * DK + DV], mixed[:, 2 * DK + DV :])
    for number, part in enumerate(rest, 1):
        payload_ref[number * rows + 16 : (number + 1) * rows + 16] = part.astype(jnp.bfloat16)


def joined(left, right):
    (left_high, left_low), (right_high, right_low) = left, right
    return dot(
        jnp.concatenate([left_high, left_high, left_low], axis=1),
        jnp.concatenate([right_high, right_low, right_high], axis=0),
    )


def unit_lower_inverses(stricts, row, column):
    inner = (row >> 3) == (column >> 3)
    identity = jnp.where(row == column, 1.0, 0.0)
    number = range(len(stricts))
    smalls = [jnp.where(inner, strict, 0.0) for strict in stricts]
    rests = [halves(jnp.where(inner, 0.0, strict)) for strict in stricts]
    small = [halves(part) for part in smalls]
    inverses = [identity - part for part in smalls]
    split = [halves(inverse) for inverse in inverses]
    seconds = [halves(joined(part, part)) for part in small]
    fourths = [halves(joined(second, second)) for second in seconds]
    inverses = [inverses[n] + joined(split[n], seconds[n]) for n in number]
    split = [halves(inverse) for inverse in inverses]
    inverses = [inverses[n] + joined(split[n], fourths[n]) for n in number]
    split = [halves(inverse) for inverse in inverses]
    steps = [halves(joined(split[n], rests[n])) for n in number]
    doubles = [halves(joined(step, step)) for step in steps]
    results = [inverses[n] - joined(steps[n], split[n]) for n in number]
    quads = [halves(joined(double, double)) for double in doubles]
    results = [results[n] + joined(doubles[n], halves(results[n])) for n in number]
    return [results[n] + joined(quads[n], halves(results[n])) for n in number]


def key_terms(chunks):
    rows = chunks[0][0].shape[0]
    half = rows // 2
    shift = half.bit_length() - 1
    row = lax.broadcasted_iota(jnp.int32, (rows, 1), 0)
    column = lax.broadcasted_iota(jnp.int32, (1, rows), 1)
    together = (row >> shift) == (column >> shift)
    inclusive = together & (row >= column)
    strictly = together & (row > column)
    early = column < half
    below = jnp.where(inclusive, 1.0, 0.0).astype(jnp.bfloat16)
    diagonal = jnp.where(row == column, 1.0, 0.0).astype(jnp.bfloat16)
    below, diagonal = (jnp.concatenate([left, left], axis=1) for left in (below, diagonal))
    items = [(chunk, head) for chunk in range(len(chunks)) for head in range(2)]
    keys = [key for key, _ in chunks]
    extras = [extra.astype(jnp.float32) for _, extra in chunks]

    def spread(left, chunk, place):
        lanes = [
            jnp.broadcast_to(extras[chunk][n : n + 1], (rows, rows)).astype(jnp.bfloat16) for n in (place, place + 2)
        ]
        return dot(left, jnp.concatenate(lanes, axis=1), ((1,), (1,)))

    sums = [dot(extra, below[:, :rows], ((1,), (1,))) for _, extra in chunks]
    key_grams = [dot(key, key, ((1,), (1,))) for key in keys]
    totals = {item: spread(below, *item) for item in items}
    betas = {(chunk, head): spread(diagonal, chunk, head + 4) for chunk, head in items}
    total_rows = {(c, h): sums[c][h : h + 1] + sums[c][h + 2 : h + 3] for c, h in items}
    decays = {item: jnp.exp(jnp.where(inclusive, totals[item] - total_rows[item], NEGATIVE)) for item in items}
    stricts = [jnp.where(strictly, betas[item] * key_grams[item[0]] * decays[item], 0.0) for item in items]
    wide = [key.astype(jnp.float32) for key in keys]
    turned = [jnp.transpose(key) for key in wide]
    growths = {item: jnp.exp(totals[item]) for item in items}
    inverses = [halves(inverse) for inverse in unit_lower_inverses(stricts, row, column)]
    terms = []
    for item, (high, low) in zip(items, inverses):
        total = total_rows[item]
        end = jnp.where(early, total[:, half - 1 : half], total[:, rows - 1 : rows])
        carried = turned[item[0]] * jnp.exp(end - total)
        carried = [jnp.where(early, carried, 0.0), jnp.where(early, 0.0, carried)]
        weighted = (betas[item] * growths[item] * wide[item[0]]).astype(jnp.bfloat16)
        lefts = jnp.concatenate(carried, axis=0).astype(jnp.bfloat16)
        terms.append((betas[item], decays[item], growths[item], weighted, lefts, high, low, jnp.exp(end)))
    return terms


def finish_terms(source, query, key, values, terms, offset_ref, linear_ref, local_ref, growth_ref):
    rows = query.shape[0]
    half = rows // 2
    query_gram = dot(query, key, ((1,), (1,)))
    solved = []
    for value, (beta, _, _, weighted, _, high, low, _) in zip(values, terms):
        right = jnp.concatenate([(beta * value.astype(jnp.float32)).astype(jnp.bfloat16), weighted], axis=1)
        solved.append((dot(high, right) + dot(low, right)).astype(jnp.bfloat16))
    moved = []
    for part, (_, decay, _, _, lefts, _, _, _) in zip(solved, terms):
        moved.append(dot(jnp.concatenate([lefts, (query_gram * decay).astype(jnp.bfloat16)], axis=0), part))
    for head, (part, (_, _, growth, _, _, _, _, ends)) in enumerate(zip(moved, terms)):
        attended = part[2 * DK :]
        local_ref[source, head] = attended[:, :DV]
        reads = (growth * query.astype(jnp.float32) - attended[:, DV:]).astype(jnp.bfloat16)
        for block in range(2):
            state = part[block * DK : (block + 1) * DK]
            offset_ref[source, head, block] = state[:, :DV]
            linear_ref[source, head, block, 0:DK] = state[:, DV:].astype(jnp.bfloat16)
            linear_ref[source, head, block, DK : DK + half] = reads[block * half : (block + 1) * half]
            last = (block + 1) * half - 1
            growth_ref[source, head, block] = jnp.broadcast_to(ends[:, last : last + 1], growth_ref.shape[3:])


def source_of(mask):
    return jnp.bitwise_xor(lax.axis_index("ctx"), mask)


def block_kernel(masks, *refs):
    payload_refs, outs = refs[: len(masks)], refs[-4:]
    rows = (payload_refs[0].shape[0] - 16) // 4
    keys = [ref[0:rows] for ref in payload_refs]
    terms = key_terms([(key, ref[rows : rows + 16]) for key, ref in zip(keys, payload_refs)])
    for number, (mask, ref) in enumerate(zip(masks, payload_refs)):
        query, *values = (ref[n * rows + 16 : (n + 1) * rows + 16] for n in (1, 2, 3))
        finish_terms(source_of(mask), query, keys[number], values, terms[2 * number : 2 * number + 2], *outs)


def scan_kernel(offset_ref, linear_ref, local_ref, growth_ref, gain_ref, own_ref, back1, back2, back3, outs):
    count = offset_ref.shape[0]
    half = local_ref.shape[2] // 2
    rank = lax.axis_index("ctx")
    states = [None, None]
    for number in range(2 * count):
        source, block = (number, 0) if number < count else (2 * count - 1 - number, 1)
        block_rows = slice(block * half, (block + 1) * half)
        for head in range(2):
            out = local_ref[source, head, block_rows]
            state = offset_ref[source, head, block]
            if states[head] is not None:
                moved = dot(linear_ref[source, head, block], states[head].astype(jnp.bfloat16))
                out = out + moved[DK:]
                state = state - moved[:DK] + growth_ref[source, head, block, 0:1] * states[head]
            states[head] = state
            scale = lax.rsqrt(jnp.mean(out * out, axis=1, keepdims=True) + EPSILON)
            outs[source, block_rows, head * DV : (head + 1) * DV] = (out * scale * gain_ref[...]).astype(jnp.bfloat16)
    own_ref[...] = outs[rank]
    for mask, back in enumerate((back1, back2, back3), 1):
        back[...] = outs[jnp.bitwise_xor(rank, mask)]


def place_kernel(own_ref, back3, back1, back2, out_ref, sems):
    width = own_ref.shape[1]
    rank = lax.axis_index("ctx")
    copies = []
    for mask, back in enumerate((own_ref, back1, back2, back3)):
        columns = pl.ds(pl.multiple_of(jnp.bitwise_xor(rank, mask) * width, width), width)
        copies.append(pltpu.make_async_copy(back, out_ref.at[:, columns], sems.at[mask]))
        copies[-1].start()
    for copy in copies:
        copy.wait()


def owner_local(
    att_query,
    att_gate,
    att_kv,
    residual,
    out_weight,
    norm_gain,
    in_weight,
    beta_weight,
    log_decay,
    delta_gain,
):
    bf16, f32 = jnp.bfloat16, jnp.float32
    rows, head_columns = att_query.shape
    model = out_weight.shape[1]
    half_model = model // 2
    value_here = log_decay.shape[1]
    masks = (2, 3, 1)
    piece = pl.pallas_call(
        piece_kernel,
        out_shape=pltpu.VMEM((rows, HD), bf16),
        in_specs=[IN_HBM],
        out_specs=IN_VMEM,
        scratch_shapes=[pltpu.SemaphoreType.DMA],
        compiler_params=pltpu.CompilerParams(vmem_limit_bytes=4 * MIB),
    )(in_hbm(att_kv))
    mine = {mask: swapped(piece, "ctx", mask) for mask in masks[::-1]}
    piece, *late = lax.optimization_barrier((piece, att_query, att_gate, att_kv, out_weight, residual))
    late = fetched(*late)
    mine[3], (att_query, att_gate, att_kv, out_weight, residual) = lax.optimization_barrier((mine[3], late))
    twin = {3: swapped(mine[3], "sub"), 1: swapped(mine[1], "sub")}
    mine[2] = lax.optimization_barrier((mine[2], twin[3]))[0]
    twin[2] = swapped(mine[2], "sub")
    heads, send = vmem_call(
        attention_kernel,
        [((rows, head_columns), bf16), ((rows, half_model), bf16)],
        [att_query, att_gate, att_kv, mine[1], mine[2], mine[3], twin[1], twin[2], twin[3], out_weight, residual],
        [
            pltpu.VMEM((4 * rows, HD), bf16),
            pltpu.VMEM((4 * rows, HD), bf16),
            pltpu.VMEM((rows, half_model), f32),
        ],
    )
    came = swapped(send, "sub")
    keep = vmem_call(keep_kernel, [((rows, half_model), f32)], [heads, out_weight, residual])[0]
    came, keep = lax.optimization_barrier((came, keep))
    chip_sum, send = vmem_call(
        chip_sum_kernel, [((rows, half_model), f32), ((rows, half_model), bf16)], [keep, came]
    )
    came = swapped(send, "head")
    send, *late = lax.optimization_barrier((send, in_weight, norm_gain[None, :], beta_weight.T, log_decay.T))
    late = fetched(*late)
    came, (in_weight, norm_gain, beta_weight, log_decay) = lax.optimization_barrier((came, late))
    hidden = vmem_call(hidden_kernel, [((rows, half_model), bf16)], [chip_sum, came])[0]
    twin_hidden = swapped(hidden, "sub")
    sums = vmem_call(
        own_half_kernel,
        [((rows, in_weight.shape[1]), f32), ((value_here, rows), f32), ((rows, LANES), f32)],
        [hidden, norm_gain, in_weight, beta_weight],
    )
    twin_hidden, (mixed, logits, squares) = lax.optimization_barrier((twin_hidden, sums))
    payload_shape = ((4 * rows + 16, LANES), bf16)
    payloads = {}
    scaled, scale, extra, payloads[2] = vmem_call(
        twin_half_kernel,
        [((rows, half_model), bf16), ((rows, LANES), f32), ((2 * value_here, rows), f32), payload_shape],
        [twin_hidden, norm_gain, beta_weight, log_decay, logits, squares, in_weight, mixed],
        [pltpu.VMEM((16, LANES), f32)],
    )
    for mask in (3, 1, 0):
        payloads[mask] = vmem_call(
            functools.partial(payload_kernel, mask),
            [payload_shape],
            [scaled, scale, in_weight, mixed, extra],
            [pltpu.VMEM((16, LANES), f32)],
        )[0]
    new_residual = vmem_call(residual_kernel, [(residual.shape, bf16)], [hidden, twin_hidden], last=True)[0]
    came = {mask: swapped(payloads[mask], "ctx", mask) for mask in masks}
    came[0] = payloads[0]
    half = rows // 2
    terms_shapes = [
        ((4, 2, 2, DK, DV), f32),
        ((4, 2, 2, DK + half, DK), bf16),
        ((4, 2, rows, DV), f32),
        ((4, 2, 2, 8, LANES), f32),
    ]
    terms = []
    for group in GROUPS:
        terms = vmem_call(
            functools.partial(block_kernel, group),
            terms_shapes,
            [*(came[mask] for mask in group), *terms],
            aliases={len(group) + i: i for i in range(4)} if terms else None,
        )
    own, *backs = vmem_call(
        scan_kernel,
        [((rows, 2 * DV), bf16)] * 4,
        [*terms, delta_gain[None, :]],
        [pltpu.VMEM((4, rows, 2 * DV), bf16)],
    )
    backs = {mask: swapped(backs[mask - 1], "ctx", mask) for mask in masks}
    delta_out = pl.pallas_call(
        place_kernel,
        out_shape=jax.ShapeDtypeStruct((rows, value_here * DV), bf16),
        in_specs=[IN_VMEM] * 4,
        out_specs=IN_HBM,
        scratch_shapes=[pltpu.SemaphoreType.DMA((4,))],
        compiler_params=pltpu.CompilerParams(vmem_limit_bytes=4 * MIB),
    )(*[in_vmem(back) for back in (own, backs[3], backs[1], backs[2])])
    return (new_residual, delta_out)


def solution(mesh):
    local = owner_local if owners_fit(mesh) else hop_local
    return jax.shard_map(
        local,
        mesh=mesh,
        in_specs=(
            P(("groups", "ctx"), ("head", "sub")),
            P(("groups", "ctx"), ("head", "sub")),
            P(("groups", "ctx"), None),
            P(("groups", "ctx"), ("head", "sub")),
            P(("head", "sub"), None),
            P(),
            P(None, ("head", "sub")),
            P(None, ("head", "sub")),
            P(("groups", "ctx"), ("head", "sub")),
            P(),
        ),
        out_specs=(P(("groups", "ctx"), ("head", "sub")), P(("groups", "ctx"), ("head", "sub"))),
        check_vma=False,
    )
```

```python
import functools

import jax
import jax.numpy as jnp
from jax import lax
from jax.experimental import pallas as pl
from jax.experimental.pallas import tpu as pltpu
from jax.sharding import PartitionSpec as P

HEADS = 16
KV_HEADS = 2
HD = 256
DK = 128
DV = 128


TOP_PRECISION = lax.Precision.HIGHEST
EPSILON = 1e-06
NEGATIVE = -1e30


def passed_along(value, axis, steps):
    count = lax.axis_size(axis)
    initial, last = (max(0, -steps), min(count, count - steps))
    return lax.ppermute(value, axis, [(source, source + steps) for source in range(initial, last)])


def stored_positions(first_row, row_total, half_rows, ctx_count):
    row_index = first_row + jnp.arange(row_total, dtype=jnp.int32)
    device_of = row_index // (2 * half_rows)
    within_dev = row_index % (2 * half_rows)
    block_number = jnp.where(within_dev < half_rows, device_of, 2 * ctx_count - 1 - device_of)
    return block_number * half_rows + within_dev % half_rows


def unit_rows(matrix):
    return matrix * lax.rsqrt(jnp.sum(matrix * matrix, axis=-1, keepdims=True) + EPSILON)


def to_blocks(array, half_rows):
    heads_count = array.shape[1]
    width = array.shape[2]
    shaped = array.reshape(2, half_rows, heads_count, width).transpose(2, 0, 1, 3)
    return shaped.reshape(heads_count * 2, half_rows, width)


def block_terms(query_rows, key_rows, value_rows, beta_rows, decay_rows):
    length = query_rows.shape[0]
    cumulative = jnp.cumsum(decay_rows)
    position = jnp.arange(length)
    on_or_below = position[:, None] >= position[None, :]
    strictly_below = position[:, None] > position[None, :]
    decay_gap = cumulative[:, None] - cumulative[None, :]
    decay_grid = jnp.where(on_or_below, jnp.exp(jnp.where(on_or_below, decay_gap, 0.0)), 0.0)
    key_gram = jnp.dot(key_rows, key_rows.T, precision=TOP_PRECISION)
    system = jnp.eye(length, dtype=jnp.float32) + jnp.where(
        strictly_below, beta_rows[:, None] * key_gram * decay_grid, 0.0
    )
    growth = jnp.exp(cumulative)
    right_side = beta_rows[:, None] * jnp.concatenate(
        [value_rows, growth[:, None] * key_rows], axis=1
    )
    solved = jax.scipy.linalg.solve_triangular(system, right_side, lower=True, unit_diagonal=True)
    update_rows = solved[:, : value_rows.shape[1]]
    weight_rows = solved[:, value_rows.shape[1] :]
    attend_grid = jnp.where(
        on_or_below, jnp.dot(query_rows, key_rows.T, precision=TOP_PRECISION) * decay_grid, 0.0
    )
    local_out = jnp.dot(attend_grid, update_rows, precision=TOP_PRECISION)
    read_rows = growth[:, None] * query_rows - jnp.dot(
        attend_grid, weight_rows, precision=TOP_PRECISION
    )
    carried_keys = jnp.exp(cumulative[-1] - cumulative)[:, None] * key_rows
    identity_map = jnp.eye(key_rows.shape[1], dtype=jnp.float32)
    transition = jnp.exp(cumulative[-1]) * identity_map - jnp.dot(
        carried_keys.T, weight_rows, precision=TOP_PRECISION
    )
    offset_state = jnp.dot(carried_keys.T, update_rows, precision=TOP_PRECISION)
    return (local_out, read_rows, transition, offset_state)


def apply_map(matrix_maps, offsets, states):
    return jnp.einsum("hij,hjk->hik", matrix_maps, states, precision=TOP_PRECISION) + offsets


def attend_rows(running, query_block, key_block, value_block, visible, score_scale):
    run_max, run_sum, run_acc = running
    scores = (
        jnp.einsum("rhd,kd->rhk", query_block, key_block, preferred_element_type=jnp.float32)
        * score_scale
    )
    if visible is not None:
        scores = jnp.where(visible[:, None, :], scores, NEGATIVE)
    new_max = jnp.maximum(run_max, jnp.max(scores, axis=2))
    weights = jnp.exp(scores - new_max[:, :, None])
    if visible is not None:
        weights = jnp.where(visible[:, None, :], weights, 0.0)
    rescale = jnp.exp(run_max - new_max)
    run_sum = run_sum * rescale + jnp.sum(weights, axis=2)
    added = jnp.einsum(
        "rhk,kd->rhd", weights.astype(jnp.bfloat16), value_block, preferred_element_type=jnp.float32
    )
    run_acc = run_acc * rescale[:, :, None] + added
    return (new_max, run_sum, run_acc)


def hop_local(
    att_query,
    att_gate,
    att_kv,
    residual,
    out_weight,
    norm_gain,
    in_weight,
    beta_weight,
    log_decay,
    delta_gain,
):
    ctx_count = lax.axis_size("ctx")
    ctx_rank = lax.axis_index("ctx")
    shard_rank = lax.axis_index(("head", "sub"))
    rows_here = att_query.shape[0]
    half_rows = rows_here // 2
    heads_here = att_query.shape[1] // HD
    kv_number = shard_rank * heads_here // (HEADS // KV_HEADS)
    key_local = lax.dynamic_slice_in_dim(att_kv, kv_number * 2 * HD, HD, 1)
    value_local = lax.dynamic_slice_in_dim(att_kv, kv_number * 2 * HD + HD, HD, 1)
    query_heads = att_query.reshape(rows_here, heads_here, HD)
    late_queries = query_heads[half_rows:]
    query_places = stored_positions(ctx_rank * rows_here, rows_here, half_rows, ctx_count)
    same_visible = query_places[:, None] >= query_places[None, :]
    score_scale = HD ** (-0.5)

    def earlier_shard(running, key_shard, value_shard):
        return attend_rows(
            running, query_heads, key_shard[:half_rows], value_shard[:half_rows], None, score_scale
        )

    def same_shard(running, key_shard, value_shard):
        return attend_rows(running, query_heads, key_shard, value_shard, same_visible, score_scale)

    def later_shard(running, key_shard, value_shard):
        late_part = tuple((member[half_rows:] for member in running))
        renewed = attend_rows(late_part, late_queries, key_shard, value_shard, None, score_scale)
        return tuple(
            (
                jnp.concatenate([member[:half_rows], latest], axis=0)
                for member, latest in zip(running, renewed)
            )
        )

    start_running = (
        jnp.full((rows_here, heads_here), NEGATIVE, jnp.float32),
        jnp.zeros((rows_here, heads_here), jnp.float32),
        jnp.zeros((rows_here, heads_here, HD), jnp.float32),
    )
    key_block = lax.all_gather(key_local, "ctx", axis=0, tiled=True)
    value_block = lax.all_gather(value_local, "ctx", axis=0, tiled=True)
    piece_rows = key_block.shape[0]

    def one_shard(number, current):
        offset = number * rows_here
        key_shard = lax.dynamic_slice_in_dim(key_block, offset, rows_here, 0)
        value_shard = lax.dynamic_slice_in_dim(value_block, offset, rows_here, 0)
        shard_number = offset // rows_here
        branch = jnp.clip(shard_number - ctx_rank, -1, 1) + 1
        return lax.switch(
            branch, [earlier_shard, same_shard, later_shard], current, key_shard, value_shard
        )

    run_max, run_sum, run_acc = lax.fori_loop(0, piece_rows // rows_here, one_shard, start_running)
    gate_heads = jax.nn.sigmoid(att_gate.reshape(rows_here, heads_here, HD).astype(jnp.float32))
    att_heads = (
        (run_acc / run_sum[:, :, None] * gate_heads)
        .astype(jnp.bfloat16)
        .reshape(rows_here, heads_here * HD)
    )
    partial_term = jnp.dot(att_heads, out_weight, preferred_element_type=jnp.float32)
    col_width = residual.shape[1]
    col_start = shard_rank * col_width
    placed = lax.dynamic_slice_in_dim(partial_term, col_start, col_width, 1) + residual.astype(
        jnp.float32
    )
    partial_term = lax.dynamic_update_slice_in_dim(partial_term, placed, col_start, 1)
    hidden = lax.psum(partial_term.astype(jnp.bfloat16), ("head", "sub")).astype(jnp.float32)
    mean_square = jnp.mean(hidden * hidden, axis=1, keepdims=True)
    normed = (hidden * lax.rsqrt(mean_square + EPSILON) * norm_gain).astype(jnp.bfloat16)
    new_residual = lax.dynamic_slice_in_dim(hidden, col_start, col_width, 1).astype(jnp.bfloat16)
    mixed_cols = jnp.dot(normed, in_weight, preferred_element_type=jnp.float32)
    beta_logits = jnp.dot(normed, beta_weight, preferred_element_type=jnp.float32)
    key_here = in_weight.shape[1] // (2 * DK + 2 * DV)
    value_here = 2 * key_here
    grouped = mixed_cols.reshape(rows_here, key_here, 2 * DK + 2 * DV)
    query_unit = jnp.repeat(unit_rows(jax.nn.silu(grouped[:, :, :DK])) * DK ** (-0.5), 2, axis=1)
    key_unit = jnp.repeat(unit_rows(jax.nn.silu(grouped[:, :, DK : 2 * DK])), 2, axis=1)
    value_all = jax.nn.silu(grouped[:, :, 2 * DK :]).reshape(rows_here, value_here, DV)
    beta_all = jax.nn.sigmoid(beta_logits)
    local_out, read_rows, transition, offset_state = jax.vmap(block_terms)(
        to_blocks(query_unit, half_rows),
        to_blocks(key_unit, half_rows),
        to_blocks(value_all, half_rows),
        to_blocks(beta_all[:, :, None], half_rows)[:, :, 0],
        to_blocks(log_decay[:, :, None], half_rows)[:, :, 0],
    )
    transition = transition.reshape(value_here, 2, DK, DK)
    offset_state = offset_state.reshape(value_here, 2, DK, DV)
    early_map, late_map = (transition[:, 0], transition[:, 1])
    early_offset, late_offset = (offset_state[:, 0], offset_state[:, 1])
    last_rank = ctx_count - 1
    zero_states = jnp.zeros_like(early_offset)

    def early_turn(number, incoming):
        return passed_along(
            apply_map(early_map, early_offset, incoming).astype(jnp.bfloat16), "ctx", 1
        ).astype(jnp.float32)

    early_in = lax.fori_loop(0, ctx_count - 1, early_turn, zero_states)
    early_end = apply_map(early_map, early_offset, early_in)
    late_start = jnp.where(ctx_rank == last_rank, early_end, zero_states)

    def late_turn(number, incoming):
        moved = passed_along(
            apply_map(late_map, late_offset, incoming).astype(jnp.bfloat16), "ctx", -1
        ).astype(jnp.float32)
        return jnp.where(ctx_rank == last_rank, early_end, moved)

    late_in = lax.fori_loop(0, ctx_count - 1, late_turn, late_start)
    states_in = jnp.stack([early_in, late_in], axis=1)
    block_out = local_out.reshape(value_here, 2, half_rows, DV) + jnp.einsum(
        "hbck,hbkv->hbcv",
        read_rows.reshape(value_here, 2, half_rows, DK),
        states_in,
        precision=TOP_PRECISION,
    )
    token_out = block_out.transpose(1, 2, 0, 3).reshape(rows_here, value_here, DV)
    out_square = jnp.mean(token_out * token_out, axis=2, keepdims=True)
    delta_out = (token_out * lax.rsqrt(out_square + EPSILON) * delta_gain).astype(jnp.bfloat16)
    return (new_residual, delta_out.reshape(rows_here, value_here * DV))


KEY_HEADS = 16
IN_VMEM = pl.BlockSpec(memory_space=pltpu.VMEM)
IN_HBM = pl.BlockSpec(memory_space=pl.ANY)
MIB = 2**20
LANES = 128
GROUPS = ((0,), (2,), (1,), (3,))


def owners_fit(mesh):
    shards = mesh.shape["head"] * mesh.shape["sub"]
    key_here = KEY_HEADS // shards
    return mesh.shape["head"] == 2 and mesh.shape["sub"] == 2 and key_here == mesh.shape["ctx"]


def in_vmem(array):
    return pltpu.with_memory_space_constraint(array, pltpu.VMEM)


def in_hbm(array):
    return pltpu.with_memory_space_constraint(array, pltpu.HBM)


def vmem_call(kernel, outs, operands, scratch=(), limit=16, aliases=None, last=False, cost=None):
    make = jax.ShapeDtypeStruct if last else pltpu.VMEM
    return pl.pallas_call(
        kernel,
        out_shape=[make(shape, dtype) for shape, dtype in outs],
        in_specs=[IN_VMEM] * len(operands),
        out_specs=[IN_VMEM] * len(outs),
        scratch_shapes=list(scratch),
        input_output_aliases=aliases or {},
        cost_estimate=cost,
        compiler_params=pltpu.CompilerParams(vmem_limit_bytes=limit * MIB),
    )(*[in_vmem(operand) for operand in operands])


def swapped(value, axis, mask=1):
    return lax.ppermute(value, axis, [(i, i ^ mask) for i in range(lax.axis_size(axis))])


def dot(left, right, dims=((1,), (0,))):
    return lax.dot_general(left, right, (dims, ((), ())), preferred_element_type=jnp.float32)


def halves(value):
    high = value.astype(jnp.bfloat16)
    return high, (value - high.astype(jnp.float32)).astype(jnp.bfloat16)


def sigmoid(value):
    return 1.0 / (1.0 + jnp.exp(-value))


def silu(value):
    return value / (1.0 + jnp.exp(-value))


def piece_kernel(kv_ref, piece_ref, sem):
    start = (lax.axis_index("head") * 2 + lax.axis_index("sub")) * HD
    copy = pltpu.make_async_copy(kv_ref.at[:, pl.ds(pl.multiple_of(start, HD), HD)], piece_ref, sem)
    copy.start()
    copy.wait()


def fetch_kernel(*refs):
    count = len(refs) // 2
    copies = [
        pltpu.make_async_copy(refs[n], refs[count + n], refs[-1].at[n]) for n in range(count)
    ]
    for copy in copies:
        copy.start()
    for copy in copies:
        copy.wait()


def fetched(*arrays):
    moved = sum(array.size * array.dtype.itemsize for array in arrays)
    return pl.pallas_call(
        fetch_kernel,
        out_shape=[pltpu.VMEM(array.shape, array.dtype) for array in arrays],
        in_specs=[IN_HBM] * len(arrays),
        out_specs=[IN_VMEM] * len(arrays),
        scratch_shapes=[pltpu.SemaphoreType.DMA((len(arrays),))],
        compiler_params=pltpu.CompilerParams(vmem_limit_bytes=4 * MIB),
        cost_estimate=pl.CostEstimate(flops=0, bytes_accessed=moved, transcendentals=0),
    )(*[in_hbm(array) for array in arrays])


def attend(query_ref, gate_ref, keys, values, rows, key_total, visible):
    count = query_ref.shape[1] // HD
    columns = [slice(head * HD, (head + 1) * HD) for head in range(count)]
    size = rows.stop - rows.start
    queries = jnp.concatenate([query_ref[rows, part] for part in columns], axis=0)
    gates = [sigmoid(gate_ref[rows, part].astype(jnp.float32)) for part in columns]
    scores = dot(queries, keys[0:key_total], ((1,), (1,))) * HD ** (-0.5)
    scores = jnp.where(jnp.concatenate([visible] * count, axis=0), scores, NEGATIVE)
    weights = jnp.exp(scores - jnp.max(scores, axis=1, keepdims=True))
    total = jnp.sum(weights, axis=1, keepdims=True)
    gathered = dot(weights.astype(jnp.bfloat16), values[0:key_total]) / total
    gated = [gathered[head * size : (head + 1) * size] * gates[head] for head in range(count)]
    return jnp.concatenate(gated, axis=1).astype(jnp.bfloat16)


def attention_kernel(
    query_ref, gate_ref, kv_ref, mine1, mine2, mine3, twin1, twin2, twin3, weight_ref, residual_ref,
    heads_ref, send_ref, keys, values, sums,
):
    half = query_ref.shape[0] // 2
    ctx_rank, head_rank, sub_rank = (lax.axis_index(name) for name in ("ctx", "head", "sub"))
    count = 4
    own_start = pl.multiple_of(head_rank * 2 * HD, 2 * HD)

    def put(target, mask, part):
        target[mask * half : (mask + 1) * half] = part[0:half]
        target[(count + mask) * half : (count + mask + 1) * half] = part[half : 2 * half]

    put(keys, 0, kv_ref[:, pl.ds(own_start, HD)])
    put(values, 0, kv_ref[:, pl.ds(own_start + HD, HD)])

    @pl.when(sub_rank == 0)
    def _():
        for mask, (mine, twin) in enumerate(((mine1, twin1), (mine2, twin2), (mine3, twin3)), 1):
            put(keys, mask, mine[...])
            put(values, mask, twin[...])

    @pl.when(sub_rank != 0)
    def _():
        for mask, (mine, twin) in enumerate(((mine1, twin1), (mine2, twin2), (mine3, twin3)), 1):
            put(keys, mask, twin[...])
            put(values, mask, mine[...])

    shift = half.bit_length() - 1
    row = lax.broadcasted_iota(jnp.int32, (half, 1), 0)
    column = lax.broadcasted_iota(jnp.int32, (1, 2 * count * half), 1)
    device = jnp.bitwise_xor(ctx_rank, (column >> shift) & (count - 1))
    block = jnp.where(column < count * half, device, 2 * count - 1 - device)
    key_place = block * half + (column & (half - 1))
    for part, block_here in enumerate((ctx_rank, 2 * count - 1 - ctx_rank)):
        rows = slice(part * half, (part + 1) * half)
        key_total = (part + 1) * count * half
        visible = row + block_here * half >= key_place[:, :key_total]
        heads_ref[rows] = attend(query_ref, gate_ref, keys, values, rows, key_total, visible)
    mid = send_ref.shape[1]
    width = residual_ref.shape[1]
    sums[...] = dot(heads_ref[...], weight_ref[:, pl.ds(pl.multiple_of((1 - sub_rank) * mid, mid), mid)])

    @pl.when(sub_rank != head_rank)
    def _():
        sums[:, pl.ds(pl.multiple_of(sub_rank * width, width), width)] += residual_ref[...].astype(jnp.float32)

    send_ref[...] = sums[...].astype(jnp.bfloat16)


def keep_kernel(heads_ref, weight_ref, residual_ref, keep_ref):
    head_rank, sub_rank = lax.axis_index("head"), lax.axis_index("sub")
    mid = keep_ref.shape[1]
    width = residual_ref.shape[1]
    keep_ref[...] = dot(heads_ref[...], weight_ref[:, pl.ds(pl.multiple_of(sub_rank * mid, mid), mid)])

    @pl.when(sub_rank == head_rank)
    def _():
        keep_ref[:, pl.ds(pl.multiple_of(sub_rank * width, width), width)] += residual_ref[...].astype(jnp.float32)


def chip_sum_kernel(keep_ref, came_ref, sum_ref, send_ref):
    total = keep_ref[...] + came_ref[...].astype(jnp.float32)
    sum_ref[...] = total
    send_ref[...] = total.astype(jnp.bfloat16)


def hidden_kernel(keep_ref, came_ref, hidden_ref):
    hidden_ref[...] = (keep_ref[...] + came_ref[...].astype(jnp.float32)).astype(jnp.bfloat16)


def half_of(ref, own):
    sub_rank = lax.axis_index("sub")
    mid = ref.shape[-1] // 2
    return pl.ds(pl.multiple_of((sub_rank if own else 1 - sub_rank) * mid, mid), mid)


def own_half_kernel(own_ref, gain_ref, weight_ref, beta_ref, mixed_ref, logit_ref, square_ref):
    mid = own_ref.shape[1]
    own = own_ref[...].astype(jnp.float32)
    columns = half_of(gain_ref, True)
    scaled = (own * gain_ref[:, columns]).astype(jnp.bfloat16)
    square_ref[...] = jnp.broadcast_to(jnp.sum(own * own, axis=1, keepdims=True), square_ref.shape)
    logit_ref[...] = dot(beta_ref[:, columns], scaled, ((1,), (1,)))
    rows = pl.ds(pl.multiple_of(lax.axis_index("sub") * mid, mid), mid)
    mixed_ref[...] = dot(scaled, weight_ref[rows, :])


def twin_half_kernel(
    twin_ref, gain_ref, beta_ref, decay_ref, logit_ref, square_ref, weight_ref, mixed_ref,
    scaled_ref, scale_ref, extra_ref, payload_ref, small,
):
    twin = twin_ref[...].astype(jnp.float32)
    columns = half_of(gain_ref, False)
    scaled_ref[...] = (twin * gain_ref[:, columns]).astype(jnp.bfloat16)
    squares = square_ref[...] + jnp.sum(twin * twin, axis=1, keepdims=True)
    scale = lax.rsqrt(squares / gain_ref.shape[1] + EPSILON)
    scale_ref[...] = scale
    values = decay_ref.shape[0]
    logits = logit_ref[...] + dot(beta_ref[:, columns], scaled_ref[...], ((1,), (1,)))
    extra_ref[0:values] = decay_ref[...]
    extra_ref[values : 2 * values] = sigmoid(logits * jnp.transpose(scale)[0:1])
    payload_kernel(2, scaled_ref, scale_ref, weight_ref, mixed_ref, extra_ref, payload_ref, small)


def residual_kernel(own_ref, twin_ref, residual_ref):
    head_rank, sub_rank = lax.axis_index("head"), lax.axis_index("sub")
    width = residual_ref.shape[1]
    columns = pl.ds(pl.multiple_of(sub_rank * width, width), width)

    @pl.when(sub_rank == head_rank)
    def _():
        residual_ref[...] = own_ref[:, columns]

    @pl.when(sub_rank != head_rank)
    def _():
        residual_ref[...] = twin_ref[:, columns]


def payload_kernel(mask, scaled_ref, scale_ref, weight_ref, mixed_ref, extra_ref, payload_ref, small):
    rows, mid = scaled_ref.shape
    group = 2 * DK + 2 * DV
    target = jnp.bitwise_xor(lax.axis_index("ctx"), mask)
    columns = pl.ds(pl.multiple_of(target * group, group), group)
    weight_rows = pl.ds(pl.multiple_of((1 - lax.axis_index("sub")) * mid, mid), mid)
    mixed = mixed_ref[:, columns] + dot(scaled_ref[...], weight_ref[weight_rows, columns])
    mixed = silu(mixed * scale_ref[:, 0:1])
    query, key = mixed[:, :DK], mixed[:, DK : 2 * DK]
    payload_ref[0:rows] = unit_rows(key).astype(jnp.bfloat16)
    values = extra_ref.shape[0] // 2
    small[...] = jnp.zeros_like(small)
    for place, base in ((0, 0), (4, values)):
        full = extra_ref[pl.ds(base + 2 * target, 2), :]
        high = full.astype(jnp.bfloat16).astype(jnp.float32)
        small[place : place + 2] = high
        small[place + 2 : place + 4] = full - high
    payload_ref[rows : rows + 16] = small[...].astype(jnp.bfloat16)
    rest = (unit_rows(query) * DK ** (-0.5), mixed[:, 2 * DK : 2 * DK + DV], mixed[:, 2 * DK + DV :])
    for number, part in enumerate(rest, 1):
        payload_ref[number * rows + 16 : (number + 1) * rows + 16] = part.astype(jnp.bfloat16)


def joined(left, right):
    (left_high, left_low), (right_high, right_low) = left, right
    right_high, right_low = apart(right_high), apart(right_low)
    return dot(
        jnp.concatenate([left_high, left_high, left_low], axis=1),
        jnp.concatenate([right_high, right_low, right_high], axis=0),
    )


def apart(pair):
    first = lax.broadcasted_iota(jnp.int32, pair.shape, 1) < pair.shape[1] // 2
    zero = jnp.zeros_like(pair)
    return jnp.concatenate([jnp.where(first, pair, zero), jnp.where(first, zero, pair)], axis=0)


def unit_lower_inverses(stricts):
    half = stricts[0].shape[0]
    row = lax.broadcasted_iota(jnp.int32, (half, 1), 0)
    column = lax.broadcasted_iota(jnp.int32, (1, 2 * half), 1) & (half - 1)
    inner = (row >> 3) == (column >> 3)
    identity = jnp.where(row == column, 1.0, 0.0)
    number = range(len(stricts))
    smalls = [jnp.where(inner, strict, 0.0) for strict in stricts]
    rests = [halves(jnp.where(inner, 0.0, strict)) for strict in stricts]
    small = [halves(part) for part in smalls]
    inverses = [identity - part for part in smalls]
    split = [halves(inverse) for inverse in inverses]
    seconds = [halves(joined(part, part)) for part in small]
    fourths = [halves(joined(second, second)) for second in seconds]
    inverses = [inverses[n] + joined(split[n], seconds[n]) for n in number]
    split = [halves(inverse) for inverse in inverses]
    inverses = [inverses[n] + joined(split[n], fourths[n]) for n in number]
    split = [halves(inverse) for inverse in inverses]
    steps = [halves(joined(split[n], rests[n])) for n in number]
    doubles = [halves(joined(step, step)) for step in steps]
    results = [inverses[n] - joined(steps[n], split[n]) for n in number]
    quads = [halves(joined(double, double)) for double in doubles]
    results = [results[n] + joined(doubles[n], halves(results[n])) for n in number]
    return [results[n] + joined(quads[n], halves(results[n])) for n in number]


def key_terms(chunks):
    rows = chunks[0][0].shape[0]
    half = rows // 2
    shift = half.bit_length() - 1
    row = lax.broadcasted_iota(jnp.int32, (rows, 1), 0)
    column = lax.broadcasted_iota(jnp.int32, (1, rows), 1)
    together = (row >> shift) == (column >> shift)
    inclusive = together & (row >= column)
    strictly = together & (row > column)
    early = column < half
    below = jnp.where(inclusive, 1.0, 0.0).astype(jnp.bfloat16)
    diagonal = jnp.where(row == column, 1.0, 0.0).astype(jnp.bfloat16)
    below, diagonal = (jnp.concatenate([left, left], axis=1) for left in (below, diagonal))
    items = [(chunk, head) for chunk in range(len(chunks)) for head in range(2)]
    keys = [key for key, _ in chunks]
    extras = [extra.astype(jnp.float32) for _, extra in chunks]

    def spread(left, chunk, place):
        lanes = [
            jnp.broadcast_to(extras[chunk][n : n + 1], (rows, rows)).astype(jnp.bfloat16) for n in (place, place + 2)
        ]
        return dot(left, jnp.concatenate(lanes, axis=1), ((1,), (1,)))

    sums = [dot(extra, below[:, :rows], ((1,), (1,))) for _, extra in chunks]
    key_grams = [dot(key, key, ((1,), (1,))) for key in keys]
    totals = {item: spread(below, *item) for item in items}
    betas = {(chunk, head): spread(diagonal, chunk, head + 4) for chunk, head in items}
    total_rows = {(c, h): sums[c][h : h + 1] + sums[c][h + 2 : h + 3] for c, h in items}
    decays = {item: jnp.exp(jnp.where(inclusive, totals[item] - total_rows[item], NEGATIVE)) for item in items}
    stricts = [jnp.where(strictly, betas[item] * key_grams[item[0]] * decays[item], 0.0) for item in items]
    wide = [key.astype(jnp.float32) for key in keys]
    turned = [jnp.transpose(key) for key in wide]
    growths = {item: jnp.exp(totals[item]) for item in items}
    pairs = [strict[:half] + strict[half:] for strict in stricts]
    inverses = [[apart(part) for part in halves(inverse)] for inverse in unit_lower_inverses(pairs)]
    terms = []
    for item, (high, low) in zip(items, inverses):
        total = total_rows[item]
        end = jnp.where(early, total[:, half - 1 : half], total[:, rows - 1 : rows])
        carried = turned[item[0]] * jnp.exp(end - total)
        carried = [jnp.where(early, carried, 0.0), jnp.where(early, 0.0, carried)]
        weighted = (betas[item] * growths[item] * wide[item[0]]).astype(jnp.bfloat16)
        lefts = jnp.concatenate(carried, axis=0).astype(jnp.bfloat16)
        terms.append((betas[item], decays[item], growths[item], weighted, lefts, high, low, jnp.exp(end)))
    return terms


def finish_terms(source, query, key, values, terms, offset_ref, linear_ref, local_ref, growth_ref):
    rows = query.shape[0]
    half = rows // 2
    query_gram = dot(query, key, ((1,), (1,)))
    solved = []
    for value, (beta, _, _, weighted, _, high, low, _) in zip(values, terms):
        right = jnp.concatenate([(beta * value.astype(jnp.float32)).astype(jnp.bfloat16), weighted], axis=1)
        solved.append((dot(high, right) + dot(low, right)).astype(jnp.bfloat16))
    moved = []
    for part, (_, decay, _, _, lefts, _, _, _) in zip(solved, terms):
        moved.append(dot(jnp.concatenate([lefts, (query_gram * decay).astype(jnp.bfloat16)], axis=0), part))
    for head, (part, (_, _, growth, _, _, _, _, ends)) in enumerate(zip(moved, terms)):
        attended = part[2 * DK :]
        local_ref[source, head] = attended[:, :DV]
        reads = (growth * query.astype(jnp.float32) - attended[:, DV:]).astype(jnp.bfloat16)
        for block in range(2):
            state = part[block * DK : (block + 1) * DK]
            offset_ref[source, head, block] = state[:, :DV]
            linear_ref[source, head, block, 0:DK] = state[:, DV:].astype(jnp.bfloat16)
            linear_ref[source, head, block, DK : DK + half] = reads[block * half : (block + 1) * half]
            last = (block + 1) * half - 1
            growth_ref[source, head, block] = jnp.broadcast_to(ends[:, last : last + 1], growth_ref.shape[3:])


def source_of(mask):
    return jnp.bitwise_xor(lax.axis_index("ctx"), mask)


def block_kernel(masks, *refs):
    payload_refs, outs = refs[: len(masks)], refs[-4:]
    rows = (payload_refs[0].shape[0] - 16) // 4
    keys = [ref[0:rows] for ref in payload_refs]
    terms = key_terms([(key, ref[rows : rows + 16]) for key, ref in zip(keys, payload_refs)])
    for number, (mask, ref) in enumerate(zip(masks, payload_refs)):
        query, *values = (ref[n * rows + 16 : (n + 1) * rows + 16] for n in (1, 2, 3))
        finish_terms(source_of(mask), query, keys[number], values, terms[2 * number : 2 * number + 2], *outs)


def scan_kernel(offset_ref, linear_ref, local_ref, growth_ref, gain_ref, own_ref, back1, back2, back3, outs):
    count = offset_ref.shape[0]
    half = local_ref.shape[2] // 2
    rank = lax.axis_index("ctx")
    states = [None, None]
    for number in range(2 * count):
        source, block = (number, 0) if number < count else (2 * count - 1 - number, 1)
        block_rows = slice(block * half, (block + 1) * half)
        for head in range(2):
            out = local_ref[source, head, block_rows]
            state = offset_ref[source, head, block]
            if states[head] is not None:
                moved = dot(linear_ref[source, head, block], states[head].astype(jnp.bfloat16))
                out = out + moved[DK:]
                state = state - moved[:DK] + growth_ref[source, head, block, 0:1] * states[head]
            states[head] = state
            scale = lax.rsqrt(jnp.mean(out * out, axis=1, keepdims=True) + EPSILON)
            outs[source, block_rows, head * DV : (head + 1) * DV] = (out * scale * gain_ref[...]).astype(jnp.bfloat16)
    own_ref[...] = outs[rank]
    for mask, back in enumerate((back1, back2, back3), 1):
        back[...] = outs[jnp.bitwise_xor(rank, mask)]


def place_kernel(own_ref, back3, back1, back2, out_ref, sems):
    width = own_ref.shape[1]
    rank = lax.axis_index("ctx")
    copies = []
    for mask, back in enumerate((own_ref, back1, back2, back3)):
        columns = pl.ds(pl.multiple_of(jnp.bitwise_xor(rank, mask) * width, width), width)
        copies.append(pltpu.make_async_copy(back, out_ref.at[:, columns], sems.at[mask]))
        copies[-1].start()
    for copy in copies:
        copy.wait()


def owner_local(
    att_query,
    att_gate,
    att_kv,
    residual,
    out_weight,
    norm_gain,
    in_weight,
    beta_weight,
    log_decay,
    delta_gain,
):
    bf16, f32 = jnp.bfloat16, jnp.float32
    rows, head_columns = att_query.shape
    model = out_weight.shape[1]
    half_model = model // 2
    value_here = log_decay.shape[1]
    masks = (2, 3, 1)
    piece = pl.pallas_call(
        piece_kernel,
        out_shape=pltpu.VMEM((rows, HD), bf16),
        in_specs=[IN_HBM],
        out_specs=IN_VMEM,
        scratch_shapes=[pltpu.SemaphoreType.DMA],
        compiler_params=pltpu.CompilerParams(vmem_limit_bytes=4 * MIB),
    )(in_hbm(att_kv))
    mine = {mask: swapped(piece, "ctx", mask) for mask in masks[::-1]}
    piece, *late = lax.optimization_barrier((piece, att_query, att_gate, att_kv, out_weight, residual))
    late = fetched(*late)
    mine[3], (att_query, att_gate, att_kv, out_weight, residual) = lax.optimization_barrier((mine[3], late))
    twin = {3: swapped(mine[3], "sub"), 1: swapped(mine[1], "sub")}
    mine[2] = lax.optimization_barrier((mine[2], twin[3]))[0]
    twin[2] = swapped(mine[2], "sub")
    heads, send = vmem_call(
        attention_kernel,
        [((rows, head_columns), bf16), ((rows, half_model), bf16)],
        [att_query, att_gate, att_kv, mine[1], mine[2], mine[3], twin[1], twin[2], twin[3], out_weight, residual],
        [
            pltpu.VMEM((4 * rows, HD), bf16),
            pltpu.VMEM((4 * rows, HD), bf16),
            pltpu.VMEM((rows, half_model), f32),
        ],
    )
    came = swapped(send, "sub")
    keep = vmem_call(keep_kernel, [((rows, half_model), f32)], [heads, out_weight, residual])[0]
    came, keep = lax.optimization_barrier((came, keep))
    chip_sum, send = vmem_call(
        chip_sum_kernel, [((rows, half_model), f32), ((rows, half_model), bf16)], [keep, came]
    )
    came = swapped(send, "head")
    send, *late = lax.optimization_barrier((send, in_weight, norm_gain[None, :], beta_weight.T, log_decay.T))
    late = fetched(*late)
    came, (in_weight, norm_gain, beta_weight, log_decay) = lax.optimization_barrier((came, late))
    hidden = vmem_call(hidden_kernel, [((rows, half_model), bf16)], [chip_sum, came])[0]
    twin_hidden = swapped(hidden, "sub")
    sums = vmem_call(
        own_half_kernel,
        [((rows, in_weight.shape[1]), f32), ((value_here, rows), f32), ((rows, LANES), f32)],
        [hidden, norm_gain, in_weight, beta_weight],
    )
    twin_hidden, (mixed, logits, squares) = lax.optimization_barrier((twin_hidden, sums))
    payload_shape = ((4 * rows + 16, LANES), bf16)
    payloads = {}
    scaled, scale, extra, payloads[2] = vmem_call(
        twin_half_kernel,
        [((rows, half_model), bf16), ((rows, LANES), f32), ((2 * value_here, rows), f32), payload_shape],
        [twin_hidden, norm_gain, beta_weight, log_decay, logits, squares, in_weight, mixed],
        [pltpu.VMEM((16, LANES), f32)],
    )
    for mask in (3, 1, 0):
        payloads[mask] = vmem_call(
            functools.partial(payload_kernel, mask),
            [payload_shape],
            [scaled, scale, in_weight, mixed, extra],
            [pltpu.VMEM((16, LANES), f32)],
        )[0]
    new_residual = vmem_call(residual_kernel, [(residual.shape, bf16)], [hidden, twin_hidden], last=True)[0]
    came = {mask: swapped(payloads[mask], "ctx", mask) for mask in masks}
    came[0] = payloads[0]
    half = rows // 2
    terms_shapes = [
        ((4, 2, 2, DK, DV), f32),
        ((4, 2, 2, DK + half, DK), bf16),
        ((4, 2, rows, DV), f32),
        ((4, 2, 2, 8, LANES), f32),
    ]
    terms = []
    for group in GROUPS:
        terms = vmem_call(
            functools.partial(block_kernel, group),
            terms_shapes,
            [*(came[mask] for mask in group), *terms],
            aliases={len(group) + i: i for i in range(4)} if terms else None,
        )
    own, *backs = vmem_call(
        scan_kernel,
        [((rows, 2 * DV), bf16)] * 4,
        [*terms, delta_gain[None, :]],
        [pltpu.VMEM((4, rows, 2 * DV), bf16)],
    )
    backs = {mask: swapped(backs[mask - 1], "ctx", mask) for mask in masks}
    delta_out = pl.pallas_call(
        place_kernel,
        out_shape=jax.ShapeDtypeStruct((rows, value_here * DV), bf16),
        in_specs=[IN_VMEM] * 4,
        out_specs=IN_HBM,
        scratch_shapes=[pltpu.SemaphoreType.DMA((4,))],
        compiler_params=pltpu.CompilerParams(vmem_limit_bytes=4 * MIB),
    )(*[in_vmem(back) for back in (own, backs[3], backs[1], backs[2])])
    return (new_residual, delta_out)


def solution(mesh):
    local = owner_local if owners_fit(mesh) else hop_local
    return jax.shard_map(
        local,
        mesh=mesh,
        in_specs=(
            P(("groups", "ctx"), ("head", "sub")),
            P(("groups", "ctx"), ("head", "sub")),
            P(("groups", "ctx"), None),
            P(("groups", "ctx"), ("head", "sub")),
            P(("head", "sub"), None),
            P(),
            P(None, ("head", "sub")),
            P(None, ("head", "sub")),
            P(("groups", "ctx"), ("head", "sub")),
            P(),
        ),
        out_specs=(P(("groups", "ctx"), ("head", "sub")), P(("groups", "ctx"), ("head", "sub"))),
        check_vma=False,
    )
```

```python
import functools

import jax
import jax.numpy as jnp
from jax import lax
from jax.experimental import pallas as pl
from jax.experimental.pallas import tpu as pltpu
from jax.sharding import PartitionSpec as P

HEADS = 16
KV_HEADS = 2
HD = 256
DK = 128
DV = 128


TOP_PRECISION = lax.Precision.HIGHEST
EPSILON = 1e-06
NEGATIVE = -1e30


def passed_along(value, axis, steps):
    count = lax.axis_size(axis)
    initial, last = (max(0, -steps), min(count, count - steps))
    return lax.ppermute(value, axis, [(source, source + steps) for source in range(initial, last)])


def stored_positions(first_row, row_total, half_rows, ctx_count):
    row_index = first_row + jnp.arange(row_total, dtype=jnp.int32)
    device_of = row_index // (2 * half_rows)
    within_dev = row_index % (2 * half_rows)
    block_number = jnp.where(within_dev < half_rows, device_of, 2 * ctx_count - 1 - device_of)
    return block_number * half_rows + within_dev % half_rows


def unit_rows(matrix):
    return matrix * lax.rsqrt(jnp.sum(matrix * matrix, axis=-1, keepdims=True) + EPSILON)


def to_blocks(array, half_rows):
    heads_count = array.shape[1]
    width = array.shape[2]
    shaped = array.reshape(2, half_rows, heads_count, width).transpose(2, 0, 1, 3)
    return shaped.reshape(heads_count * 2, half_rows, width)


def block_terms(query_rows, key_rows, value_rows, beta_rows, decay_rows):
    length = query_rows.shape[0]
    cumulative = jnp.cumsum(decay_rows)
    position = jnp.arange(length)
    on_or_below = position[:, None] >= position[None, :]
    strictly_below = position[:, None] > position[None, :]
    decay_gap = cumulative[:, None] - cumulative[None, :]
    decay_grid = jnp.where(on_or_below, jnp.exp(jnp.where(on_or_below, decay_gap, 0.0)), 0.0)
    key_gram = jnp.dot(key_rows, key_rows.T, precision=TOP_PRECISION)
    system = jnp.eye(length, dtype=jnp.float32) + jnp.where(
        strictly_below, beta_rows[:, None] * key_gram * decay_grid, 0.0
    )
    growth = jnp.exp(cumulative)
    right_side = beta_rows[:, None] * jnp.concatenate(
        [value_rows, growth[:, None] * key_rows], axis=1
    )
    solved = jax.scipy.linalg.solve_triangular(system, right_side, lower=True, unit_diagonal=True)
    update_rows = solved[:, : value_rows.shape[1]]
    weight_rows = solved[:, value_rows.shape[1] :]
    attend_grid = jnp.where(
        on_or_below, jnp.dot(query_rows, key_rows.T, precision=TOP_PRECISION) * decay_grid, 0.0
    )
    local_out = jnp.dot(attend_grid, update_rows, precision=TOP_PRECISION)
    read_rows = growth[:, None] * query_rows - jnp.dot(
        attend_grid, weight_rows, precision=TOP_PRECISION
    )
    carried_keys = jnp.exp(cumulative[-1] - cumulative)[:, None] * key_rows
    identity_map = jnp.eye(key_rows.shape[1], dtype=jnp.float32)
    transition = jnp.exp(cumulative[-1]) * identity_map - jnp.dot(
        carried_keys.T, weight_rows, precision=TOP_PRECISION
    )
    offset_state = jnp.dot(carried_keys.T, update_rows, precision=TOP_PRECISION)
    return (local_out, read_rows, transition, offset_state)


def apply_map(matrix_maps, offsets, states):
    return jnp.einsum("hij,hjk->hik", matrix_maps, states, precision=TOP_PRECISION) + offsets


def attend_rows(running, query_block, key_block, value_block, visible, score_scale):
    run_max, run_sum, run_acc = running
    scores = (
        jnp.einsum("rhd,kd->rhk", query_block, key_block, preferred_element_type=jnp.float32)
        * score_scale
    )
    if visible is not None:
        scores = jnp.where(visible[:, None, :], scores, NEGATIVE)
    new_max = jnp.maximum(run_max, jnp.max(scores, axis=2))
    weights = jnp.exp(scores - new_max[:, :, None])
    if visible is not None:
        weights = jnp.where(visible[:, None, :], weights, 0.0)
    rescale = jnp.exp(run_max - new_max)
    run_sum = run_sum * rescale + jnp.sum(weights, axis=2)
    added = jnp.einsum(
        "rhk,kd->rhd", weights.astype(jnp.bfloat16), value_block, preferred_element_type=jnp.float32
    )
    run_acc = run_acc * rescale[:, :, None] + added
    return (new_max, run_sum, run_acc)


def hop_local(
    att_query,
    att_gate,
    att_kv,
    residual,
    out_weight,
    norm_gain,
    in_weight,
    beta_weight,
    log_decay,
    delta_gain,
):
    ctx_count = lax.axis_size("ctx")
    ctx_rank = lax.axis_index("ctx")
    shard_rank = lax.axis_index(("head", "sub"))
    rows_here = att_query.shape[0]
    half_rows = rows_here // 2
    heads_here = att_query.shape[1] // HD
    kv_number = shard_rank * heads_here // (HEADS // KV_HEADS)
    key_local = lax.dynamic_slice_in_dim(att_kv, kv_number * 2 * HD, HD, 1)
    value_local = lax.dynamic_slice_in_dim(att_kv, kv_number * 2 * HD + HD, HD, 1)
    query_heads = att_query.reshape(rows_here, heads_here, HD)
    late_queries = query_heads[half_rows:]
    query_places = stored_positions(ctx_rank * rows_here, rows_here, half_rows, ctx_count)
    same_visible = query_places[:, None] >= query_places[None, :]
    score_scale = HD ** (-0.5)

    def earlier_shard(running, key_shard, value_shard):
        return attend_rows(
            running, query_heads, key_shard[:half_rows], value_shard[:half_rows], None, score_scale
        )

    def same_shard(running, key_shard, value_shard):
        return attend_rows(running, query_heads, key_shard, value_shard, same_visible, score_scale)

    def later_shard(running, key_shard, value_shard):
        late_part = tuple((member[half_rows:] for member in running))
        renewed = attend_rows(late_part, late_queries, key_shard, value_shard, None, score_scale)
        return tuple(
            (
                jnp.concatenate([member[:half_rows], latest], axis=0)
                for member, latest in zip(running, renewed)
            )
        )

    start_running = (
        jnp.full((rows_here, heads_here), NEGATIVE, jnp.float32),
        jnp.zeros((rows_here, heads_here), jnp.float32),
        jnp.zeros((rows_here, heads_here, HD), jnp.float32),
    )
    key_block = lax.all_gather(key_local, "ctx", axis=0, tiled=True)
    value_block = lax.all_gather(value_local, "ctx", axis=0, tiled=True)
    piece_rows = key_block.shape[0]

    def one_shard(number, current):
        offset = number * rows_here
        key_shard = lax.dynamic_slice_in_dim(key_block, offset, rows_here, 0)
        value_shard = lax.dynamic_slice_in_dim(value_block, offset, rows_here, 0)
        shard_number = offset // rows_here
        branch = jnp.clip(shard_number - ctx_rank, -1, 1) + 1
        return lax.switch(
            branch, [earlier_shard, same_shard, later_shard], current, key_shard, value_shard
        )

    run_max, run_sum, run_acc = lax.fori_loop(0, piece_rows // rows_here, one_shard, start_running)
    gate_heads = jax.nn.sigmoid(att_gate.reshape(rows_here, heads_here, HD).astype(jnp.float32))
    att_heads = (
        (run_acc / run_sum[:, :, None] * gate_heads)
        .astype(jnp.bfloat16)
        .reshape(rows_here, heads_here * HD)
    )
    partial_term = jnp.dot(att_heads, out_weight, preferred_element_type=jnp.float32)
    col_width = residual.shape[1]
    col_start = shard_rank * col_width
    placed = lax.dynamic_slice_in_dim(partial_term, col_start, col_width, 1) + residual.astype(
        jnp.float32
    )
    partial_term = lax.dynamic_update_slice_in_dim(partial_term, placed, col_start, 1)
    hidden = lax.psum(partial_term.astype(jnp.bfloat16), ("head", "sub")).astype(jnp.float32)
    mean_square = jnp.mean(hidden * hidden, axis=1, keepdims=True)
    normed = (hidden * lax.rsqrt(mean_square + EPSILON) * norm_gain).astype(jnp.bfloat16)
    new_residual = lax.dynamic_slice_in_dim(hidden, col_start, col_width, 1).astype(jnp.bfloat16)
    mixed_cols = jnp.dot(normed, in_weight, preferred_element_type=jnp.float32)
    beta_logits = jnp.dot(normed, beta_weight, preferred_element_type=jnp.float32)
    key_here = in_weight.shape[1] // (2 * DK + 2 * DV)
    value_here = 2 * key_here
    grouped = mixed_cols.reshape(rows_here, key_here, 2 * DK + 2 * DV)
    query_unit = jnp.repeat(unit_rows(jax.nn.silu(grouped[:, :, :DK])) * DK ** (-0.5), 2, axis=1)
    key_unit = jnp.repeat(unit_rows(jax.nn.silu(grouped[:, :, DK : 2 * DK])), 2, axis=1)
    value_all = jax.nn.silu(grouped[:, :, 2 * DK :]).reshape(rows_here, value_here, DV)
    beta_all = jax.nn.sigmoid(beta_logits)
    local_out, read_rows, transition, offset_state = jax.vmap(block_terms)(
        to_blocks(query_unit, half_rows),
        to_blocks(key_unit, half_rows),
        to_blocks(value_all, half_rows),
        to_blocks(beta_all[:, :, None], half_rows)[:, :, 0],
        to_blocks(log_decay[:, :, None], half_rows)[:, :, 0],
    )
    transition = transition.reshape(value_here, 2, DK, DK)
    offset_state = offset_state.reshape(value_here, 2, DK, DV)
    early_map, late_map = (transition[:, 0], transition[:, 1])
    early_offset, late_offset = (offset_state[:, 0], offset_state[:, 1])
    last_rank = ctx_count - 1
    zero_states = jnp.zeros_like(early_offset)

    def early_turn(number, incoming):
        return passed_along(
            apply_map(early_map, early_offset, incoming).astype(jnp.bfloat16), "ctx", 1
        ).astype(jnp.float32)

    early_in = lax.fori_loop(0, ctx_count - 1, early_turn, zero_states)
    early_end = apply_map(early_map, early_offset, early_in)
    late_start = jnp.where(ctx_rank == last_rank, early_end, zero_states)

    def late_turn(number, incoming):
        moved = passed_along(
            apply_map(late_map, late_offset, incoming).astype(jnp.bfloat16), "ctx", -1
        ).astype(jnp.float32)
        return jnp.where(ctx_rank == last_rank, early_end, moved)

    late_in = lax.fori_loop(0, ctx_count - 1, late_turn, late_start)
    states_in = jnp.stack([early_in, late_in], axis=1)
    block_out = local_out.reshape(value_here, 2, half_rows, DV) + jnp.einsum(
        "hbck,hbkv->hbcv",
        read_rows.reshape(value_here, 2, half_rows, DK),
        states_in,
        precision=TOP_PRECISION,
    )
    token_out = block_out.transpose(1, 2, 0, 3).reshape(rows_here, value_here, DV)
    out_square = jnp.mean(token_out * token_out, axis=2, keepdims=True)
    delta_out = (token_out * lax.rsqrt(out_square + EPSILON) * delta_gain).astype(jnp.bfloat16)
    return (new_residual, delta_out.reshape(rows_here, value_here * DV))


KEY_HEADS = 16
IN_VMEM = pl.BlockSpec(memory_space=pltpu.VMEM)
IN_HBM = pl.BlockSpec(memory_space=pl.ANY)
MIB = 2**20
LANES = 128
GROUPS = ((0,), (2,), (1,), (3,))


def owners_fit(mesh):
    shards = mesh.shape["head"] * mesh.shape["sub"]
    key_here = KEY_HEADS // shards
    return mesh.shape["head"] == 2 and mesh.shape["sub"] == 2 and key_here == mesh.shape["ctx"]


def in_vmem(array):
    return pltpu.with_memory_space_constraint(array, pltpu.VMEM)


def in_hbm(array):
    return pltpu.with_memory_space_constraint(array, pltpu.HBM)


def vmem_call(kernel, outs, operands, scratch=(), limit=16, aliases=None, last=False, cost=None):
    make = jax.ShapeDtypeStruct if last else pltpu.VMEM
    return pl.pallas_call(
        kernel,
        out_shape=[make(shape, dtype) for shape, dtype in outs],
        in_specs=[IN_VMEM] * len(operands),
        out_specs=[IN_VMEM] * len(outs),
        scratch_shapes=list(scratch),
        input_output_aliases=aliases or {},
        cost_estimate=cost,
        compiler_params=pltpu.CompilerParams(vmem_limit_bytes=limit * MIB),
    )(*[in_vmem(operand) for operand in operands])


def swapped(value, axis, mask=1):
    return lax.ppermute(value, axis, [(i, i ^ mask) for i in range(lax.axis_size(axis))])


def dot(left, right, dims=((1,), (0,))):
    return lax.dot_general(left, right, (dims, ((), ())), preferred_element_type=jnp.float32)


def halves(value):
    high = value.astype(jnp.bfloat16)
    return high, (value - high.astype(jnp.float32)).astype(jnp.bfloat16)


def sigmoid(value):
    return 1.0 / (1.0 + jnp.exp(-value))


def silu(value):
    return value / (1.0 + jnp.exp(-value))


def piece_kernel(kv_ref, piece_ref, sem):
    start = (lax.axis_index("head") * 2 + lax.axis_index("sub")) * HD
    copy = pltpu.make_async_copy(kv_ref.at[:, pl.ds(pl.multiple_of(start, HD), HD)], piece_ref, sem)
    copy.start()
    copy.wait()


def fetch_kernel(*refs):
    count = len(refs) // 2
    copies = [
        pltpu.make_async_copy(refs[n], refs[count + n], refs[-1].at[n]) for n in range(count)
    ]
    for copy in copies:
        copy.start()
    for copy in copies:
        copy.wait()


def fetched(*arrays):
    moved = sum(array.size * array.dtype.itemsize for array in arrays)
    return pl.pallas_call(
        fetch_kernel,
        out_shape=[pltpu.VMEM(array.shape, array.dtype) for array in arrays],
        in_specs=[IN_HBM] * len(arrays),
        out_specs=[IN_VMEM] * len(arrays),
        scratch_shapes=[pltpu.SemaphoreType.DMA((len(arrays),))],
        compiler_params=pltpu.CompilerParams(vmem_limit_bytes=4 * MIB),
        cost_estimate=pl.CostEstimate(flops=0, bytes_accessed=moved, transcendentals=0),
    )(*[in_hbm(array) for array in arrays])


def attend(query_ref, gate_ref, keys, values, rows, key_total, visible):
    count = query_ref.shape[1] // HD
    columns = [slice(head * HD, (head + 1) * HD) for head in range(count)]
    size = rows.stop - rows.start
    queries = jnp.concatenate([query_ref[rows, part] for part in columns], axis=0)
    gates = [sigmoid(gate_ref[rows, part].astype(jnp.float32)) for part in columns]
    scores = dot(queries, keys[0:key_total], ((1,), (1,))) * HD ** (-0.5)
    scores = jnp.where(jnp.concatenate([visible] * count, axis=0), scores, NEGATIVE)
    weights = jnp.exp(scores - jnp.max(scores, axis=1, keepdims=True))
    total = jnp.sum(weights, axis=1, keepdims=True)
    gathered = dot(weights.astype(jnp.bfloat16), values[0:key_total]) / total
    gated = [gathered[head * size : (head + 1) * size] * gates[head] for head in range(count)]
    return jnp.concatenate(gated, axis=1).astype(jnp.bfloat16)


def attention_kernel(
    query_ref, gate_ref, kv_ref, mine1, mine2, mine3, twin1, twin2, twin3, weight_ref, residual_ref,
    heads_ref, send_ref, keys, values, sums,
):
    half = query_ref.shape[0] // 2
    ctx_rank, head_rank, sub_rank = (lax.axis_index(name) for name in ("ctx", "head", "sub"))
    count = 4
    own_start = pl.multiple_of(head_rank * 2 * HD, 2 * HD)

    def put(target, mask, part):
        target[mask * half : (mask + 1) * half] = part[0:half]
        target[(count + mask) * half : (count + mask + 1) * half] = part[half : 2 * half]

    put(keys, 0, kv_ref[:, pl.ds(own_start, HD)])
    put(values, 0, kv_ref[:, pl.ds(own_start + HD, HD)])

    @pl.when(sub_rank == 0)
    def _():
        for mask, (mine, twin) in enumerate(((mine1, twin1), (mine2, twin2), (mine3, twin3)), 1):
            put(keys, mask, mine[...])
            put(values, mask, twin[...])

    @pl.when(sub_rank != 0)
    def _():
        for mask, (mine, twin) in enumerate(((mine1, twin1), (mine2, twin2), (mine3, twin3)), 1):
            put(keys, mask, twin[...])
            put(values, mask, mine[...])

    shift = half.bit_length() - 1
    row = lax.broadcasted_iota(jnp.int32, (half, 1), 0)
    column = lax.broadcasted_iota(jnp.int32, (1, 2 * count * half), 1)
    device = jnp.bitwise_xor(ctx_rank, (column >> shift) & (count - 1))
    block = jnp.where(column < count * half, device, 2 * count - 1 - device)
    key_place = block * half + (column & (half - 1))
    for part, block_here in enumerate((ctx_rank, 2 * count - 1 - ctx_rank)):
        rows = slice(part * half, (part + 1) * half)
        key_total = (part + 1) * count * half
        visible = row + block_here * half >= key_place[:, :key_total]
        heads_ref[rows] = attend(query_ref, gate_ref, keys, values, rows, key_total, visible)
    mid = send_ref.shape[1]
    width = residual_ref.shape[1]
    sums[...] = dot(heads_ref[...], weight_ref[:, pl.ds(pl.multiple_of((1 - sub_rank) * mid, mid), mid)])

    @pl.when(sub_rank != head_rank)
    def _():
        sums[:, pl.ds(pl.multiple_of(sub_rank * width, width), width)] += residual_ref[...].astype(jnp.float32)

    send_ref[...] = sums[...].astype(jnp.bfloat16)


def keep_kernel(heads_ref, weight_ref, residual_ref, keep_ref):
    head_rank, sub_rank = lax.axis_index("head"), lax.axis_index("sub")
    mid = keep_ref.shape[1]
    width = residual_ref.shape[1]
    keep_ref[...] = dot(heads_ref[...], weight_ref[:, pl.ds(pl.multiple_of(sub_rank * mid, mid), mid)])

    @pl.when(sub_rank == head_rank)
    def _():
        keep_ref[:, pl.ds(pl.multiple_of(sub_rank * width, width), width)] += residual_ref[...].astype(jnp.float32)


def chip_sum_kernel(keep_ref, came_ref, sum_ref, send_ref):
    total = keep_ref[...] + came_ref[...].astype(jnp.float32)
    sum_ref[...] = total
    send_ref[...] = total.astype(jnp.bfloat16)


def hidden_kernel(keep_ref, came_ref, hidden_ref):
    hidden_ref[...] = (keep_ref[...] + came_ref[...].astype(jnp.float32)).astype(jnp.bfloat16)


def half_of(ref, own):
    sub_rank = lax.axis_index("sub")
    mid = ref.shape[-1] // 2
    return pl.ds(pl.multiple_of((sub_rank if own else 1 - sub_rank) * mid, mid), mid)


def own_half_kernel(own_ref, gain_ref, weight_ref, beta_ref, mixed_ref, logit_ref, square_ref):
    mid = own_ref.shape[1]
    own = own_ref[...].astype(jnp.float32)
    columns = half_of(gain_ref, True)
    scaled = (own * gain_ref[:, columns]).astype(jnp.bfloat16)
    square_ref[...] = jnp.broadcast_to(jnp.sum(own * own, axis=1, keepdims=True), square_ref.shape)
    logit_ref[...] = dot(beta_ref[:, columns], scaled, ((1,), (1,)))
    rows = pl.ds(pl.multiple_of(lax.axis_index("sub") * mid, mid), mid)
    mixed_ref[...] = dot(scaled, weight_ref[rows, :])


def twin_half_kernel(
    twin_ref, gain_ref, beta_ref, decay_ref, logit_ref, square_ref, weight_ref, mixed_ref,
    scaled_ref, scale_ref, extra_ref, payload_ref, small,
):
    twin = twin_ref[...].astype(jnp.float32)
    columns = half_of(gain_ref, False)
    scaled_ref[...] = (twin * gain_ref[:, columns]).astype(jnp.bfloat16)
    squares = square_ref[...] + jnp.sum(twin * twin, axis=1, keepdims=True)
    scale = lax.rsqrt(squares / gain_ref.shape[1] + EPSILON)
    scale_ref[...] = scale
    values = decay_ref.shape[0]
    logits = logit_ref[...] + dot(beta_ref[:, columns], scaled_ref[...], ((1,), (1,)))
    extra_ref[0:values] = decay_ref[...]
    extra_ref[values : 2 * values] = sigmoid(logits * jnp.transpose(scale)[0:1])
    payload_kernel(2, scaled_ref, scale_ref, weight_ref, mixed_ref, extra_ref, payload_ref, small)


def residual_kernel(own_ref, twin_ref, residual_ref):
    head_rank, sub_rank = lax.axis_index("head"), lax.axis_index("sub")
    width = residual_ref.shape[1]
    columns = pl.ds(pl.multiple_of(sub_rank * width, width), width)

    @pl.when(sub_rank == head_rank)
    def _():
        residual_ref[...] = own_ref[:, columns]

    @pl.when(sub_rank != head_rank)
    def _():
        residual_ref[...] = twin_ref[:, columns]


def payload_kernel(mask, scaled_ref, scale_ref, weight_ref, mixed_ref, extra_ref, payload_ref, small):
    rows, mid = scaled_ref.shape
    group = 2 * DK + 2 * DV
    target = jnp.bitwise_xor(lax.axis_index("ctx"), mask)
    columns = pl.ds(pl.multiple_of(target * group, group), group)
    weight_rows = pl.ds(pl.multiple_of((1 - lax.axis_index("sub")) * mid, mid), mid)
    mixed = mixed_ref[:, columns] + dot(scaled_ref[...], weight_ref[weight_rows, columns])
    mixed = silu(mixed * scale_ref[:, 0:1])
    query, key = mixed[:, :DK], mixed[:, DK : 2 * DK]
    payload_ref[0:rows] = unit_rows(key).astype(jnp.bfloat16)
    values = extra_ref.shape[0] // 2
    small[...] = jnp.zeros_like(small)
    for place, base in ((0, 0), (4, values)):
        full = extra_ref[pl.ds(base + 2 * target, 2), :]
        high = full.astype(jnp.bfloat16).astype(jnp.float32)
        small[place : place + 2] = high
        small[place + 2 : place + 4] = full - high
    payload_ref[rows : rows + 16] = small[...].astype(jnp.bfloat16)
    rest = (unit_rows(query) * DK ** (-0.5), mixed[:, 2 * DK : 2 * DK + DV], mixed[:, 2 * DK + DV :])
    for number, part in enumerate(rest, 1):
        payload_ref[number * rows + 16 : (number + 1) * rows + 16] = part.astype(jnp.bfloat16)


def joined(left, right):
    (left_high, left_low), (right_high, right_low) = left, right
    right_high, right_low = apart(right_high), apart(right_low)
    return dot(
        jnp.concatenate([left_high, left_high, left_low], axis=1),
        jnp.concatenate([right_high, right_low, right_high], axis=0),
    )


def apart(pair):
    first = lax.broadcasted_iota(jnp.int32, pair.shape, 1) < pair.shape[1] // 2
    zero = jnp.zeros_like(pair)
    return jnp.concatenate([jnp.where(first, pair, zero), jnp.where(first, zero, pair)], axis=0)


def unit_lower_inverses(stricts):
    half = stricts[0].shape[0]
    row = lax.broadcasted_iota(jnp.int32, (half, 1), 0)
    column = lax.broadcasted_iota(jnp.int32, (1, 2 * half), 1) & (half - 1)
    inner = (row >> 3) == (column >> 3)
    identity = jnp.where(row == column, 1.0, 0.0)
    number = range(len(stricts))
    smalls = [jnp.where(inner, strict, 0.0) for strict in stricts]
    rests = [halves(jnp.where(inner, 0.0, strict)) for strict in stricts]
    small = [halves(part) for part in smalls]
    inverses = [identity - part for part in smalls]
    split = [halves(inverse) for inverse in inverses]
    seconds = [halves(joined(part, part)) for part in small]
    fourths = [halves(joined(second, second)) for second in seconds]
    inverses = [inverses[n] + joined(split[n], seconds[n]) for n in number]
    split = [halves(inverse) for inverse in inverses]
    inverses = [inverses[n] + joined(split[n], fourths[n]) for n in number]
    split = [halves(inverse) for inverse in inverses]
    steps = [halves(joined(split[n], rests[n])) for n in number]
    doubles = [halves(joined(step, step)) for step in steps]
    results = [inverses[n] - joined(steps[n], split[n]) for n in number]
    quads = [halves(joined(double, double)) for double in doubles]
    results = [results[n] + joined(doubles[n], halves(results[n])) for n in number]
    return [results[n] + joined(quads[n], halves(results[n])) for n in number]


def key_terms(chunks):
    rows = chunks[0][0].shape[0]
    half = rows // 2
    shift = half.bit_length() - 1
    row = lax.broadcasted_iota(jnp.int32, (rows, 1), 0)
    column = lax.broadcasted_iota(jnp.int32, (1, rows), 1)
    together = (row >> shift) == (column >> shift)
    inclusive = together & (row >= column)
    strictly = together & (row > column)
    early = column < half
    below = jnp.where(inclusive, 1.0, 0.0).astype(jnp.bfloat16)
    diagonal = jnp.where(row == column, 1.0, 0.0).astype(jnp.bfloat16)
    below, diagonal = (jnp.concatenate([left, left], axis=1) for left in (below, diagonal))
    items = [(chunk, head) for chunk in range(len(chunks)) for head in range(2)]
    keys = [key for key, _ in chunks]
    extras = [extra.astype(jnp.float32) for _, extra in chunks]

    def spread(left, chunk, place):
        lanes = [
            jnp.broadcast_to(extras[chunk][n : n + 1], (rows, rows)).astype(jnp.bfloat16) for n in (place, place + 2)
        ]
        return dot(left, jnp.concatenate(lanes, axis=1), ((1,), (1,)))

    sums = [dot(extra, below[:, :rows], ((1,), (1,))) for _, extra in chunks]
    key_grams = [dot(key, key, ((1,), (1,))) for key in keys]
    totals = {item: spread(below, *item) for item in items}
    betas = {(chunk, head): spread(diagonal, chunk, head + 4) for chunk, head in items}
    total_rows = {(c, h): sums[c][h : h + 1] + sums[c][h + 2 : h + 3] for c, h in items}
    decays = {item: jnp.exp(jnp.where(inclusive, totals[item] - total_rows[item], NEGATIVE)) for item in items}
    stricts = [jnp.where(strictly, betas[item] * key_grams[item[0]] * decays[item], 0.0) for item in items]
    wide = [key.astype(jnp.float32) for key in keys]
    turned = [jnp.transpose(key) for key in wide]
    growths = {item: jnp.exp(totals[item]) for item in items}
    pairs = [strict[:half] + strict[half:] for strict in stricts]
    inverses = [[apart(part) for part in halves(inverse)] for inverse in unit_lower_inverses(pairs)]
    terms = []
    for item, (high, low) in zip(items, inverses):
        total = total_rows[item]
        end = jnp.where(early, total[:, half - 1 : half], total[:, rows - 1 : rows])
        carried = turned[item[0]] * jnp.exp(end - total)
        carried = [jnp.where(early, carried, 0.0), jnp.where(early, 0.0, carried)]
        weighted = (betas[item] * growths[item] * wide[item[0]]).astype(jnp.bfloat16)
        lefts = jnp.concatenate(carried, axis=0).astype(jnp.bfloat16)
        terms.append((betas[item], decays[item], growths[item], weighted, lefts, high, low, jnp.exp(end)))
    return terms


def finish_terms(source, query, key, values, terms, offset_ref, linear_ref, local_ref, growth_ref):
    rows = query.shape[0]
    half = rows // 2
    query_gram = dot(query, key, ((1,), (1,)))
    solved = []
    for value, (beta, _, _, weighted, _, high, low, _) in zip(values, terms):
        right = jnp.concatenate([(beta * value.astype(jnp.float32)).astype(jnp.bfloat16), weighted], axis=1)
        both = dot(jnp.concatenate([high, low], axis=1), jnp.concatenate([right, right], axis=0))
        solved.append(both.astype(jnp.bfloat16))
    moved = []
    for part, (_, decay, _, _, lefts, _, _, _) in zip(solved, terms):
        moved.append(dot(jnp.concatenate([lefts, (query_gram * decay).astype(jnp.bfloat16)], axis=0), part))
    for head, (part, (_, _, growth, _, _, _, _, ends)) in enumerate(zip(moved, terms)):
        attended = part[2 * DK :]
        local_ref[source, head] = attended[:, :DV]
        reads = (growth * query.astype(jnp.float32) - attended[:, DV:]).astype(jnp.bfloat16)
        for block in range(2):
            state = part[block * DK : (block + 1) * DK]
            offset_ref[source, head, block] = state[:, :DV]
            linear_ref[source, head, block, 0:DK] = state[:, DV:].astype(jnp.bfloat16)
            linear_ref[source, head, block, DK : DK + half] = reads[block * half : (block + 1) * half]
            last = (block + 1) * half - 1
            growth_ref[source, head, block] = jnp.broadcast_to(ends[:, last : last + 1], growth_ref.shape[3:])


def source_of(mask):
    return jnp.bitwise_xor(lax.axis_index("ctx"), mask)


def block_kernel(masks, *refs):
    payload_refs, outs = refs[: len(masks)], refs[-4:]
    rows = (payload_refs[0].shape[0] - 16) // 4
    keys = [ref[0:rows] for ref in payload_refs]
    terms = key_terms([(key, ref[rows : rows + 16]) for key, ref in zip(keys, payload_refs)])
    for number, (mask, ref) in enumerate(zip(masks, payload_refs)):
        query, *values = (ref[n * rows + 16 : (n + 1) * rows + 16] for n in (1, 2, 3))
        finish_terms(source_of(mask), query, keys[number], values, terms[2 * number : 2 * number + 2], *outs)


def scan_kernel(offset_ref, linear_ref, local_ref, growth_ref, gain_ref, own_ref, back1, back2, back3, outs):
    count = offset_ref.shape[0]
    half = local_ref.shape[2] // 2
    rank = lax.axis_index("ctx")
    states = [None, None]
    for number in range(2 * count):
        source, block = (number, 0) if number < count else (2 * count - 1 - number, 1)
        block_rows = slice(block * half, (block + 1) * half)
        for head in range(2):
            out = local_ref[source, head, block_rows]
            state = offset_ref[source, head, block]
            if states[head] is not None:
                moved = dot(linear_ref[source, head, block], states[head].astype(jnp.bfloat16))
                out = out + moved[DK:]
                state = state - moved[:DK] + growth_ref[source, head, block, 0:1] * states[head]
            states[head] = state
            scale = lax.rsqrt(jnp.mean(out * out, axis=1, keepdims=True) + EPSILON)
            outs[source, block_rows, head * DV : (head + 1) * DV] = (out * scale * gain_ref[...]).astype(jnp.bfloat16)
    own_ref[...] = outs[rank]
    for mask, back in enumerate((back1, back2, back3), 1):
        back[...] = outs[jnp.bitwise_xor(rank, mask)]


def place_kernel(own_ref, back3, back1, back2, out_ref, sems):
    width = own_ref.shape[1]
    rank = lax.axis_index("ctx")
    copies = []
    for mask, back in enumerate((own_ref, back1, back2, back3)):
        columns = pl.ds(pl.multiple_of(jnp.bitwise_xor(rank, mask) * width, width), width)
        copies.append(pltpu.make_async_copy(back, out_ref.at[:, columns], sems.at[mask]))
        copies[-1].start()
    for copy in copies:
        copy.wait()


def owner_local(
    att_query,
    att_gate,
    att_kv,
    residual,
    out_weight,
    norm_gain,
    in_weight,
    beta_weight,
    log_decay,
    delta_gain,
):
    bf16, f32 = jnp.bfloat16, jnp.float32
    rows, head_columns = att_query.shape
    model = out_weight.shape[1]
    half_model = model // 2
    value_here = log_decay.shape[1]
    masks = (2, 3, 1)
    piece = pl.pallas_call(
        piece_kernel,
        out_shape=pltpu.VMEM((rows, HD), bf16),
        in_specs=[IN_HBM],
        out_specs=IN_VMEM,
        scratch_shapes=[pltpu.SemaphoreType.DMA],
        compiler_params=pltpu.CompilerParams(vmem_limit_bytes=4 * MIB),
    )(in_hbm(att_kv))
    mine = {mask: swapped(piece, "ctx", mask) for mask in masks[::-1]}
    piece, *late = lax.optimization_barrier((piece, att_query, att_gate, att_kv, out_weight, residual))
    late = fetched(*late)
    mine[3], (att_query, att_gate, att_kv, out_weight, residual) = lax.optimization_barrier((mine[3], late))
    twin = {3: swapped(mine[3], "sub"), 1: swapped(mine[1], "sub")}
    mine[2] = lax.optimization_barrier((mine[2], twin[3]))[0]
    twin[2] = swapped(mine[2], "sub")
    heads, send = vmem_call(
        attention_kernel,
        [((rows, head_columns), bf16), ((rows, half_model), bf16)],
        [att_query, att_gate, att_kv, mine[1], mine[2], mine[3], twin[1], twin[2], twin[3], out_weight, residual],
        [
            pltpu.VMEM((4 * rows, HD), bf16),
            pltpu.VMEM((4 * rows, HD), bf16),
            pltpu.VMEM((rows, half_model), f32),
        ],
    )
    came = swapped(send, "sub")
    keep = vmem_call(keep_kernel, [((rows, half_model), f32)], [heads, out_weight, residual])[0]
    came, keep = lax.optimization_barrier((came, keep))
    chip_sum, send = vmem_call(
        chip_sum_kernel, [((rows, half_model), f32), ((rows, half_model), bf16)], [keep, came]
    )
    came = swapped(send, "head")
    send, *late = lax.optimization_barrier((send, in_weight, norm_gain[None, :], beta_weight.T, log_decay.T))
    late = fetched(*late)
    came, (in_weight, norm_gain, beta_weight, log_decay) = lax.optimization_barrier((came, late))
    hidden = vmem_call(hidden_kernel, [((rows, half_model), bf16)], [chip_sum, came])[0]
    twin_hidden = swapped(hidden, "sub")
    sums = vmem_call(
        own_half_kernel,
        [((rows, in_weight.shape[1]), f32), ((value_here, rows), f32), ((rows, LANES), f32)],
        [hidden, norm_gain, in_weight, beta_weight],
    )
    twin_hidden, (mixed, logits, squares) = lax.optimization_barrier((twin_hidden, sums))
    payload_shape = ((4 * rows + 16, LANES), bf16)
    payloads = {}
    scaled, scale, extra, payloads[2] = vmem_call(
        twin_half_kernel,
        [((rows, half_model), bf16), ((rows, LANES), f32), ((2 * value_here, rows), f32), payload_shape],
        [twin_hidden, norm_gain, beta_weight, log_decay, logits, squares, in_weight, mixed],
        [pltpu.VMEM((16, LANES), f32)],
    )
    for mask in (3, 1, 0):
        payloads[mask] = vmem_call(
            functools.partial(payload_kernel, mask),
            [payload_shape],
            [scaled, scale, in_weight, mixed, extra],
            [pltpu.VMEM((16, LANES), f32)],
        )[0]
    new_residual = vmem_call(residual_kernel, [(residual.shape, bf16)], [hidden, twin_hidden], last=True)[0]
    came = {mask: swapped(payloads[mask], "ctx", mask) for mask in masks}
    came[0] = payloads[0]
    half = rows // 2
    terms_shapes = [
        ((4, 2, 2, DK, DV), f32),
        ((4, 2, 2, DK + half, DK), bf16),
        ((4, 2, rows, DV), f32),
        ((4, 2, 2, 8, LANES), f32),
    ]
    terms = []
    for group in GROUPS:
        terms = vmem_call(
            functools.partial(block_kernel, group),
            terms_shapes,
            [*(came[mask] for mask in group), *terms],
            aliases={len(group) + i: i for i in range(4)} if terms else None,
        )
    own, *backs = vmem_call(
        scan_kernel,
        [((rows, 2 * DV), bf16)] * 4,
        [*terms, delta_gain[None, :]],
        [pltpu.VMEM((4, rows, 2 * DV), bf16)],
    )
    backs = {mask: swapped(backs[mask - 1], "ctx", mask) for mask in masks}
    delta_out = pl.pallas_call(
        place_kernel,
        out_shape=jax.ShapeDtypeStruct((rows, value_here * DV), bf16),
        in_specs=[IN_VMEM] * 4,
        out_specs=IN_HBM,
        scratch_shapes=[pltpu.SemaphoreType.DMA((4,))],
        compiler_params=pltpu.CompilerParams(vmem_limit_bytes=4 * MIB),
    )(*[in_vmem(back) for back in (own, backs[3], backs[1], backs[2])])
    return (new_residual, delta_out)


def solution(mesh):
    local = owner_local if owners_fit(mesh) else hop_local
    return jax.shard_map(
        local,
        mesh=mesh,
        in_specs=(
            P(("groups", "ctx"), ("head", "sub")),
            P(("groups", "ctx"), ("head", "sub")),
            P(("groups", "ctx"), None),
            P(("groups", "ctx"), ("head", "sub")),
            P(("head", "sub"), None),
            P(),
            P(None, ("head", "sub")),
            P(None, ("head", "sub")),
            P(("groups", "ctx"), ("head", "sub")),
            P(),
        ),
        out_specs=(P(("groups", "ctx"), ("head", "sub")), P(("groups", "ctx"), ("head", "sub"))),
        check_vma=False,
    )
```

```python
import functools

import jax
import jax.numpy as jnp
from jax import lax
from jax.experimental import pallas as pl
from jax.experimental.pallas import tpu as pltpu
from jax.sharding import PartitionSpec as P

HEADS = 16
KV_HEADS = 2
HD = 256
DK = 128
DV = 128


TOP_PRECISION = lax.Precision.HIGHEST
EPSILON = 1e-06
NEGATIVE = -1e30


def passed_along(value, axis, steps):
    count = lax.axis_size(axis)
    initial, last = (max(0, -steps), min(count, count - steps))
    return lax.ppermute(value, axis, [(source, source + steps) for source in range(initial, last)])


def stored_positions(first_row, row_total, half_rows, ctx_count):
    row_index = first_row + jnp.arange(row_total, dtype=jnp.int32)
    device_of = row_index // (2 * half_rows)
    within_dev = row_index % (2 * half_rows)
    block_number = jnp.where(within_dev < half_rows, device_of, 2 * ctx_count - 1 - device_of)
    return block_number * half_rows + within_dev % half_rows


def unit_rows(matrix):
    return matrix * lax.rsqrt(jnp.sum(matrix * matrix, axis=-1, keepdims=True) + EPSILON)


def to_blocks(array, half_rows):
    heads_count = array.shape[1]
    width = array.shape[2]
    shaped = array.reshape(2, half_rows, heads_count, width).transpose(2, 0, 1, 3)
    return shaped.reshape(heads_count * 2, half_rows, width)


def block_terms(query_rows, key_rows, value_rows, beta_rows, decay_rows):
    length = query_rows.shape[0]
    cumulative = jnp.cumsum(decay_rows)
    position = jnp.arange(length)
    on_or_below = position[:, None] >= position[None, :]
    strictly_below = position[:, None] > position[None, :]
    decay_gap = cumulative[:, None] - cumulative[None, :]
    decay_grid = jnp.where(on_or_below, jnp.exp(jnp.where(on_or_below, decay_gap, 0.0)), 0.0)
    key_gram = jnp.dot(key_rows, key_rows.T, precision=TOP_PRECISION)
    system = jnp.eye(length, dtype=jnp.float32) + jnp.where(
        strictly_below, beta_rows[:, None] * key_gram * decay_grid, 0.0
    )
    growth = jnp.exp(cumulative)
    right_side = beta_rows[:, None] * jnp.concatenate(
        [value_rows, growth[:, None] * key_rows], axis=1
    )
    solved = jax.scipy.linalg.solve_triangular(system, right_side, lower=True, unit_diagonal=True)
    update_rows = solved[:, : value_rows.shape[1]]
    weight_rows = solved[:, value_rows.shape[1] :]
    attend_grid = jnp.where(
        on_or_below, jnp.dot(query_rows, key_rows.T, precision=TOP_PRECISION) * decay_grid, 0.0
    )
    local_out = jnp.dot(attend_grid, update_rows, precision=TOP_PRECISION)
    read_rows = growth[:, None] * query_rows - jnp.dot(
        attend_grid, weight_rows, precision=TOP_PRECISION
    )
    carried_keys = jnp.exp(cumulative[-1] - cumulative)[:, None] * key_rows
    identity_map = jnp.eye(key_rows.shape[1], dtype=jnp.float32)
    transition = jnp.exp(cumulative[-1]) * identity_map - jnp.dot(
        carried_keys.T, weight_rows, precision=TOP_PRECISION
    )
    offset_state = jnp.dot(carried_keys.T, update_rows, precision=TOP_PRECISION)
    return (local_out, read_rows, transition, offset_state)


def apply_map(matrix_maps, offsets, states):
    return jnp.einsum("hij,hjk->hik", matrix_maps, states, precision=TOP_PRECISION) + offsets


def attend_rows(running, query_block, key_block, value_block, visible, score_scale):
    run_max, run_sum, run_acc = running
    scores = (
        jnp.einsum("rhd,kd->rhk", query_block, key_block, preferred_element_type=jnp.float32)
        * score_scale
    )
    if visible is not None:
        scores = jnp.where(visible[:, None, :], scores, NEGATIVE)
    new_max = jnp.maximum(run_max, jnp.max(scores, axis=2))
    weights = jnp.exp(scores - new_max[:, :, None])
    if visible is not None:
        weights = jnp.where(visible[:, None, :], weights, 0.0)
    rescale = jnp.exp(run_max - new_max)
    run_sum = run_sum * rescale + jnp.sum(weights, axis=2)
    added = jnp.einsum(
        "rhk,kd->rhd", weights.astype(jnp.bfloat16), value_block, preferred_element_type=jnp.float32
    )
    run_acc = run_acc * rescale[:, :, None] + added
    return (new_max, run_sum, run_acc)


def hop_local(
    att_query,
    att_gate,
    att_kv,
    residual,
    out_weight,
    norm_gain,
    in_weight,
    beta_weight,
    log_decay,
    delta_gain,
):
    ctx_count = lax.axis_size("ctx")
    ctx_rank = lax.axis_index("ctx")
    shard_rank = lax.axis_index(("head", "sub"))
    rows_here = att_query.shape[0]
    half_rows = rows_here // 2
    heads_here = att_query.shape[1] // HD
    kv_number = shard_rank * heads_here // (HEADS // KV_HEADS)
    key_local = lax.dynamic_slice_in_dim(att_kv, kv_number * 2 * HD, HD, 1)
    value_local = lax.dynamic_slice_in_dim(att_kv, kv_number * 2 * HD + HD, HD, 1)
    query_heads = att_query.reshape(rows_here, heads_here, HD)
    late_queries = query_heads[half_rows:]
    query_places = stored_positions(ctx_rank * rows_here, rows_here, half_rows, ctx_count)
    same_visible = query_places[:, None] >= query_places[None, :]
    score_scale = HD ** (-0.5)

    def earlier_shard(running, key_shard, value_shard):
        return attend_rows(
            running, query_heads, key_shard[:half_rows], value_shard[:half_rows], None, score_scale
        )

    def same_shard(running, key_shard, value_shard):
        return attend_rows(running, query_heads, key_shard, value_shard, same_visible, score_scale)

    def later_shard(running, key_shard, value_shard):
        late_part = tuple((member[half_rows:] for member in running))
        renewed = attend_rows(late_part, late_queries, key_shard, value_shard, None, score_scale)
        return tuple(
            (
                jnp.concatenate([member[:half_rows], latest], axis=0)
                for member, latest in zip(running, renewed)
            )
        )

    start_running = (
        jnp.full((rows_here, heads_here), NEGATIVE, jnp.float32),
        jnp.zeros((rows_here, heads_here), jnp.float32),
        jnp.zeros((rows_here, heads_here, HD), jnp.float32),
    )
    key_block = lax.all_gather(key_local, "ctx", axis=0, tiled=True)
    value_block = lax.all_gather(value_local, "ctx", axis=0, tiled=True)
    piece_rows = key_block.shape[0]

    def one_shard(number, current):
        offset = number * rows_here
        key_shard = lax.dynamic_slice_in_dim(key_block, offset, rows_here, 0)
        value_shard = lax.dynamic_slice_in_dim(value_block, offset, rows_here, 0)
        shard_number = offset // rows_here
        branch = jnp.clip(shard_number - ctx_rank, -1, 1) + 1
        return lax.switch(
            branch, [earlier_shard, same_shard, later_shard], current, key_shard, value_shard
        )

    run_max, run_sum, run_acc = lax.fori_loop(0, piece_rows // rows_here, one_shard, start_running)
    gate_heads = jax.nn.sigmoid(att_gate.reshape(rows_here, heads_here, HD).astype(jnp.float32))
    att_heads = (
        (run_acc / run_sum[:, :, None] * gate_heads)
        .astype(jnp.bfloat16)
        .reshape(rows_here, heads_here * HD)
    )
    partial_term = jnp.dot(att_heads, out_weight, preferred_element_type=jnp.float32)
    col_width = residual.shape[1]
    col_start = shard_rank * col_width
    placed = lax.dynamic_slice_in_dim(partial_term, col_start, col_width, 1) + residual.astype(
        jnp.float32
    )
    partial_term = lax.dynamic_update_slice_in_dim(partial_term, placed, col_start, 1)
    hidden = lax.psum(partial_term.astype(jnp.bfloat16), ("head", "sub")).astype(jnp.float32)
    mean_square = jnp.mean(hidden * hidden, axis=1, keepdims=True)
    normed = (hidden * lax.rsqrt(mean_square + EPSILON) * norm_gain).astype(jnp.bfloat16)
    new_residual = lax.dynamic_slice_in_dim(hidden, col_start, col_width, 1).astype(jnp.bfloat16)
    mixed_cols = jnp.dot(normed, in_weight, preferred_element_type=jnp.float32)
    beta_logits = jnp.dot(normed, beta_weight, preferred_element_type=jnp.float32)
    key_here = in_weight.shape[1] // (2 * DK + 2 * DV)
    value_here = 2 * key_here
    grouped = mixed_cols.reshape(rows_here, key_here, 2 * DK + 2 * DV)
    query_unit = jnp.repeat(unit_rows(jax.nn.silu(grouped[:, :, :DK])) * DK ** (-0.5), 2, axis=1)
    key_unit = jnp.repeat(unit_rows(jax.nn.silu(grouped[:, :, DK : 2 * DK])), 2, axis=1)
    value_all = jax.nn.silu(grouped[:, :, 2 * DK :]).reshape(rows_here, value_here, DV)
    beta_all = jax.nn.sigmoid(beta_logits)
    local_out, read_rows, transition, offset_state = jax.vmap(block_terms)(
        to_blocks(query_unit, half_rows),
        to_blocks(key_unit, half_rows),
        to_blocks(value_all, half_rows),
        to_blocks(beta_all[:, :, None], half_rows)[:, :, 0],
        to_blocks(log_decay[:, :, None], half_rows)[:, :, 0],
    )
    transition = transition.reshape(value_here, 2, DK, DK)
    offset_state = offset_state.reshape(value_here, 2, DK, DV)
    early_map, late_map = (transition[:, 0], transition[:, 1])
    early_offset, late_offset = (offset_state[:, 0], offset_state[:, 1])
    last_rank = ctx_count - 1
    zero_states = jnp.zeros_like(early_offset)

    def early_turn(number, incoming):
        return passed_along(
            apply_map(early_map, early_offset, incoming).astype(jnp.bfloat16), "ctx", 1
        ).astype(jnp.float32)

    early_in = lax.fori_loop(0, ctx_count - 1, early_turn, zero_states)
    early_end = apply_map(early_map, early_offset, early_in)
    late_start = jnp.where(ctx_rank == last_rank, early_end, zero_states)

    def late_turn(number, incoming):
        moved = passed_along(
            apply_map(late_map, late_offset, incoming).astype(jnp.bfloat16), "ctx", -1
        ).astype(jnp.float32)
        return jnp.where(ctx_rank == last_rank, early_end, moved)

    late_in = lax.fori_loop(0, ctx_count - 1, late_turn, late_start)
    states_in = jnp.stack([early_in, late_in], axis=1)
    block_out = local_out.reshape(value_here, 2, half_rows, DV) + jnp.einsum(
        "hbck,hbkv->hbcv",
        read_rows.reshape(value_here, 2, half_rows, DK),
        states_in,
        precision=TOP_PRECISION,
    )
    token_out = block_out.transpose(1, 2, 0, 3).reshape(rows_here, value_here, DV)
    out_square = jnp.mean(token_out * token_out, axis=2, keepdims=True)
    delta_out = (token_out * lax.rsqrt(out_square + EPSILON) * delta_gain).astype(jnp.bfloat16)
    return (new_residual, delta_out.reshape(rows_here, value_here * DV))


KEY_HEADS = 16
IN_VMEM = pl.BlockSpec(memory_space=pltpu.VMEM)
IN_HBM = pl.BlockSpec(memory_space=pl.ANY)
MIB = 2**20
LANES = 128
GROUPS = ((0,), (2,), (1,), (3,))


def owners_fit(mesh):
    shards = mesh.shape["head"] * mesh.shape["sub"]
    key_here = KEY_HEADS // shards
    return mesh.shape["head"] == 2 and mesh.shape["sub"] == 2 and key_here == mesh.shape["ctx"]


def in_vmem(array):
    return pltpu.with_memory_space_constraint(array, pltpu.VMEM)


def in_hbm(array):
    return pltpu.with_memory_space_constraint(array, pltpu.HBM)


def vmem_call(kernel, outs, operands, scratch=(), limit=16, aliases=None, last=False, cost=None):
    make = jax.ShapeDtypeStruct if last else pltpu.VMEM
    return pl.pallas_call(
        kernel,
        out_shape=[make(shape, dtype) for shape, dtype in outs],
        in_specs=[IN_VMEM] * len(operands),
        out_specs=[IN_VMEM] * len(outs),
        scratch_shapes=list(scratch),
        input_output_aliases=aliases or {},
        cost_estimate=cost,
        compiler_params=pltpu.CompilerParams(vmem_limit_bytes=limit * MIB),
    )(*[in_vmem(operand) for operand in operands])


def swapped(value, axis, mask=1):
    return lax.ppermute(value, axis, [(i, i ^ mask) for i in range(lax.axis_size(axis))])


def dot(left, right, dims=((1,), (0,))):
    return lax.dot_general(left, right, (dims, ((), ())), preferred_element_type=jnp.float32)


def halves(value):
    high = value.astype(jnp.bfloat16)
    return high, (value - high.astype(jnp.float32)).astype(jnp.bfloat16)


def sigmoid(value):
    return 1.0 / (1.0 + jnp.exp(-value))


def silu(value):
    return value / (1.0 + jnp.exp(-value))


def piece_kernel(kv_ref, piece_ref, sem):
    start = (lax.axis_index("head") * 2 + lax.axis_index("sub")) * HD
    copy = pltpu.make_async_copy(kv_ref.at[:, pl.ds(pl.multiple_of(start, HD), HD)], piece_ref, sem)
    copy.start()
    copy.wait()


def fetch_kernel(*refs):
    count = len(refs) // 2
    copies = [
        pltpu.make_async_copy(refs[n], refs[count + n], refs[-1].at[n]) for n in range(count)
    ]
    for copy in copies:
        copy.start()
    for copy in copies:
        copy.wait()


def fetched(*arrays):
    moved = sum(array.size * array.dtype.itemsize for array in arrays)
    return pl.pallas_call(
        fetch_kernel,
        out_shape=[pltpu.VMEM(array.shape, array.dtype) for array in arrays],
        in_specs=[IN_HBM] * len(arrays),
        out_specs=[IN_VMEM] * len(arrays),
        scratch_shapes=[pltpu.SemaphoreType.DMA((len(arrays),))],
        compiler_params=pltpu.CompilerParams(vmem_limit_bytes=4 * MIB),
        cost_estimate=pl.CostEstimate(flops=0, bytes_accessed=moved, transcendentals=0),
    )(*[in_hbm(array) for array in arrays])


def attend(query_ref, gate_ref, keys, values, rows, key_total, visible):
    count = query_ref.shape[1] // HD
    columns = [slice(head * HD, (head + 1) * HD) for head in range(count)]
    size = rows.stop - rows.start
    queries = jnp.concatenate([query_ref[rows, part] for part in columns], axis=0)
    gates = [sigmoid(gate_ref[rows, part].astype(jnp.float32)) for part in columns]
    scores = dot(queries, keys[0:key_total], ((1,), (1,))) * HD ** (-0.5)
    scores = jnp.where(jnp.concatenate([visible] * count, axis=0), scores, NEGATIVE)
    weights = jnp.exp(scores - jnp.max(scores, axis=1, keepdims=True))
    total = jnp.sum(weights, axis=1, keepdims=True)
    gathered = dot(weights.astype(jnp.bfloat16), values[0:key_total]) / total
    gated = [gathered[head * size : (head + 1) * size] * gates[head] for head in range(count)]
    return jnp.concatenate(gated, axis=1).astype(jnp.bfloat16)


def attention_kernel(
    query_ref, gate_ref, kv_ref, mine1, mine2, mine3, twin1, twin2, twin3, weight_ref, residual_ref,
    heads_ref, send_ref, keys, values, sums,
):
    half = query_ref.shape[0] // 2
    ctx_rank, head_rank, sub_rank = (lax.axis_index(name) for name in ("ctx", "head", "sub"))
    count = 4
    own_start = pl.multiple_of(head_rank * 2 * HD, 2 * HD)

    def put(target, mask, part):
        target[mask * half : (mask + 1) * half] = part[0:half]
        target[(count + mask) * half : (count + mask + 1) * half] = part[half : 2 * half]

    put(keys, 0, kv_ref[:, pl.ds(own_start, HD)])
    put(values, 0, kv_ref[:, pl.ds(own_start + HD, HD)])

    @pl.when(sub_rank == 0)
    def _():
        for mask, (mine, twin) in enumerate(((mine1, twin1), (mine2, twin2), (mine3, twin3)), 1):
            put(keys, mask, mine[...])
            put(values, mask, twin[...])

    @pl.when(sub_rank != 0)
    def _():
        for mask, (mine, twin) in enumerate(((mine1, twin1), (mine2, twin2), (mine3, twin3)), 1):
            put(keys, mask, twin[...])
            put(values, mask, mine[...])

    shift = half.bit_length() - 1
    row = lax.broadcasted_iota(jnp.int32, (half, 1), 0)
    column = lax.broadcasted_iota(jnp.int32, (1, 2 * count * half), 1)
    device = jnp.bitwise_xor(ctx_rank, (column >> shift) & (count - 1))
    block = jnp.where(column < count * half, device, 2 * count - 1 - device)
    key_place = block * half + (column & (half - 1))
    for part, block_here in enumerate((ctx_rank, 2 * count - 1 - ctx_rank)):
        rows = slice(part * half, (part + 1) * half)
        key_total = (part + 1) * count * half
        visible = row + block_here * half >= key_place[:, :key_total]
        heads_ref[rows] = attend(query_ref, gate_ref, keys, values, rows, key_total, visible)
    mid = send_ref.shape[1]
    width = residual_ref.shape[1]
    sums[...] = dot(heads_ref[...], weight_ref[:, pl.ds(pl.multiple_of((1 - sub_rank) * mid, mid), mid)])

    @pl.when(sub_rank != head_rank)
    def _():
        sums[:, pl.ds(pl.multiple_of(sub_rank * width, width), width)] += residual_ref[...].astype(jnp.float32)

    send_ref[...] = sums[...].astype(jnp.bfloat16)


def keep_kernel(heads_ref, weight_ref, residual_ref, keep_ref):
    head_rank, sub_rank = lax.axis_index("head"), lax.axis_index("sub")
    mid = keep_ref.shape[1]
    width = residual_ref.shape[1]
    keep_ref[...] = dot(heads_ref[...], weight_ref[:, pl.ds(pl.multiple_of(sub_rank * mid, mid), mid)])

    @pl.when(sub_rank == head_rank)
    def _():
        keep_ref[:, pl.ds(pl.multiple_of(sub_rank * width, width), width)] += residual_ref[...].astype(jnp.float32)


def chip_sum_kernel(keep_ref, came_ref, sum_ref, send_ref):
    total = keep_ref[...] + came_ref[...].astype(jnp.float32)
    sum_ref[...] = total
    send_ref[...] = total.astype(jnp.bfloat16)


def hidden_kernel(keep_ref, came_ref, hidden_ref):
    hidden_ref[...] = (keep_ref[...] + came_ref[...].astype(jnp.float32)).astype(jnp.bfloat16)


def half_of(ref, own):
    sub_rank = lax.axis_index("sub")
    mid = ref.shape[-1] // 2
    return pl.ds(pl.multiple_of((sub_rank if own else 1 - sub_rank) * mid, mid), mid)


def own_half_kernel(own_ref, gain_ref, weight_ref, beta_ref, mixed_ref, logit_ref, square_ref):
    mid = own_ref.shape[1]
    own = own_ref[...].astype(jnp.float32)
    columns = half_of(gain_ref, True)
    scaled = (own * gain_ref[:, columns]).astype(jnp.bfloat16)
    square_ref[...] = jnp.broadcast_to(jnp.sum(own * own, axis=1, keepdims=True), square_ref.shape)
    logit_ref[...] = dot(beta_ref[:, columns], scaled, ((1,), (1,)))
    rows = pl.ds(pl.multiple_of(lax.axis_index("sub") * mid, mid), mid)
    mixed_ref[...] = dot(scaled, weight_ref[rows, :])


def twin_half_kernel(
    twin_ref, gain_ref, beta_ref, decay_ref, logit_ref, square_ref, weight_ref, mixed_ref,
    scaled_ref, scale_ref, extra_ref, payload_ref, small,
):
    twin = twin_ref[...].astype(jnp.float32)
    columns = half_of(gain_ref, False)
    scaled_ref[...] = (twin * gain_ref[:, columns]).astype(jnp.bfloat16)
    squares = square_ref[...] + jnp.sum(twin * twin, axis=1, keepdims=True)
    scale = lax.rsqrt(squares / gain_ref.shape[1] + EPSILON)
    scale_ref[...] = scale
    values = decay_ref.shape[0]
    logits = logit_ref[...] + dot(beta_ref[:, columns], scaled_ref[...], ((1,), (1,)))
    extra_ref[0:values] = decay_ref[...]
    extra_ref[values : 2 * values] = sigmoid(logits * jnp.transpose(scale)[0:1])
    payload_kernel(2, scaled_ref, scale_ref, weight_ref, mixed_ref, extra_ref, payload_ref, small)


def residual_kernel(own_ref, twin_ref, residual_ref):
    head_rank, sub_rank = lax.axis_index("head"), lax.axis_index("sub")
    width = residual_ref.shape[1]
    columns = pl.ds(pl.multiple_of(sub_rank * width, width), width)

    @pl.when(sub_rank == head_rank)
    def _():
        residual_ref[...] = own_ref[:, columns]

    @pl.when(sub_rank != head_rank)
    def _():
        residual_ref[...] = twin_ref[:, columns]


def payload_kernel(mask, scaled_ref, scale_ref, weight_ref, mixed_ref, extra_ref, payload_ref, small):
    rows, mid = scaled_ref.shape
    group = 2 * DK + 2 * DV
    target = jnp.bitwise_xor(lax.axis_index("ctx"), mask)
    columns = pl.ds(pl.multiple_of(target * group, group), group)
    weight_rows = pl.ds(pl.multiple_of((1 - lax.axis_index("sub")) * mid, mid), mid)
    mixed = mixed_ref[:, columns] + dot(scaled_ref[...], weight_ref[weight_rows, columns])
    mixed = silu(mixed * scale_ref[:, 0:1])
    query, key = mixed[:, :DK], mixed[:, DK : 2 * DK]
    payload_ref[0:rows] = unit_rows(key).astype(jnp.bfloat16)
    values = extra_ref.shape[0] // 2
    small[...] = jnp.zeros_like(small)
    for place, base in ((0, 0), (4, values)):
        full = extra_ref[pl.ds(base + 2 * target, 2), :]
        high = full.astype(jnp.bfloat16).astype(jnp.float32)
        small[place : place + 2] = high
        small[place + 2 : place + 4] = full - high
    payload_ref[rows : rows + 16] = small[...].astype(jnp.bfloat16)
    rest = (unit_rows(query) * DK ** (-0.5), mixed[:, 2 * DK : 2 * DK + DV], mixed[:, 2 * DK + DV :])
    for number, part in enumerate(rest, 1):
        payload_ref[number * rows + 16 : (number + 1) * rows + 16] = part.astype(jnp.bfloat16)


def joined(left, right):
    (left_high, left_low), (right_high, right_low) = left, right
    right_high, right_low = apart(right_high), apart(right_low)
    return dot(
        jnp.concatenate([left_high, left_high, left_low], axis=1),
        jnp.concatenate([right_high, right_low, right_high], axis=0),
    )


def apart(pair):
    first = lax.broadcasted_iota(jnp.int32, pair.shape, 1) < pair.shape[1] // 2
    zero = jnp.zeros_like(pair)
    return jnp.concatenate([jnp.where(first, pair, zero), jnp.where(first, zero, pair)], axis=0)


def unit_lower_inverses(stricts):
    half = stricts[0].shape[0]
    row = lax.broadcasted_iota(jnp.int32, (half, 1), 0)
    column = lax.broadcasted_iota(jnp.int32, (1, 2 * half), 1) & (half - 1)
    inner = (row >> 3) == (column >> 3)
    identity = jnp.where(row == column, 1.0, 0.0)
    number = range(len(stricts))
    smalls = [jnp.where(inner, strict, 0.0) for strict in stricts]
    rests = [halves(jnp.where(inner, 0.0, strict)) for strict in stricts]
    small = [halves(part) for part in smalls]
    inverses = [identity - part for part in smalls]
    split = [halves(inverse) for inverse in inverses]
    seconds = [halves(joined(part, part)) for part in small]
    fourths = [halves(joined(second, second)) for second in seconds]
    inverses = [inverses[n] + joined(split[n], seconds[n]) for n in number]
    split = [halves(inverse) for inverse in inverses]
    inverses = [inverses[n] + joined(split[n], fourths[n]) for n in number]
    split = [halves(inverse) for inverse in inverses]
    steps = [halves(joined(split[n], rests[n])) for n in number]
    doubles = [halves(joined(step, step)) for step in steps]
    results = [inverses[n] - joined(steps[n], split[n]) for n in number]
    quads = [halves(joined(double, double)) for double in doubles]
    results = [results[n] + joined(doubles[n], halves(results[n])) for n in number]
    return [results[n] + joined(quads[n], halves(results[n])) for n in number]


def key_terms(chunks):
    rows = chunks[0][0].shape[0]
    half = rows // 2
    shift = half.bit_length() - 1
    row = lax.broadcasted_iota(jnp.int32, (rows, 1), 0)
    column = lax.broadcasted_iota(jnp.int32, (1, rows), 1)
    together = (row >> shift) == (column >> shift)
    inclusive = together & (row >= column)
    strictly = together & (row > column)
    early = column < half
    below = jnp.where(inclusive, 1.0, 0.0).astype(jnp.bfloat16)
    diagonal = jnp.where(row == column, 1.0, 0.0).astype(jnp.bfloat16)
    below, diagonal = (jnp.concatenate([left, left], axis=1) for left in (below, diagonal))
    items = [(chunk, head) for chunk in range(len(chunks)) for head in range(2)]
    keys = [key for key, _ in chunks]
    extras = [extra.astype(jnp.float32) for _, extra in chunks]

    def spread(left, chunk, place):
        lanes = [
            jnp.broadcast_to(extras[chunk][n : n + 1], (rows, rows)).astype(jnp.bfloat16) for n in (place, place + 2)
        ]
        return dot(left, jnp.concatenate(lanes, axis=1), ((1,), (1,)))

    sums = [dot(extra, below[:, :rows], ((1,), (1,))) for _, extra in chunks]
    key_grams = [dot(key, key, ((1,), (1,))) for key in keys]
    totals = {item: spread(below, *item) for item in items}
    betas = {(chunk, head): spread(diagonal, chunk, head + 4) for chunk, head in items}
    total_rows = {(c, h): sums[c][h : h + 1] + sums[c][h + 2 : h + 3] for c, h in items}
    decays = {item: jnp.exp(jnp.where(inclusive, totals[item] - total_rows[item], NEGATIVE)) for item in items}
    stricts = [jnp.where(strictly, betas[item] * key_grams[item[0]] * decays[item], 0.0) for item in items]
    wide = [key.astype(jnp.float32) for key in keys]
    turned = [jnp.transpose(key) for key in wide]
    growths = {item: jnp.exp(totals[item]) for item in items}
    pairs = [strict[:half] + strict[half:] for strict in stricts]
    inverses = [[apart(part) for part in halves(inverse)] for inverse in unit_lower_inverses(pairs)]
    terms = []
    for item, (high, low) in zip(items, inverses):
        total = total_rows[item]
        end = jnp.where(early, total[:, half - 1 : half], total[:, rows - 1 : rows])
        carried = turned[item[0]] * jnp.exp(end - total)
        carried = [jnp.where(early, carried, 0.0), jnp.where(early, 0.0, carried)]
        weighted = (betas[item] * growths[item] * wide[item[0]]).astype(jnp.bfloat16)
        lefts = jnp.concatenate(carried, axis=0).astype(jnp.bfloat16)
        terms.append((betas[item], decays[item], growths[item], weighted, lefts, high, low, jnp.exp(end)))
    return terms


def finish_terms(source, query, key, values, terms, offset_ref, linear_ref, local_ref, growth_ref):
    rows = query.shape[0]
    half = rows // 2
    query_gram = dot(query, key, ((1,), (1,)))
    solved = []
    for value, (beta, _, _, weighted, _, high, low, _) in zip(values, terms):
        right = jnp.concatenate([(beta * value.astype(jnp.float32)).astype(jnp.bfloat16), weighted], axis=1)
        both = dot(jnp.concatenate([high, low], axis=1), jnp.concatenate([right, right], axis=0))
        solved.append(both.astype(jnp.bfloat16))
    moved = []
    for part, (_, decay, _, _, lefts, _, _, _) in zip(solved, terms):
        moved.append(dot(jnp.concatenate([lefts, (query_gram * decay).astype(jnp.bfloat16)], axis=0), part))
    for head, (part, (_, _, growth, _, _, _, _, ends)) in enumerate(zip(moved, terms)):
        attended = part[2 * DK :]
        local_ref[source, head] = attended[:, :DV]
        reads = (growth * query.astype(jnp.float32) - attended[:, DV:]).astype(jnp.bfloat16)
        for block in range(2):
            state = part[block * DK : (block + 1) * DK]
            offset_ref[source, head, block] = state[:, :DV]
            linear_ref[source, head, block, 0:DK] = state[:, DV:].astype(jnp.bfloat16)
            linear_ref[source, head, block, DK : DK + half] = reads[block * half : (block + 1) * half]
            last = (block + 1) * half - 1
            growth_ref[source, head, block] = jnp.broadcast_to(ends[:, last : last + 1], growth_ref.shape[3:])


def source_of(mask):
    return jnp.bitwise_xor(lax.axis_index("ctx"), mask)


def block_kernel(masks, *refs):
    payload_refs, outs = refs[: len(masks)], refs[-4:]
    rows = (payload_refs[0].shape[0] - 16) // 4
    keys = [ref[0:rows] for ref in payload_refs]
    terms = key_terms([(key, ref[rows : rows + 16]) for key, ref in zip(keys, payload_refs)])
    for number, (mask, ref) in enumerate(zip(masks, payload_refs)):
        query, *values = (ref[n * rows + 16 : (n + 1) * rows + 16] for n in (1, 2, 3))
        finish_terms(source_of(mask), query, keys[number], values, terms[2 * number : 2 * number + 2], *outs)


def scan_kernel(offset_ref, linear_ref, local_ref, growth_ref, gain_ref, own_ref, back1, back2, back3, outs):
    count = offset_ref.shape[0]
    half = local_ref.shape[2] // 2
    rank = lax.axis_index("ctx")
    order = [(n, 0) for n in range(count)] + [(n, 1) for n in reversed(range(count))]
    before = []
    states = [None, None]
    for source, block in order:
        before.append([None if state is None else state.astype(jnp.bfloat16) for state in states])
        for head in range(2):
            state = offset_ref[source, head, block]
            if states[head] is not None:
                moved = dot(linear_ref[source, head, block, 0:DK], before[-1][head])
                state = state - moved + growth_ref[source, head, block, 0:1] * states[head]
            states[head] = state
    for (source, block), entering in zip(order, before):
        block_rows = slice(block * half, (block + 1) * half)
        for head in range(2):
            out = local_ref[source, head, block_rows]
            if entering[head] is not None:
                out = out + dot(linear_ref[source, head, block, DK : DK + half], entering[head])
            scale = lax.rsqrt(jnp.mean(out * out, axis=1, keepdims=True) + EPSILON)
            outs[source, block_rows, head * DV : (head + 1) * DV] = (out * scale * gain_ref[...]).astype(jnp.bfloat16)
    own_ref[...] = outs[rank]
    for mask, back in enumerate((back1, back2, back3), 1):
        back[...] = outs[jnp.bitwise_xor(rank, mask)]


def place_kernel(own_ref, back3, back1, back2, out_ref, sems):
    width = own_ref.shape[1]
    rank = lax.axis_index("ctx")
    copies = []
    for mask, back in enumerate((own_ref, back1, back2, back3)):
        columns = pl.ds(pl.multiple_of(jnp.bitwise_xor(rank, mask) * width, width), width)
        copies.append(pltpu.make_async_copy(back, out_ref.at[:, columns], sems.at[mask]))
        copies[-1].start()
    for copy in copies:
        copy.wait()


def owner_local(
    att_query,
    att_gate,
    att_kv,
    residual,
    out_weight,
    norm_gain,
    in_weight,
    beta_weight,
    log_decay,
    delta_gain,
):
    bf16, f32 = jnp.bfloat16, jnp.float32
    rows, head_columns = att_query.shape
    model = out_weight.shape[1]
    half_model = model // 2
    value_here = log_decay.shape[1]
    masks = (2, 3, 1)
    piece = pl.pallas_call(
        piece_kernel,
        out_shape=pltpu.VMEM((rows, HD), bf16),
        in_specs=[IN_HBM],
        out_specs=IN_VMEM,
        scratch_shapes=[pltpu.SemaphoreType.DMA],
        compiler_params=pltpu.CompilerParams(vmem_limit_bytes=4 * MIB),
    )(in_hbm(att_kv))
    mine = {mask: swapped(piece, "ctx", mask) for mask in masks[::-1]}
    piece, *late = lax.optimization_barrier((piece, att_query, att_gate, att_kv, out_weight, residual))
    late = fetched(*late)
    mine[3], (att_query, att_gate, att_kv, out_weight, residual) = lax.optimization_barrier((mine[3], late))
    twin = {3: swapped(mine[3], "sub"), 1: swapped(mine[1], "sub")}
    mine[2] = lax.optimization_barrier((mine[2], twin[3]))[0]
    twin[2] = swapped(mine[2], "sub")
    heads, send = vmem_call(
        attention_kernel,
        [((rows, head_columns), bf16), ((rows, half_model), bf16)],
        [att_query, att_gate, att_kv, mine[1], mine[2], mine[3], twin[1], twin[2], twin[3], out_weight, residual],
        [
            pltpu.VMEM((4 * rows, HD), bf16),
            pltpu.VMEM((4 * rows, HD), bf16),
            pltpu.VMEM((rows, half_model), f32),
        ],
    )
    came = swapped(send, "sub")
    keep = vmem_call(keep_kernel, [((rows, half_model), f32)], [heads, out_weight, residual])[0]
    came, keep = lax.optimization_barrier((came, keep))
    chip_sum, send = vmem_call(
        chip_sum_kernel, [((rows, half_model), f32), ((rows, half_model), bf16)], [keep, came]
    )
    came = swapped(send, "head")
    send, *late = lax.optimization_barrier((send, in_weight, norm_gain[None, :], beta_weight.T, log_decay.T))
    late = fetched(*late)
    came, (in_weight, norm_gain, beta_weight, log_decay) = lax.optimization_barrier((came, late))
    hidden = vmem_call(hidden_kernel, [((rows, half_model), bf16)], [chip_sum, came])[0]
    twin_hidden = swapped(hidden, "sub")
    sums = vmem_call(
        own_half_kernel,
        [((rows, in_weight.shape[1]), f32), ((value_here, rows), f32), ((rows, LANES), f32)],
        [hidden, norm_gain, in_weight, beta_weight],
    )
    twin_hidden, (mixed, logits, squares) = lax.optimization_barrier((twin_hidden, sums))
    payload_shape = ((4 * rows + 16, LANES), bf16)
    payloads = {}
    scaled, scale, extra, payloads[2] = vmem_call(
        twin_half_kernel,
        [((rows, half_model), bf16), ((rows, LANES), f32), ((2 * value_here, rows), f32), payload_shape],
        [twin_hidden, norm_gain, beta_weight, log_decay, logits, squares, in_weight, mixed],
        [pltpu.VMEM((16, LANES), f32)],
    )
    for mask in (3, 1, 0):
        payloads[mask] = vmem_call(
            functools.partial(payload_kernel, mask),
            [payload_shape],
            [scaled, scale, in_weight, mixed, extra],
            [pltpu.VMEM((16, LANES), f32)],
        )[0]
    new_residual = vmem_call(residual_kernel, [(residual.shape, bf16)], [hidden, twin_hidden], last=True)[0]
    came = {mask: swapped(payloads[mask], "ctx", mask) for mask in masks}
    came[0] = payloads[0]
    half = rows // 2
    terms_shapes = [
        ((4, 2, 2, DK, DV), f32),
        ((4, 2, 2, DK + half, DK), bf16),
        ((4, 2, rows, DV), f32),
        ((4, 2, 2, 8, LANES), f32),
    ]
    terms = []
    for group in GROUPS:
        terms = vmem_call(
            functools.partial(block_kernel, group),
            terms_shapes,
            [*(came[mask] for mask in group), *terms],
            aliases={len(group) + i: i for i in range(4)} if terms else None,
        )
    own, *backs = vmem_call(
        scan_kernel,
        [((rows, 2 * DV), bf16)] * 4,
        [*terms, delta_gain[None, :]],
        [pltpu.VMEM((4, rows, 2 * DV), bf16)],
    )
    backs = {mask: swapped(backs[mask - 1], "ctx", mask) for mask in masks}
    delta_out = pl.pallas_call(
        place_kernel,
        out_shape=jax.ShapeDtypeStruct((rows, value_here * DV), bf16),
        in_specs=[IN_VMEM] * 4,
        out_specs=IN_HBM,
        scratch_shapes=[pltpu.SemaphoreType.DMA((4,))],
        compiler_params=pltpu.CompilerParams(vmem_limit_bytes=4 * MIB),
    )(*[in_vmem(back) for back in (own, backs[3], backs[1], backs[2])])
    return (new_residual, delta_out)


def solution(mesh):
    local = owner_local if owners_fit(mesh) else hop_local
    return jax.shard_map(
        local,
        mesh=mesh,
        in_specs=(
            P(("groups", "ctx"), ("head", "sub")),
            P(("groups", "ctx"), ("head", "sub")),
            P(("groups", "ctx"), None),
            P(("groups", "ctx"), ("head", "sub")),
            P(("head", "sub"), None),
            P(),
            P(None, ("head", "sub")),
            P(None, ("head", "sub")),
            P(("groups", "ctx"), ("head", "sub")),
            P(),
        ),
        out_specs=(P(("groups", "ctx"), ("head", "sub")), P(("groups", "ctx"), ("head", "sub"))),
        check_vma=False,
    )
```
